32 devices in a mesh: gx: 4 (over y, core), gy: 4 (over z), gz: 2 (over x).
Axes of the slice: x: 2, y: 2, z: 4, core: 2. Of those that a mesh axis runs over, the one named last changes fastest.
Arguments:
- chi: float32 [64, 64, 256], P('gx', 'gy', 'gz'), may hold values from 0.05 to 4
- inducing: float32 [3, 64, 64, 256], P(None, 'gx', 'gy', 'gz'), may hold values from -6 to 6
- record_dest: int32 [4, 4, 2, 1024, 1], P('gx', 'gy', 'gz'), may hold values from 0 to 1; in each aligned block of 1024 rows (0 to 1023, 1024 to 2047, ..., all dimensions but the last counted through in order) at most 640 rows name the same one
- record_cell: int32 [4, 4, 2, 1024], P('gx', 'gy', 'gz'), may hold values from 0 to 32767
- record_value: float32 [4, 4, 2, 1024], P('gx', 'gy', 'gz'), may hold values from -16 to 16
Outputs:
- potential: float32 [64, 64, 256], P('gx', 'gy', 'gz')
The draws below stay inside these ranges and needn't reach their ends.
Inputs may be any that keep to these rules, and one draw needn't show every extreme that they name: `record_dest`: among the records of one device, at most 640 go to any one depth brick; in some devices exactly 640 do.
All inputs are finite; a program needn't handle non-finite values.
Results may differ from the reference program's by a relative error of at most 0.0001.
Values sent between devices are 32-bit elements; how exact they have to be, the bound alone decides.
No kernel may reach another device: no remote copies, remote signals or barrier semaphores. Data moves between devices by JAX's collectives and lax.ppermute only.
A program may use at most 64 MiB of HBM per device.

```python
import math
import jax
import jax.numpy as jnp
import numpy as np
from jax import lax

CX = 16
CY = 16
CZ = 128
RECS = 1024
SMOOTH = 2
LEVELS = 3
COARSE_SWEEPS = 8
CAP = 640
NX = 64
NY = 64
NZ = 256
N_GX = 4
N_GY = 4
N_GZ = 2


def touch_ends(entries, stream_key, least, high):
    dims = entries.shape
    place = [jax.random.randint(jax.random.fold_in(stream_key, axis), (), 0, dims[axis]) for axis in range(len(dims))]
    entries = entries.at[tuple(place)].set(least)
    longest = dims.index(max(dims))
    place[longest] = (place[longest] + 1) % dims[longest]
    return entries.at[tuple(place)].set(high)


def block_levels(own_key, shape, pieces, smallest, largest):
    def one(axis_at, shards_of):
        heights = jax.random.uniform(jax.random.fold_in(jax.random.fold_in(own_key, 6), axis_at), (shards_of,), jnp.float32, smallest / len(pieces), largest / len(pieces))
        return jnp.repeat(jnp.exp(heights), shape[axis_at] // shards_of).reshape((-1,) + (1,) * (len(shape) - axis_at - 1))

    level = one(*pieces[0])
    for cut in pieces[1:]:
        level = level * one(*cut)
    return level


def assign_block(stream_key, own, number, rows, amount, top, reach, slope):
    sequence = jax.random.permutation(stream_key, amount)
    heavy_load, usual = portions_of(amount, rows * top, reach, slope, True), portions_of(amount, rows * top, reach, slope, False)
    places = jnp.arange(amount)

    def named(lengths, turn):
        used = int((lengths > 0).sum())
        fixed = max(1, used // 4)
        shifted = fixed + (places - fixed + turn * (used - fixed)) % max(1, amount - fixed)
        return jnp.zeros((amount,), jnp.int32).at[sequence[jnp.where(places < fixed, places, shifted)]].set(jnp.asarray(lengths, jnp.int32))

    lengths = jnp.where(number % 4 == 0, named(heavy_load, number // 4), named(usual, number - number // 4 - 1))
    mixed = jax.random.permutation(jax.random.fold_in(own, 3), amount)
    source_of, taker = mixed[0:amount // 2 * 2:2], mixed[1:amount // 2 * 2:2]
    room = jnp.minimum(lengths[source_of] - 1, reach - lengths[taker]) // 2
    room = jnp.where((source_of == sequence[0]) | (taker == sequence[0]) | (lengths[taker] == 0), 0, jnp.maximum(room, 0))
    shifted = jax.random.randint(jax.random.fold_in(own, 4), (amount // 2,), 0, 1 << 20) % (room + 1)
    lengths = lengths.at[source_of].add(-shifted).at[taker].add(shifted)
    labels = jnp.searchsorted(jnp.cumsum(lengths), jnp.arange(rows * top), side="right").astype(jnp.int32)
    grid = labels.reshape(top, rows).T
    grid = grid[jax.random.permutation(jax.random.fold_in(own, 1), rows)]
    turn = jax.random.randint(jax.random.fold_in(own, 2), (rows, 1), 0, top)
    return jnp.take_along_axis(grid, (jnp.arange(top)[None, :] + turn) % top, axis=1)


def portions_of(amount, total, bound, lean, full):
    loads = [(1 << 20) // math.isqrt(standing ** lean) + 1 for standing in range(1, amount + 1)]
    largest = bound if full else min(bound, max(-(-total // amount), total * loads[0] // sum(loads)))
    least = 1 if total - largest >= amount - 1 else 0
    counts, surplus = [largest] + [least] * (amount - 1), total - largest - least * (amount - 1)
    while surplus > 0:
        candidates = [i for i in range(1, amount) if counts[i] < largest] or [i for i in range(1, amount) if counts[i] < bound]
        pool, left = sum([loads[i] for i in candidates]), surplus
        for i in candidates:
            extra = min(bound - counts[i], max(1, left * loads[i] // pool), surplus)
            counts[i] = counts[i] + extra
            surplus = surplus - extra
    return np.array(counts)


def scatter_about(stream_key, dims, scale, reach, split=(), held_as=jnp.bfloat16):
    loudness = block_levels(stream_key, dims, split, -0.22, 0.18) if split else 1.0
    array = jax.random.normal(stream_key, dims, jnp.float32) * scale * loudness
    return jnp.minimum(jnp.maximum(array, -reach), reach).astype(held_as)


def setup_inputs(seed: int = 0) -> dict:
    keys = jax.random.split(jax.random.key(seed), 6)
    chi = jnp.clip(jnp.exp(math.log(4.0) - 4.3820266 * jax.random.uniform(keys[0], (NX, NY, NZ), jnp.float32) ** block_levels(keys[0], (NX, NY, NZ), ((0, 4), (1, 4), (2, 2)), -0.2, 0.2)), 0.05, 4.0)
    inducing = scatter_about(keys[1], (3, NX, NY, NZ), 1.0, 6.0, ((1, 4), (2, 4), (3, 2)), jnp.float32)
    record_dest_keys = jax.random.split(jax.random.fold_in(keys[2], 1), N_GX * N_GY * N_GZ * RECS // RECS)
    record_dest_turns = jax.random.permutation(jax.random.fold_in(keys[2], 3), N_GX * N_GY * N_GZ * RECS // RECS)
    record_dest = jax.vmap(lambda own, number: assign_block(jax.random.fold_in(keys[2], 2), own, number, RECS, N_GZ, 1, CAP, 1))(record_dest_keys, record_dest_turns).reshape((N_GX, N_GY, N_GZ, RECS, 1))
    record_cell = touch_ends(jax.random.randint(keys[3], (N_GX, N_GY, N_GZ, RECS), 0, CX * CY * CZ), jax.random.fold_in(keys[3], 1), 0, (CX * CY * CZ) - 1).astype(jnp.int32)
    record_value = scatter_about(keys[4], (N_GX, N_GY, N_GZ, RECS), 4.0, 16.0, ((0, 4), (1, 4), (2, 2)), jnp.float32)
    return dict(chi=chi, inducing=inducing, record_dest=record_dest, record_cell=record_cell, record_value=record_value)


OMEGA = 0.8


def restrict(x):
    s = x.shape
    return x.reshape(s[0] // 2, 2, s[1] // 2, 2, s[2] // 2, 2).mean(axis=(1, 3, 5))


def prolong(e):
    return jnp.repeat(jnp.repeat(jnp.repeat(e, 2, 0), 2, 1), 2, 2)


def neighbours(padded):
    return [padded[2:, 1:-1, 1:-1], padded[:-2, 1:-1, 1:-1], padded[1:-1, 2:, 1:-1],
            padded[1:-1, :-2, 1:-1], padded[1:-1, 1:-1, 2:], padded[1:-1, 1:-1, :-2]]


def coefficients(kappa):
    center = kappa
    return [0.5 * (center + other) for other in neighbours(jnp.pad(kappa, 1))]


def apply_op(v, coefs, scale):
    total = jnp.zeros_like(v)
    for coef, other in zip(coefs, neighbours(jnp.pad(v, 1))):
        total = total + coef * (v - other)
    return scale * total


def cycle(level, rhs, kappas):
    scale = 0.25 ** level
    coefs = coefficients(kappas[level])
    diag = scale * (coefs[0] + coefs[1] + coefs[2] + coefs[3] + coefs[4] + coefs[5])
    sweeps = COARSE_SWEEPS if level == LEVELS else SMOOTH
    v = OMEGA * rhs / diag
    for sweep in range(sweeps - 1):
        v = v + OMEGA * (rhs - apply_op(v, coefs, scale)) / diag
    if level == LEVELS:
        return v
    resid = rhs - apply_op(v, coefs, scale)
    corr = cycle(level + 1, restrict(resid), kappas)
    v = v + prolong(corr)
    for sweep in range(SMOOTH):
        v = v + OMEGA * (rhs - apply_op(v, coefs, scale)) / diag
    return v


def reference(chi, inducing, record_dest, record_cell, record_value):
    moment = chi[None] * inducing
    px = jnp.pad(moment[0], 1)
    py = jnp.pad(moment[1], 1)
    pz = jnp.pad(moment[2], 1)
    source = -0.5 * ((px[2:, 1:-1, 1:-1] - px[:-2, 1:-1, 1:-1])
                     + (py[1:-1, 2:, 1:-1] - py[1:-1, :-2, 1:-1])
                     + (pz[1:-1, 1:-1, 2:] - pz[1:-1, 1:-1, :-2]))
    dest = record_dest[..., 0].astype(jnp.int32)
    cell = record_cell.astype(jnp.int32)
    shape = cell.shape
    row_a = lax.broadcasted_iota(jnp.int32, shape, 0)
    row_b = lax.broadcasted_iota(jnp.int32, shape, 1)
    xpos = row_a * CX + cell // (CY * CZ)
    ypos = row_b * CY + (cell // CZ) % CY
    zpos = dest * CZ + cell % CZ
    flat = ((xpos * NY + ypos) * NZ + zpos).reshape(-1)
    rhs = source.reshape(-1).at[flat].add(record_value.reshape(-1)).reshape(source.shape)
    kappas = [1.0 + chi]
    for level in range(LEVELS):
        kappas.append(restrict(kappas[-1]))
    return cycle(0, rhs, kappas)
```

```python
import functools

import jax
import jax.numpy as jnp
from jax import lax
from jax.experimental import pallas as pl
from jax.experimental.pallas import tpu as pltpu
from jax.sharding import PartitionSpec as P

SMOOTH = 2
LEVELS = 3
COARSE_SWEEPS = 8
CAP = 640


OMEGA = 0.8


def padded_2(cells, sides, width):
    for axis, dim in sides:
        count = lax.axis_size(axis)
        ends = count - 1
        head = lax.slice_in_dim(cells, 0, width, axis=dim)
        tail = lax.slice_in_dim(cells, cells.shape[dim] - width, cells.shape[dim], axis=dim)
        cells = jnp.concatenate(
            [
                lax.ppermute(tail, axis, [(i, (i + 1) % count) for i in range(ends)]),
                cells,
                lax.ppermute(head, axis, [((i + 1) % count, i) for i in range(ends)]),
            ],
            axis=dim,
        )
    return cells


def restrict(x):
    s = x.shape
    return x.reshape(s[0] // 2, 2, s[1] // 2, 2, s[2] // 2, 2).mean(axis=(1, 3, 5))


def prolong(e):
    return jnp.repeat(jnp.repeat(jnp.repeat(e, 2, 0), 2, 1), 2, 2)


def neighbours(padded):
    return [
        padded[2:, 1:-1, 1:-1],
        padded[:-2, 1:-1, 1:-1],
        padded[1:-1, 2:, 1:-1],
        padded[1:-1, :-2, 1:-1],
        padded[1:-1, 1:-1, 2:],
        padded[1:-1, 1:-1, :-2],
    ]


def face_pad(x):
    return padded_2(x, (("gx", 0), ("gy", 1), ("gz", 2)), 1)


def coefficients(kappa):
    return [0.5 * (kappa + other) for other in neighbours(face_pad(kappa))]


def apply_op(v, coefs, scale):
    total = jnp.zeros_like(v)
    for coef, other in zip(coefs, neighbours(face_pad(v))):
        total = total + coef * (v - other)
    return scale * total


def cycle(level, rhs, kappa):
    scale = 0.25**level
    coefs = coefficients(kappa)
    diag = scale * (coefs[0] + coefs[1] + coefs[2] + coefs[3] + coefs[4] + coefs[5])
    v = OMEGA * rhs / diag
    for sweep in range((COARSE_SWEEPS if level == LEVELS else SMOOTH) - 1):
        v = v + OMEGA * (rhs - apply_op(v, coefs, scale)) / diag
    if level == LEVELS:
        return v
    resid = rhs - apply_op(v, coefs, scale)
    corr = cycle(level + 1, restrict(resid), restrict(kappa))
    v = v + prolong(corr)
    for sweep in range(SMOOTH):
        v = v + OMEGA * (rhs - apply_op(v, coefs, scale)) / diag
    return v


def general(chi, inducing, record_dest, record_cell, record_value):
    n_gz = lax.axis_size("gz")
    dest = record_dest[0, 0, 0, :, 0]
    cells = record_cell[0, 0, 0]
    values = record_value[0, 0, 0]
    onehot = (dest[:, None] == jnp.arange(n_gz, dtype=jnp.int32)[None, :]).astype(jnp.int32)
    ranks = jnp.sum((jnp.cumsum(onehot, axis=0) - 1) * onehot, axis=1)
    outgoing = jnp.zeros((n_gz, 2, CAP), jnp.float32)
    outgoing = outgoing.at[dest, 0, ranks].set(values)
    outgoing = outgoing.at[dest, 1, ranks].set(cells.astype(jnp.float32))
    incoming = lax.all_to_all(outgoing, "gz", split_axis=0, concat_axis=0, tiled=True)
    in_values = incoming[:, 0].reshape(-1)
    in_cells = incoming[:, 1].reshape(-1).astype(jnp.int32)
    moment_x = face_pad(chi * inducing[0])
    moment_y = face_pad(chi * inducing[1])
    moment_z = face_pad(chi * inducing[2])
    source = -0.5 * (
        moment_x[2:, 1:-1, 1:-1]
        - moment_x[:-2, 1:-1, 1:-1]
        + (moment_y[1:-1, 2:, 1:-1] - moment_y[1:-1, :-2, 1:-1])
        + (moment_z[1:-1, 1:-1, 2:] - moment_z[1:-1, 1:-1, :-2])
    )
    rhs = source.reshape(-1).at[in_cells].add(in_values).reshape(source.shape)
    return cycle(0, rhs, 1.0 + chi)


F32 = jnp.float32
BF16 = jnp.bfloat16
ROWS = 42
PLANES = 36


def iota(shape, dim):
    return lax.broadcasted_iota(jnp.int32, shape, dim)


def roll(x, shift, axis):
    shift = shift % x.shape[axis]
    return pltpu.roll(x, shift, axis) if shift else x


def pick(flag, first, second):
    return jnp.where(jnp.full(first.shape, flag, jnp.int32) == 0, first, second)


def dot(a, b):
    return jnp.dot(a, b, precision=lax.Precision.HIGHEST, preferred_element_type=F32)


def halving(offset, factor):
    shape = (128, 128)
    return jnp.where((iota(shape, 0) >> 1) + offset == iota(shape, 1), factor, 0.0).astype(F32)


def place():
    gx, gy, gz = lax.axis_index("gx"), lax.axis_index("gy"), lax.axis_index("gz")
    return gx >> 1, gx & 1, gy, gz


def prepare_kernel(chi, inducing, dest, cell, value, source, message, coarse, mx, my, mz, kap, sums):
    _, _, _, t = place()
    for ref in (mx, my, mz):
        ref[...] = jnp.zeros_like(ref)
    kap[...] = jnp.zeros_like(kap)
    kappa = 1.0 + chi[...]
    kap[:, 4:20, :] = kappa
    mx[2:18, 4:20, 0:128] = chi[...] * inducing[0]
    my[2:18, 4:20, 0:128] = chi[...] * inducing[1]
    mz[2:18, 4:20, 0:128] = chi[...] * inducing[2]
    lane = iota((24, 128), 1)
    blocks = [jnp.zeros((24, 128), F32), jnp.zeros((24, 128), F32)]
    for i in range(18):
        dx = mx[i + 2] - mx[i]
        dy = roll(my[i + 1], -1, 0) - roll(my[i + 1], 1, 0)
        dz = roll(mz[i + 1], -1, 1) - roll(mz[i + 1], 1, 1)
        row = -0.5 * (dx + dy + dz)
        source[i] = row
        piece = pick(t, roll(row, -125, 1)[:, :128], roll(row, 1, 1)[:, :128])
        piece = jnp.where(lane < 4, piece, 0.0)
        if 1 <= i <= 16:
            k = kap[i - 1]
            k = jnp.where(lane < 4, pick(t, roll(k, -124, 1), k), 0.0)
            piece = piece + roll(k, 4, 1)
            blocks[0] = blocks[0] + roll(piece, 8 * (i - 1), 1)
        else:
            blocks[1] = blocks[1] + roll(piece, 0 if i == 0 else 8, 1)
    message[0:24] = blocks[0]
    message[24:48] = blocks[1]
    message[48:56] = value[...]
    message[56:64] = (dest[...] * 32768 + cell[...]).astype(F32)
    pairs = kappa.reshape(8, 2, 16, 128)
    sums[...] = (pairs[:, 0] + pairs[:, 1]).reshape(128, 128)
    halves = sums[pl.ds(0, 64, stride=2), :] + sums[pl.ds(1, 64, stride=2), :]
    coarse[...] = dot(halves[:32], halving(0, 0.125)) + dot(halves[32:], halving(64, 0.125))


def deposit_kernel(source, chi, mine, other, own, sent, sz, kz, at_row, hi, mid, lo):
    _, c, _, t = place()
    spot = iota((256, 128), 0)
    for j in range(16):
        ref, k = (mine, j) if j < 8 else (other, j - 8)
        value = ref[48 + k : 49 + k, :]
        code = ref[56 + k : 57 + k, :].astype(jnp.int32)
        cells = code & 32767
        column = (((code >> 15) - t) * 128 + (cells & 127)) & 255
        cut = slice(128 * j, 128 * (j + 1))
        at_row[:, cut] = jnp.where(spot == (cells >> 7), 1.0, 0.0).astype(BF16)
        here = spot == column
        for part in (hi, mid, lo):
            short = value.astype(BF16).astype(F32)
            part[:, cut] = jnp.where(here, short, 0.0).astype(BF16)
            value = value - short
    total = jnp.zeros((256, 256), F32)
    for part in (lo, mid, hi):
        total = total + lax.dot_general(
            at_row[...], part[...], (((1,), (1,)), ((), ())), preferred_element_type=F32
        )
    lane = iota((24, 128), 1)
    zeros = jnp.zeros((24, 128), F32)
    kz[...] = jnp.zeros_like(kz)
    kz[:, 4:20, 0:128] = 1.0 + chi[...]
    for i in range(18):
        if 1 <= i <= 16:
            near = roll(other[0:24], -8 * (i - 1), 1)
        else:
            near = roll(other[24:48], 0 if i == 0 else -8, 1)
        wide = jnp.concatenate([jnp.where(lane < 4, near, 0.0), zeros], 1)
        sz[i] = source[i] + pick(t, roll(wide, 127, 1), roll(wide, 253, 1))
        if 1 <= i <= 16:
            wide = jnp.concatenate([jnp.where((lane >= 4) & (lane < 8), near, 0.0), zeros], 1)
            kz[i - 1] = kz[i - 1] + pick(t, roll(wide, 124, 1), roll(wide, 248, 1))
            sz[i, 4:20, :] = sz[i, 4:20, :] + total[16 * (i - 1) : 16 * i]
    keep, give = pl.multiple_of(8 * c, 8), pl.multiple_of(8 - 8 * c, 8)
    for i in range(18):
        own[i] = sz[i, pl.ds(keep, 16), :]
        sent[i] = sz[i, pl.ds(give, 16), :]
    for i in range(16):
        own[18 + i] = kz[i, pl.ds(keep, 16), :]
        sent[18 + i] = kz[i, pl.ds(give, 16), :]


def pair_kernel(own, other, source, kappa, message):
    p, c, _, _ = place()
    source[...] = jnp.zeros_like(source)
    kappa[...] = jnp.zeros_like(kappa)
    source[pl.ds(4 + 16 * c, 18)] = own[0:18]
    low = 4 + 16 * (1 - c)
    source[pl.ds(low, 18)] = source[pl.ds(low, 18)] + other[0:18]
    kappa[pl.ds(5 + 16 * c, 16)] = own[18:34]
    kappa[pl.ds(low + 1, 16)] = other[18:34]
    message[0:4] = source[pl.ds(34 - 30 * p, 4)]
    message[4:8] = kappa[pl.ds(33 - 28 * p, 4)]


def across_kernel(source_in, kappa_in, other, source, kappa, message):
    p, c, _, _ = place()
    source[...] = source_in[...]
    kappa[...] = kappa_in[...]
    at = 36 - 34 * p
    source[pl.ds(at, 4)] = source[pl.ds(at, 4)] + other[0:4]
    kappa[pl.ds(37 - 36 * p, 4)] = other[4:8]
    first = 5 - 4 * p
    low = iota((8, 256), 0) < 4

    def body(i, _):
        s, k = source[first + i], kappa[first + i]
        s = pick(c, roll(s, -3, 0)[:8], roll(s, -9, 0)[:8])
        k = pick(c, roll(k, 0, 0)[:8], roll(k, -4, 0)[:8])
        message[i] = jnp.where(low, s, k)
        return 0

    lax.fori_loop(0, PLANES, body, 0)


def faces(kap, cx, cy, cz, weight, diag, first, count, scale, closed):
    shape = kap.shape[1:]
    last_y = iota(shape, 0) == shape[0] - 1
    first_y = iota(shape, 0) == 0
    last_z = iota(shape, 1) == shape[1] - 1
    first_z = iota(shape, 1) == 0

    def body(i, _):
        r = first + i
        k, up, down = kap[r], kap[r + 1], kap[r - 1]
        yu, yd, zu, zd = roll(k, -1, 0), roll(k, 1, 0), roll(k, -1, 1), roll(k, 1, 1)
        if closed:
            yu, yd = jnp.where(last_y, 0.0, yu), jnp.where(first_y, 0.0, yd)
            zu, zd = jnp.where(last_z, 0.0, zu), jnp.where(first_z, 0.0, zd)
        half = 0.5 * scale
        total = half * (6.0 * k + ((up + down) + (yu + yd) + (zu + zd)))
        fy, fz = half * (k + yu), half * (k + zu)
        if closed:
            fy, fz = jnp.where(last_y, 0.0, fy), jnp.where(last_z, 0.0, fz)
        cx[r] = half * (k + up)
        cy[r] = fy
        cz[r] = fz
        diag[r] = total
        weight[r] = jnp.where(k > 0.0, OMEGA / jnp.where(k > 0.0, total, 1.0), 0.0)
        return 0

    lax.fori_loop(0, count, body, 0)


def around(v, cx, cy, cz, r):
    here = v[r]
    fy, fz = cy[r], cz[r]
    return (
        (cx[r] * v[r + 1] + cx[r - 1] * v[r - 1])
        + (fy * roll(here, -1, 0) + roll(fy * here, 1, 0))
        + (fz * roll(here, -1, 1) + roll(fz * here, 1, 1))
    )


def sweep(v, out, rhs, cx, cy, cz, weight, first, count):
    def body(i, _):
        r = first + i
        out[r] = (1.0 - OMEGA) * v[r] + weight[r] * (rhs[r] + around(v, cx, cy, cz, r))
        return 0

    lax.fori_loop(0, count, body, 0)


def down_kernel(n_gy, source_in, kappa_in, other, rhs, kappa, v2, message, cx, cy, cz, weight, diag, v1, sums):
    p, c, b, _ = place()
    first = 5 - 4 * p
    edge = jnp.where(c == 0, b == 0, b == n_gy - 1).astype(jnp.int32)
    for ref in (kappa, cx, v1, v2, rhs):
        ref[0:5] = jnp.zeros((5, 16, 256), F32)
        ref[37:42] = jnp.zeros((5, 16, 256), F32)
    sub = iota((16, 256), 0)

    def merge(i, _):
        r = first + i
        got = jnp.concatenate([other[i], jnp.zeros((8, 256), F32)], 0)
        got = pick(edge, got, jnp.zeros((16, 256), F32))
        s = jnp.where(sub < 4, got, 0.0)
        k = jnp.where(sub < 4, 0.0, got)
        rhs[r] = source_in[r] + pick(c, roll(s, 1, 0), roll(s, 11, 0))
        kappa[r] = kappa_in[r] + pick(c, roll(k, -4, 0), roll(k, 8, 0))
        return 0

    lax.fori_loop(0, PLANES, merge, 0)
    faces(kappa, cx, cy, cz, weight, diag, first, PLANES, 1.0, False)

    def start(i, _):
        v1[first + i] = weight[first + i] * rhs[first + i]
        return 0

    lax.fori_loop(0, PLANES, start, 0)
    sweep(v1, v2, rhs, cx, cy, cz, weight, first, PLANES)

    def resid(r):
        return rhs[r] + around(v2, cx, cy, cz, r) - diag[r] * v2[r]

    def pair(i, _):
        sums[pl.ds(pl.multiple_of(16 * i, 16), 16), :] = (resid(2 * i + 5) + resid(2 * i + 6))[:, :128]
        return 0

    lax.fori_loop(0, 16, pair, 0)
    halves = sums[pl.ds(0, 128, stride=2), :] + sums[pl.ds(1, 128, stride=2), :]
    packed = dot(halves[:64], halving(0, 0.125)) + dot(halves[64:], halving(64, 0.125))
    low = iota((8, 128), 0) < 4
    for j in range(4):
        even, odd = packed[16 * j : 16 * j + 8], packed[16 * j + 8 : 16 * j + 16]
        tile = jnp.where(low, roll(even, -2, 0), roll(odd, 2, 0))
        for d in range(message.shape[0]):
            message[d, 8 * j : 8 * j + 8, :] = tile


def shift(x, by, axis):
    if axis == 0:
        zero = jnp.zeros((1,) + x.shape[1:], x.dtype)
        return jnp.concatenate([x[1:], zero] if by > 0 else [zero, x[:-1]], 0)
    ends = iota(x.shape, axis) == (x.shape[axis] - 1 if by > 0 else 0)
    return jnp.where(ends, 0.0, roll(x, -by, axis))


class Level:
    def __init__(self, kappa, scale):
        half = 0.5 * scale
        near = [shift(kappa, by, axis) for axis in range(3) for by in (1, -1)]
        self.diag = half * (6.0 * kappa + (near[0] + near[1]) + (near[2] + near[3]) + (near[4] + near[5]))
        self.faces = [half * (kappa + other) for other in near]
        inside = kappa > 0.0
        self.weight = jnp.where(inside, OMEGA / jnp.where(inside, self.diag, 1.0), 0.0)

    def around(self, v):
        near = [shift(v, by, axis) for axis in range(3) for by in (1, -1)]
        terms = [f * o for f, o in zip(self.faces, near)]
        return (terms[0] + terms[1]) + (terms[2] + terms[3]) + (terms[4] + terms[5])

    def sweep(self, v, rhs):
        return (1.0 - OMEGA) * v + self.weight * (rhs + self.around(v))

    def resid(self, v, rhs):
        return rhs + self.around(v) - self.diag * v


def halved(x, scratch):
    nx, ny = x.shape[0] // 2, x.shape[1] // 2
    pairs = x.reshape(nx, 2, 2 * ny, 128)
    scratch[0 : 2 * nx * ny, :] = (pairs[:, 0] + pairs[:, 1]).reshape(2 * nx * ny, 128)
    return halved_yz(scratch, nx, ny)


def halved_yz(scratch, nx, ny):
    halves = scratch[pl.ds(0, nx * ny, stride=2), :] + scratch[pl.ds(1, nx * ny, stride=2), :]
    return dot(halves, halving(0, 0.125)).reshape(nx, ny, 128)


def doubling():
    shape = (128, 128)
    return jnp.where((iota(shape, 1) >> 1) == iota(shape, 0), 1.0, 0.0).astype(F32)


def doubled_yz(e, scratch):
    nx, ny, _ = e.shape
    wide = dot(e.reshape(nx * ny, 128), doubling())
    scratch[pl.ds(0, nx * ny, stride=2), :] = wide
    scratch[pl.ds(1, nx * ny, stride=2), :] = wide
    return scratch[0 : 2 * nx * ny, :].reshape(nx, 2 * ny, 128)


def doubled(e, scratch):
    e = doubled_yz(e, scratch)
    nx, ny, _ = e.shape
    return jnp.broadcast_to(e[:, None], (nx, 2, ny, 128)).reshape(2 * nx, ny, 128)


def coarse_kernel(n_gy, kappas, mine, other, e_out, k1, r1, cx, cy, cz, weight, diag, va, vb, sums):
    p, c, b, t = place()
    n_y = 8 * n_gy
    for ref in (k1, cx, va, vb):
        ref[0] = jnp.zeros((n_y, 128), F32)
        ref[33] = jnp.zeros((n_y, 128), F32)
    left = iota((8, 128), 1) < 64
    top = iota((8, 128), 0) < 4
    for gx in range(4):
        for gy in range(n_gy):
            for x in range(4):
                cut = slice(8 * x, 8 * x + 8)
                near, far = [kappas[(gx * n_gy + gy) * 2 + gz, cut, :] for gz in range(2)]
                spot = slice(8 * gy, 8 * gy + 8)
                k1[1 + 8 * gx + x, spot, :] = jnp.where(left, near, roll(far, 64, 1))
                k1[1 + 8 * gx + 4 + x, spot, :] = jnp.where(left, roll(near, 64, 1), far)
    for pp in range(2):
        for gy in range(n_gy):
            for j in range(4):
                cut = slice(8 * j, 8 * j + 8)
                evens, odds = [], []
                for gz in range(2):
                    a = mine[(pp * n_gy + gy) * 2 + gz, cut, :]
                    o = other[(pp * n_gy + gy) * 2 + gz, cut, :]
                    first, second = pick(c, a, o), pick(c, o, a)
                    evens.append(jnp.where(top, first, roll(second, 4, 0)))
                    odds.append(jnp.where(top, roll(first, 4, 0), second))
                spot = slice(8 * gy, 8 * gy + 8)
                for odd, (near, far) in enumerate((evens, odds)):
                    r1[1 + 16 * pp + 2 * j + odd, spot, :] = jnp.where(left, near, roll(far, 64, 1))
                    r1[1 + 16 * pp + 8 + 2 * j + odd, spot, :] = jnp.where(left, roll(near, 64, 1), far)
    faces(k1, cx, cy, cz, weight, diag, 1, 32, 0.25, True)

    def start(i, _):
        va[1 + i] = weight[1 + i] * r1[1 + i]
        return 0

    lax.fori_loop(0, 32, start, 0)
    sweep(va, vb, r1, cx, cy, cz, weight, 1, 32)

    def resid(r):
        return r1[r] + around(vb, cx, cy, cz, r) - diag[r] * vb[r]

    def pair(i, _):
        sums[pl.ds(pl.multiple_of(n_y * i, 8), n_y), :] = resid(2 * i + 1) + resid(2 * i + 2)
        return 0

    lax.fori_loop(0, 16, pair, 0)
    r2 = halved_yz(sums, 16, n_y // 2)

    def kappa_pair(i, _):
        sums[pl.ds(pl.multiple_of(n_y * i, 8), n_y), :] = k1[2 * i + 1] + k1[2 * i + 2]
        return 0

    lax.fori_loop(0, 16, kappa_pair, 0)
    k2 = halved_yz(sums, 16, n_y // 2)
    middle = Level(k2, 0.0625)
    v2 = middle.weight * r2
    v2 = middle.sweep(v2, r2)
    r3 = halved(middle.resid(v2, r2), sums)
    bottom = Level(halved(k2, sums), 0.015625)
    v3 = bottom.weight * r3
    for _ in range(COARSE_SWEEPS - 1):
        v3 = bottom.sweep(v3, r3)
    v2 = v2 + doubled(v3, sums)
    for _ in range(SMOOTH):
        v2 = middle.sweep(v2, r2)
    e1 = doubled_yz(v2, sums)
    for i in range(16):
        vb[1 + 2 * i] = vb[1 + 2 * i] + e1[i]
        vb[2 + 2 * i] = vb[2 + 2 * i] + e1[i]
    sweep(vb, va, r1, cx, cy, cz, weight, 1, 32)
    sweep(va, vb, r1, cx, cy, cz, weight, 1, 32)
    e_out[...] = vb[...]


def up_kernel(n_gy, e_in, rhs, kappa, v2, out, cx, cy, cz, weight, diag, va, vb, tall):
    p, c, b, t = place()
    first = 5 - 4 * p
    n_y = 8 * n_gy
    for ref in (cx, va, vb):
        ref[0:5] = jnp.zeros((5, 16, 256), F32)
        ref[37:42] = jnp.zeros((5, 16, 256), F32)
    faces(kappa, cx, cy, cz, weight, diag, first, PLANES, 1.0, False)
    tall[:, 0:8, :] = jnp.zeros((18, 8, 128), F32)
    tall[:, 2 * n_y : 2 * n_y + 8, :] = jnp.zeros((18, 8, 128), F32)
    for k in range(18):
        e = e_in[16 * p + k]
        tall[k, pl.ds(4, n_y, stride=2), :] = e
        tall[k, pl.ds(5, n_y, stride=2), :] = e
    window = tall[:, pl.ds(pl.multiple_of(16 * b + 8 * c, 8), 16), :]
    shape = (128, 256)
    z = iota(shape, 1)
    z = jnp.where(z < 192, z, z - 256)
    spread = jnp.where(64 * t + (z >> 1) == iota(shape, 0), 1.0, 0.0).astype(F32)
    e = dot(window.reshape(288, 128), spread).reshape(18, 16, 256)
    for k in range(18):
        for r in (2 * k + 3, 2 * k + 4):
            va[r] = v2[r] + jnp.where(kappa[r] > 0.0, e[k], 0.0)
    sweep(va, vb, rhs, cx, cy, cz, weight, first, PLANES)

    def last(i, _):
        r = 5 + i
        done = (1.0 - OMEGA) * vb[r] + weight[r] * (rhs[r] + around(vb, cx, cy, cz, r))
        out[i] = roll(done[:, :128], -4, 0)[:8]
        return 0

    lax.fori_loop(0, 32, last, 0)


def call(kernel, name, outs, scratch, *args):
    return pl.pallas_call(
        kernel,
        name=name,
        out_shape=[jax.ShapeDtypeStruct(s, F32) for s in outs],
        in_specs=[pl.BlockSpec(memory_space=pltpu.VMEM)] * len(args),
        out_specs=[pl.BlockSpec(memory_space=pltpu.VMEM)] * len(outs),
        scratch_shapes=[pltpu.VMEM(s, d) for s, d in scratch],
        compiler_params=pltpu.CompilerParams(vmem_limit_bytes=48 * 1024 * 1024),
    )(*args)


def paired(chi, inducing, record_dest, record_cell, record_value):
    n_gy = lax.axis_size("gy")
    everyone = ("gx", "gy", "gz")
    window = (ROWS, 16, 256)
    big = [(window, F32)]
    source, message, kappa1 = call(
        prepare_kernel,
        "prepare",
        [(18, 24, 256), (64, 128), (32, 128)],
        [((20, 24, 256), F32)] * 3 + [((16, 24, 128), F32), ((128, 128), F32)],
        chi,
        inducing,
        record_dest.reshape(8, 128),
        record_cell.reshape(8, 128),
        record_value.reshape(8, 128),
    )
    kappas = kappa1[None]
    for axis in ("gz", "gy", "gx"):
        kappas = lax.all_gather(kappas, axis, axis=0, tiled=True)
    got = lax.ppermute(message, "gz", [(0, 1), (1, 0)])
    own, sent = call(
        deposit_kernel,
        "deposit",
        [(34, 16, 256)] * 2,
        [((18, 24, 256), F32), ((16, 24, 256), F32)] + [((256, 2048), BF16)] * 4,
        source,
        chi,
        message,
        got,
    )
    swap = [(0, 1), (1, 0), (2, 3), (3, 2)]
    got = lax.ppermute(sent, "gx", swap)
    source, kappa, message = call(pair_kernel, "pair", [window, window, (8, 16, 256)], [], own, got)
    got = lax.ppermute(message, "gx", [(0, 2), (2, 0), (1, 3), (3, 1)])
    source, kappa, message = call(
        across_kernel, "across", [window, window, (PLANES, 8, 256)], [], source, kappa, got
    )
    turns = []
    for p in range(2):
        for b in range(n_gy):
            low, high = 2 * p * n_gy + b, (2 * p + 1) * n_gy + (b - 1) % n_gy
            turns += [(low, high), (high, low)]
    got = lax.ppermute(message, ("gx", "gy"), turns)
    rhs, kappa, v2, message = call(
        functools.partial(down_kernel, n_gy),
        "down",
        [window, window, window, (4 * n_gy, 32, 128)],
        big * 6 + [((256, 128), F32)],
        source,
        kappa,
        got,
    )
    n = 2 * n_gy
    groups = [[(2 * p + c) * n + g for p in range(2) for g in range(n)] for c in range(2)]
    mine = lax.all_to_all(
        message, everyone, split_axis=0, concat_axis=0, tiled=True, axis_index_groups=groups
    )
    other = lax.ppermute(mine, "gx", swap)
    level1 = (34, 8 * n_gy, 128)
    (e,) = call(
        functools.partial(coarse_kernel, n_gy),
        "coarse",
        [level1],
        [(level1, F32)] * 9 + [((128 * n_gy, 128), F32)],
        kappas,
        mine,
        other,
    )
    (out,) = call(
        functools.partial(up_kernel, n_gy),
        "up",
        [(32, 8, 128)],
        big * 7 + [((18, 16 * n_gy + 8, 128), F32)],
        e,
        rhs,
        kappa,
        v2,
    )
    c = lax.axis_index("gx") & 1
    keep = lax.dynamic_slice_in_dim(out, 16 * c, 16, axis=0)
    give = lax.dynamic_slice_in_dim(out, 16 - 16 * c, 16, axis=0)
    got = lax.ppermute(give, "gx", swap)
    return jnp.where(
        c == 0, jnp.concatenate([keep, got], axis=1), jnp.concatenate([got, keep], axis=1)
    )


def solution(mesh):
    placed = (
        P("gx", "gy", "gz"),
        P(None, "gx", "gy", "gz"),
        P("gx", "gy", "gz", None, None),
        P("gx", "gy", "gz", None),
        P("gx", "gy", "gz", None),
    )
    small = mesh.shape["gx"] == 4 and mesh.shape["gz"] == 2 and mesh.shape["gy"] <= 4
    return jax.shard_map(
        paired if small else general,
        mesh=mesh,
        in_specs=placed,
        out_specs=P("gx", "gy", "gz"),
        check_vma=False,
    )
```

```python
import functools

import jax
import jax.numpy as jnp
from jax import lax
from jax.experimental import pallas as pl
from jax.experimental.pallas import tpu as pltpu
from jax.sharding import PartitionSpec as P

SMOOTH = 2
LEVELS = 3
COARSE_SWEEPS = 8
CAP = 640


OMEGA = 0.8


def padded_2(cells, sides, width):
    for axis, dim in sides:
        count = lax.axis_size(axis)
        ends = count - 1
        head = lax.slice_in_dim(cells, 0, width, axis=dim)
        tail = lax.slice_in_dim(cells, cells.shape[dim] - width, cells.shape[dim], axis=dim)
        cells = jnp.concatenate(
            [
                lax.ppermute(tail, axis, [(i, (i + 1) % count) for i in range(ends)]),
                cells,
                lax.ppermute(head, axis, [((i + 1) % count, i) for i in range(ends)]),
            ],
            axis=dim,
        )
    return cells


def restrict(x):
    s = x.shape
    return x.reshape(s[0] // 2, 2, s[1] // 2, 2, s[2] // 2, 2).mean(axis=(1, 3, 5))


def prolong(e):
    return jnp.repeat(jnp.repeat(jnp.repeat(e, 2, 0), 2, 1), 2, 2)


def neighbours(padded):
    return [
        padded[2:, 1:-1, 1:-1],
        padded[:-2, 1:-1, 1:-1],
        padded[1:-1, 2:, 1:-1],
        padded[1:-1, :-2, 1:-1],
        padded[1:-1, 1:-1, 2:],
        padded[1:-1, 1:-1, :-2],
    ]


def face_pad(x):
    return padded_2(x, (("gx", 0), ("gy", 1), ("gz", 2)), 1)


def coefficients(kappa):
    return [0.5 * (kappa + other) for other in neighbours(face_pad(kappa))]


def apply_op(v, coefs, scale):
    total = jnp.zeros_like(v)
    for coef, other in zip(coefs, neighbours(face_pad(v))):
        total = total + coef * (v - other)
    return scale * total


def cycle(level, rhs, kappa):
    scale = 0.25**level
    coefs = coefficients(kappa)
    diag = scale * (coefs[0] + coefs[1] + coefs[2] + coefs[3] + coefs[4] + coefs[5])
    v = OMEGA * rhs / diag
    for sweep in range((COARSE_SWEEPS if level == LEVELS else SMOOTH) - 1):
        v = v + OMEGA * (rhs - apply_op(v, coefs, scale)) / diag
    if level == LEVELS:
        return v
    resid = rhs - apply_op(v, coefs, scale)
    corr = cycle(level + 1, restrict(resid), restrict(kappa))
    v = v + prolong(corr)
    for sweep in range(SMOOTH):
        v = v + OMEGA * (rhs - apply_op(v, coefs, scale)) / diag
    return v


def general(chi, inducing, record_dest, record_cell, record_value):
    n_gz = lax.axis_size("gz")
    dest = record_dest[0, 0, 0, :, 0]
    cells = record_cell[0, 0, 0]
    values = record_value[0, 0, 0]
    onehot = (dest[:, None] == jnp.arange(n_gz, dtype=jnp.int32)[None, :]).astype(jnp.int32)
    ranks = jnp.sum((jnp.cumsum(onehot, axis=0) - 1) * onehot, axis=1)
    outgoing = jnp.zeros((n_gz, 2, CAP), jnp.float32)
    outgoing = outgoing.at[dest, 0, ranks].set(values)
    outgoing = outgoing.at[dest, 1, ranks].set(cells.astype(jnp.float32))
    incoming = lax.all_to_all(outgoing, "gz", split_axis=0, concat_axis=0, tiled=True)
    in_values = incoming[:, 0].reshape(-1)
    in_cells = incoming[:, 1].reshape(-1).astype(jnp.int32)
    moment_x = face_pad(chi * inducing[0])
    moment_y = face_pad(chi * inducing[1])
    moment_z = face_pad(chi * inducing[2])
    source = -0.5 * (
        moment_x[2:, 1:-1, 1:-1]
        - moment_x[:-2, 1:-1, 1:-1]
        + (moment_y[1:-1, 2:, 1:-1] - moment_y[1:-1, :-2, 1:-1])
        + (moment_z[1:-1, 1:-1, 2:] - moment_z[1:-1, 1:-1, :-2])
    )
    rhs = source.reshape(-1).at[in_cells].add(in_values).reshape(source.shape)
    return cycle(0, rhs, 1.0 + chi)


F32 = jnp.float32
BF16 = jnp.bfloat16
ROWS = 42
PLANES = 36
SIZE = 4


def iota(shape, dim):
    return lax.broadcasted_iota(jnp.int32, shape, dim)


def roll(x, shift, axis):
    shift = shift % x.shape[axis]
    return pltpu.roll(x, shift, axis) if shift else x


def pick(flag, first, second):
    return jnp.where(jnp.full(first.shape, flag, jnp.int32) == 0, first, second)


def dot(a, b):
    return jnp.dot(a, b, precision=lax.Precision.HIGHEST, preferred_element_type=F32)


def halving(offset, factor):
    shape = (128, 128)
    return jnp.where((iota(shape, 0) >> 1) + offset == iota(shape, 1), factor, 0.0).astype(F32)


def place():
    gx, gy, gz = lax.axis_index("gx"), lax.axis_index("gy"), lax.axis_index("gz")
    return gx >> 1, gx & 1, gy, gz


def prepare_kernel(*refs):
    given, (source, spill, message, coarse), (sums, kap), rest = refs[:5], refs[5:9], refs[9:11], refs[11:]
    chi, inducing, dest, cell, value, done = rest
    _, _, _, t = place()
    copies = [pltpu.make_async_copy(a, b, done.at[i]) for i, (a, b) in enumerate(zip(given, rest[:5]))]
    for copy in copies:
        copy.start()
    lane = iota((16, 128), 1)
    tall_lane = iota((24, 128), 1)
    zero = jnp.zeros((16, 128), F32)
    pad = jnp.zeros((8, 128), F32)
    for copy in copies:
        copy.wait()
    kap[...] = 1.0 + chi[...]
    mx = [zero, zero] + [chi[x] * inducing[0, x] for x in range(16)] + [zero, zero]
    tiles = [jnp.zeros((24, 128), F32), jnp.zeros((24, 128), F32)]
    over = zero
    for i in range(18):
        dx = mx[i + 2] - mx[i]
        if 1 <= i <= 16:
            my, mz = chi[i - 1] * inducing[1, i - 1], chi[i - 1] * inducing[2, i - 1]
            y24 = jnp.concatenate([my, pad], 0)
            dy = roll(y24, 3, 0) - roll(y24, 5, 0)
            ahead, behind = roll(mz, -1, 1), roll(mz, 1, 1)
            dz = jnp.where(lane == 127, 0.0, ahead) - jnp.where(lane == 0, 0.0, behind)
            row = -0.5 * (roll(jnp.concatenate([dx + dz, pad], 0), 4, 0) + dy)
            beyond = pick(t, 0.5 * behind, -0.5 * roll(ahead, 1, 1))
            beyond = jnp.where(lane == 0, beyond, 0.0)
            slot = pick(t, roll(beyond, 1, 1), roll(beyond, 2, 1))
            over = over + roll(slot, 8 * (i - 1), 1)
            beyond = roll(jnp.concatenate([beyond, pad], 0), 4, 0)
            k = jnp.concatenate([pick(t, roll(kap[i - 1], -124, 1), kap[i - 1]), pad], 0)
            k = jnp.where(tall_lane < 4, roll(k, 4, 0), 0.0)
        else:
            row = -0.5 * roll(jnp.concatenate([dx, pad], 0), 4, 0)
            beyond = k = jnp.zeros((24, 128), F32)
        source[i] = row
        low = jnp.where(tall_lane < 3, roll(row, -125, 1), 0.0) + roll(beyond, 3, 1)
        high = jnp.where((tall_lane > 0) & (tall_lane < 4), roll(row, 1, 1), 0.0) + beyond
        piece = pick(t, low, high) + roll(k, 4, 1)
        if 1 <= i <= 16:
            tiles[0] = tiles[0] + roll(piece, 8 * (i - 1), 1)
        else:
            tiles[1] = tiles[1] + roll(piece, 0 if i == 0 else 8, 1)
    spill[...] = roll(jnp.concatenate([over, pad], 0), 4, 0)
    message[0:24] = tiles[0]
    message[24:48] = tiles[1]
    message[48:56] = value[...]
    message[56:64] = (dest[...] * 32768 + cell[...]).astype(F32)
    pairs = kap[...].reshape(8, 2, 16, 128)
    sums[...] = (pairs[:, 0] + pairs[:, 1]).reshape(128, 128)
    halves = sums[pl.ds(0, 64, stride=2), :] + sums[pl.ds(1, 64, stride=2), :]
    coarse[...] = dot(halves[:32], halving(0, 0.125)) + dot(halves[32:], halving(64, 0.125))


def deposit_kernel(source, spill, chi, mine, other, own, sent, all_, at_row, hi, mid, lo):
    _, c, _, t = place()
    spot = iota((256, 128), 0)
    for j in range(16):
        ref, k = (mine, j) if j < 8 else (other, j - 8)
        value = ref[48 + k : 49 + k, :]
        code = ref[56 + k : 57 + k, :].astype(jnp.int32)
        cells = code & 32767
        z = ((code >> 15) - t) * 128 + (cells & 127)
        far = z - 128 + 131 * t
        column = jnp.where((far >= 0) & (far < 3), z + 1 + 130 * t, 255)
        column = jnp.where((z >= 0) & (z < 128), z, column)
        cut = slice(128 * j, 128 * (j + 1))
        at_row[:, cut] = jnp.where(spot == (cells >> 7), 1.0, 0.0).astype(BF16)
        here = spot == column
        for part in (hi, mid, lo):
            short = value.astype(BF16).astype(F32)
            part[:, cut] = jnp.where(here, short, 0.0).astype(BF16)
            value = value - short
    total = jnp.zeros((256, 256), F32)
    for part in (lo, mid, hi):
        total = total + lax.dot_general(
            at_row[...], part[...], (((1,), (1,)), ((), ())), preferred_element_type=F32
        )
    lane = iota((24, 128), 1)
    pad = jnp.zeros((8, 128), F32)
    slot, goal = 3 * t, 127 - 127 * t
    halo = other[0:24] + spill[...]
    for i in range(18):
        if 1 <= i <= 16:
            at = 16 * (i - 1)
            got = jnp.concatenate([total[at : at + 16, 128:], pad], 0)
            halo = halo + roll(jnp.where(lane < 4, roll(got, 4, 0), 0.0), 8 * (i - 1), 1)
            add = roll(jnp.concatenate([total[at : at + 16, :128], pad], 0), 4, 0)
            near = roll(other[0:24], -8 * (i - 1), 1)
        else:
            add = jnp.zeros((24, 128), F32)
            near = roll(other[24:48], 0 if i == 0 else -8, 1)
        edge = pick(t, jnp.where(lane == 127, roll(near, 127, 1), 0.0), jnp.where(lane == 0, roll(near, -3, 1), 0.0))
        all_[i] = source[i] + add + edge
    for i in range(16):
        all_[18 + i] = roll(jnp.concatenate([1.0 + chi[i], pad], 0), 4, 0)
    all_[34] = halo
    all_[35] = other[24:48]
    keep, give = pl.multiple_of(8 * c, 8), pl.multiple_of(8 - 8 * c, 8)
    own[...] = all_[:, pl.ds(keep, 16), :]
    sent[...] = all_[:, pl.ds(give, 16), :]


def pair_kernel(own, other, source, kappa, halo, message):
    p, c, _, _ = place()
    source[...] = jnp.zeros_like(source)
    kappa[...] = jnp.zeros_like(kappa)
    source[pl.ds(4 + 16 * c, 18)] = own[0:18]
    low = 4 + 16 * (1 - c)
    source[pl.ds(low, 18)] = source[pl.ds(low, 18)] + other[0:18]
    kappa[pl.ds(5 + 16 * c, 16)] = own[18:34]
    kappa[pl.ds(low + 1, 16)] = other[18:34]
    lane = iota((16, 128), 1)
    tiles = [jnp.zeros((16, 128), F32)] * 3
    for side in range(2):
        cells = roll(pick(c ^ side, own[34], other[34]), 40, 1)
        ends = pick(c ^ side, own[35], other[35])
        before, after = jnp.where(lane < 4, ends, 0.0), jnp.where((lane >= 8) & (lane < 12), ends, 0.0)
        tiles[side] = tiles[side] + jnp.where(lane >= 40, cells, 0.0) + roll(before, 32, 1)
        tiles[side + 1] = tiles[side + 1] + jnp.where(lane < 40, cells, 0.0) + roll(after, 32, 1)
    for i in range(3):
        halo[i] = tiles[i]
    message[0:4] = source[pl.ds(34 - 30 * p, 4)]
    message[4:8] = kappa[pl.ds(33 - 28 * p, 4)]
    message[8] = jnp.where(lane < 40, pick(p, roll(tiles[2], -8, 1), roll(tiles[0], -32, 1)), 0.0)


def across_kernel(source_in, kappa_in, halo_in, other, source, kappa, halo, message):
    p, c, _, _ = place()
    source[...] = source_in[...]
    kappa[...] = kappa_in[...]
    at = 36 - 34 * p
    source[pl.ds(at, 4)] = source[pl.ds(at, 4)] + other[0:4]
    kappa[pl.ds(37 - 36 * p, 4)] = other[4:8]
    zero = jnp.zeros((16, 128), F32)
    halo[0] = halo_in[0] + pick(p, zero, roll(other[8], 8, 1))
    halo[1] = halo_in[1]
    halo[2] = halo_in[2] + pick(p, roll(other[8], 32, 1), zero)
    first = 5 - 4 * p

    def cut(s, k):
        s = pick(c, roll(s, -3, 1)[:, :8], roll(s, -9, 1)[:, :8])
        k = pick(c, k[:, :8], roll(k, -4, 1)[:, :8])
        return jnp.where(iota(s.shape, 1) < 4, s, k)

    def body(i):
        message[pl.ds(i, SIZE)] = cut(source[pl.ds(first + i, SIZE)], kappa[pl.ds(first + i, SIZE)])

    chunked(PLANES, body, SIZE)
    message[PLANES:] = cut(halo[...], halo[...])


def chunked(count, body, size=4):
    def step(i, _):
        body(i * size)
        return 0

    lax.fori_loop(0, count // size, step, 0)


def faces(kap, cx, cy, cz, weight, diag, first, count, scale, closed):
    n = SIZE
    shape = (n,) + kap.shape[1:]
    last_y = iota(shape, 1) == shape[1] - 1
    first_y = iota(shape, 1) == 0
    last_z = iota(shape, 2) == shape[2] - 1
    first_z = iota(shape, 2) == 0

    def body(i):
        r = first + i
        near = kap[pl.ds(r - 1, n + 2)]
        k, up, down = near[1 : n + 1], near[2:], near[:n]
        yu, yd, zu, zd = roll(k, -1, 1), roll(k, 1, 1), roll(k, -1, 2), roll(k, 1, 2)
        if closed:
            yu, yd = jnp.where(last_y, 0.0, yu), jnp.where(first_y, 0.0, yd)
            zu, zd = jnp.where(last_z, 0.0, zu), jnp.where(first_z, 0.0, zd)
        half = 0.5 * scale
        total = half * (6.0 * k + ((up + down) + (yu + yd) + (zu + zd)))
        fy, fz = half * (k + yu), half * (k + zu)
        if closed:
            fy, fz = jnp.where(last_y, 0.0, fy), jnp.where(last_z, 0.0, fz)
        cx[pl.ds(r, n)] = half * (k + up)
        cy[pl.ds(r, n)] = fy
        cz[pl.ds(r, n)] = fz
        diag[pl.ds(r, n)] = total
        weight[pl.ds(r, n)] = jnp.where(k > 0.0, OMEGA / jnp.where(k > 0.0, total, 1.0), 0.0)

    chunked(count, body, n)


def around(v, cx, cy, cz, r, n):
    near, fx = v[pl.ds(r - 1, n + 2)], cx[pl.ds(r - 1, n + 1)]
    here, fy, fz = near[1 : n + 1], cy[pl.ds(r, n)], cz[pl.ds(r, n)]
    return here, (
        (fx[1:] * near[2:] + fx[:n] * near[:n])
        + (fy * roll(here, -1, 1) + roll(fy * here, 1, 1))
        + (fz * roll(here, -1, 2) + roll(fz * here, 1, 2))
    )


def sweep(v, out, rhs, cx, cy, cz, weight, first, count):
    def body(i):
        r = first + i
        here, total = around(v, cx, cy, cz, r, SIZE)
        out[pl.ds(r, SIZE)] = (1.0 - OMEGA) * here + weight[pl.ds(r, SIZE)] * (rhs[pl.ds(r, SIZE)] + total)

    chunked(count, body, SIZE)


def resid(v, rhs, cx, cy, cz, diag, r):
    here, total = around(v, cx, cy, cz, r, SIZE)
    return rhs[pl.ds(r, SIZE)] + total - diag[pl.ds(r, SIZE)] * here


def pair_sums(x):
    x = x.reshape((x.shape[0] // 2, 2) + x.shape[1:])
    return x[:, 0] + x[:, 1]


def down_kernel(
    n_gy, source_in, kappa_in, halo_in, other, kappa1, rhs, kappa, v2, message,
    cx, cy, cz, weight, diag, v1, sums, halo,
):
    p, c, b, t = place()
    first = 5 - 4 * p
    edge = jnp.where(c == 0, b == 0, b == n_gy - 1).astype(jnp.int32)
    for ref in (kappa, cx, v1, v2, rhs):
        ref[0:5] = jnp.zeros((5, 16, 256), F32)
        ref[37:42] = jnp.zeros((5, 16, 256), F32)

    def merge(got):
        n = got.shape[0]
        got = jnp.concatenate([got, jnp.zeros((n, 8, 128), F32)], 1)
        got = pick(edge, got, jnp.zeros_like(got))
        top = iota(got.shape, 1) < 4
        s, k = jnp.where(top, got, 0.0), jnp.where(top, 0.0, got)
        return pick(c, roll(s, 1, 1), roll(s, 11, 1)), pick(c, roll(k, -4, 1), roll(k, 8, 1))

    s, k = merge(other[PLANES:])
    halo[...] = halo_in[...] + jnp.where((iota(s.shape, 2) & 7) < 4, s, k)
    lane = iota((16, 128), 1)
    s_lanes = pick(t, (lane < 3).astype(jnp.int32), (lane >= 125).astype(jnp.int32)) > 0
    k_lanes = pick(t, (lane < 4).astype(jnp.int32), (lane >= 124).astype(jnp.int32)) > 0

    def enter(i):
        r = first + i
        rows = pl.ds(r, SIZE)
        s, k = merge(other[pl.ds(i, SIZE)])
        far_s, far_k = [], []
        for j in range(SIZE):
            tile = halo[(r + j) >> 4]
            by = 8 * ((r + j) & 15)
            far_s.append(jnp.where(s_lanes, pltpu.roll(tile, (127 - by - 2 * t) & 127, 1), 0.0)[None])
            far_k.append(jnp.where(k_lanes, pltpu.roll(tile, (124 - by - 4 * t) & 127, 1), 0.0)[None])
        rhs[rows] = jnp.concatenate([source_in[rows] + s, jnp.concatenate(far_s, 0)], 2)
        kappa[rows] = jnp.concatenate([kappa_in[rows] + k, jnp.concatenate(far_k, 0)], 2)

    chunked(PLANES, enter, SIZE)
    faces(kappa, cx, cy, cz, weight, diag, first, PLANES, 1.0, False)

    def start(i):
        r = pl.ds(first + i, SIZE)
        v1[r] = weight[r] * rhs[r]

    chunked(PLANES, start, SIZE)
    sweep(v1, v2, rhs, cx, cy, cz, weight, first, PLANES)

    def pair(i):
        two = pair_sums(resid(v2, rhs, cx, cy, cz, diag, 5 + i))
        sums[pl.ds(pl.multiple_of(8 * i, 16), 8 * SIZE), :] = two[:, :, :128].reshape(8 * SIZE, 128)

    chunked(32, pair, SIZE)
    halves = sums[pl.ds(0, 128, stride=2), :] + sums[pl.ds(1, 128, stride=2), :]
    packed = dot(halves[:64], halving(0, 0.125)) + dot(halves[64:], halving(64, 0.125))
    low = iota((8, 128), 0) < 4
    for j in range(4):
        even, odd = packed[16 * j : 16 * j + 8], packed[16 * j + 8 : 16 * j + 16]
        tile = jnp.where(low, roll(even, -2, 0), roll(odd, 2, 0))
        for d in range(message.shape[0]):
            message[d, 8 * j : 8 * j + 8, :] = tile
            message[d, 32 + 8 * j : 40 + 8 * j, :] = kappa1[8 * j : 8 * j + 8, :]


def shift(x, by, axis):
    if axis == 0:
        zero = jnp.zeros((1,) + x.shape[1:], x.dtype)
        return jnp.concatenate([x[1:], zero] if by > 0 else [zero, x[:-1]], 0)
    return roll(x, -by, axis)


SIDES = [(axis, by) for axis in range(3) for by in (1, -1)]


class Level:
    def __init__(self, kappa, scale):
        half = 0.5 * scale
        at = iota(kappa.shape, 1)
        ends = {1: at == kappa.shape[1] - 1, -1: at == 0}
        near = [shift(kappa, by, axis) for axis, by in SIDES]
        near[2:4] = [jnp.where(ends[by], 0.0, k) for by, k in zip((1, -1), near[2:4])]
        self.diag = half * (6.0 * kappa + (near[0] + near[1]) + (near[2] + near[3]) + (near[4] + near[5]))
        self.faces = [half * (kappa + other) for other in near]
        self.faces[2:4] = [jnp.where(ends[by], 0.0, f) for by, f in zip((1, -1), self.faces[2:4])]
        inside = kappa > 0.0
        self.weight = jnp.where(inside, OMEGA / jnp.where(inside, self.diag, 1.0), 0.0)

    def around(self, v):
        terms = [f * shift(v, by, axis) for f, (axis, by) in zip(self.faces, SIDES)]
        return (terms[0] + terms[1]) + (terms[2] + terms[3]) + (terms[4] + terms[5])

    def sweep(self, v, rhs):
        return (1.0 - OMEGA) * v + self.weight * (rhs + self.around(v))

    def resid(self, v, rhs):
        return rhs + self.around(v) - self.diag * v


def halved(x, scratch):
    nx, ny = x.shape[0] // 2, x.shape[1] // 2
    pairs = x.reshape(nx, 2, 2 * ny, 128)
    scratch[0 : 2 * nx * ny, :] = (pairs[:, 0] + pairs[:, 1]).reshape(2 * nx * ny, 128)
    return halved_yz(scratch, nx, ny)


def halved_yz(scratch, nx, ny):
    halves = scratch[pl.ds(0, nx * ny, stride=2), :] + scratch[pl.ds(1, nx * ny, stride=2), :]
    return dot(halves, halving(0, 0.125)).reshape(nx, ny, 128)


def doubling():
    shape = (128, 128)
    return jnp.where((iota(shape, 1) >> 1) == iota(shape, 0), 1.0, 0.0).astype(F32)


def doubled_yz(e, scratch):
    nx, ny, _ = e.shape
    wide = dot(e.reshape(nx * ny, 128), doubling())
    scratch[pl.ds(0, nx * ny, stride=2), :] = wide
    scratch[pl.ds(1, nx * ny, stride=2), :] = wide
    return scratch[0 : 2 * nx * ny, :].reshape(nx, 2 * ny, 128)


def doubled(e, scratch):
    e = doubled_yz(e, scratch)
    nx, ny, _ = e.shape
    return jnp.broadcast_to(e[:, None], (nx, 2, ny, 128)).reshape(2 * nx, ny, 128)


def coarse_kernel(n_gy, mine, other, e_out, k1, r1, cx, cy, cz, weight, diag, va, vb, sums):
    p, c, b, t = place()
    n_y = 8 * n_gy
    for ref in (k1, cx, va, vb):
        ref[0] = jnp.zeros((n_y, 128), F32)
        ref[33] = jnp.zeros((n_y, 128), F32)
    left = iota((8, 128), 1) < 64
    top = iota((8, 128), 0) < 4
    for gx in range(4):
        for gy in range(n_gy):
            for x in range(4):
                cut = slice(32 + 8 * x, 40 + 8 * x)
                both = [[ref[((gx >> 1) * n_gy + gy) * 2 + gz, cut, :] for ref in (mine, other)] for gz in range(2)]
                near, far = [pick(c ^ (gx & 1), a, o) for a, o in both]
                spot = slice(8 * gy, 8 * gy + 8)
                k1[1 + 8 * gx + x, spot, :] = jnp.where(left, near, roll(far, 64, 1))
                k1[1 + 8 * gx + 4 + x, spot, :] = jnp.where(left, roll(near, 64, 1), far)
    for pp in range(2):
        for gy in range(n_gy):
            for j in range(4):
                cut = slice(8 * j, 8 * j + 8)
                evens, odds = [], []
                for gz in range(2):
                    a = mine[(pp * n_gy + gy) * 2 + gz, cut, :]
                    o = other[(pp * n_gy + gy) * 2 + gz, cut, :]
                    first, second = pick(c, a, o), pick(c, o, a)
                    evens.append(jnp.where(top, first, roll(second, 4, 0)))
                    odds.append(jnp.where(top, roll(first, 4, 0), second))
                spot = slice(8 * gy, 8 * gy + 8)
                for odd, (near, far) in enumerate((evens, odds)):
                    r1[1 + 16 * pp + 2 * j + odd, spot, :] = jnp.where(left, near, roll(far, 64, 1))
                    r1[1 + 16 * pp + 8 + 2 * j + odd, spot, :] = jnp.where(left, roll(near, 64, 1), far)
    faces(k1, cx, cy, cz, weight, diag, 1, 32, 0.25, True)

    def start(i):
        r = pl.ds(1 + i, SIZE)
        va[r] = weight[r] * r1[r]

    chunked(32, start, SIZE)
    sweep(va, vb, r1, cx, cy, cz, weight, 1, 32)
    step = n_y * SIZE // 2

    def pair(i):
        two = pair_sums(resid(vb, r1, cx, cy, cz, diag, 1 + i))
        sums[pl.ds(pl.multiple_of(n_y // 2 * i, 8), step), :] = two.reshape(step, 128)

    chunked(32, pair, SIZE)
    r2 = halved_yz(sums, 16, n_y // 2)

    def kappa_pair(i):
        two = pair_sums(k1[pl.ds(1 + i, SIZE)])
        sums[pl.ds(pl.multiple_of(n_y // 2 * i, 8), step), :] = two.reshape(step, 128)

    chunked(32, kappa_pair, SIZE)
    k2 = halved_yz(sums, 16, n_y // 2)
    middle = Level(k2, 0.0625)
    v2 = middle.weight * r2
    v2 = middle.sweep(v2, r2)
    r3 = halved(middle.resid(v2, r2), sums)
    bottom = Level(halved(k2, sums), 0.015625)
    v3 = bottom.weight * r3
    for _ in range(COARSE_SWEEPS - 1):
        v3 = bottom.sweep(v3, r3)
    v2 = v2 + doubled(v3, sums)
    for _ in range(SMOOTH):
        v2 = middle.sweep(v2, r2)
    e1 = doubled_yz(v2, sums)
    for i in range(16):
        vb[1 + 2 * i] = vb[1 + 2 * i] + e1[i]
        vb[2 + 2 * i] = vb[2 + 2 * i] + e1[i]
    sweep(vb, va, r1, cx, cy, cz, weight, 1, 32)
    sweep(va, vb, r1, cx, cy, cz, weight, 1, 32)
    e_out[...] = vb[...]


def up_kernel(n_gy, e_in, rhs, kappa, v2, out, cx, cy, cz, weight, diag, va, vb, tall):
    p, c, b, t = place()
    first = 5 - 4 * p
    n_y = 8 * n_gy
    for ref in (cx, va, vb):
        ref[0:5] = jnp.zeros((5, 16, 256), F32)
        ref[37:42] = jnp.zeros((5, 16, 256), F32)
    faces(kappa, cx, cy, cz, weight, diag, first, PLANES, 1.0, False)
    tall[:, 0:8, :] = jnp.zeros((18, 8, 128), F32)
    tall[:, 2 * n_y : 2 * n_y + 8, :] = jnp.zeros((18, 8, 128), F32)
    for k in range(18):
        e = e_in[16 * p + k]
        tall[k, pl.ds(4, n_y, stride=2), :] = e
        tall[k, pl.ds(5, n_y, stride=2), :] = e
    window = tall[:, pl.ds(pl.multiple_of(16 * b + 8 * c, 8), 16), :]
    shape = (128, 256)
    z = iota(shape, 1)
    z = jnp.where(z < 192, z, z - 256)
    spread = jnp.where(64 * t + (z >> 1) == iota(shape, 0), 1.0, 0.0).astype(F32)
    e = dot(window.reshape(288, 128), spread).reshape(18, 16, 256)
    for k in range(18):
        for r in (2 * k + 3, 2 * k + 4):
            va[r] = v2[r] + jnp.where(kappa[r] > 0.0, e[k], 0.0)
    sweep(va, vb, rhs, cx, cy, cz, weight, first, PLANES)

    def last(i):
        r = pl.ds(5 + i, SIZE)
        here, total = around(vb, cx, cy, cz, 5 + i, SIZE)
        done = (1.0 - OMEGA) * here + weight[r] * (rhs[r] + total)
        out[pl.ds(i, SIZE)] = roll(done[:, :, :128], -4, 1)[:, :8]

    chunked(32, last, SIZE)


def call(kernel, name, outs, scratch, *args):
    return pl.pallas_call(
        kernel,
        name=name,
        out_shape=[jax.ShapeDtypeStruct(s, F32) for s in outs],
        in_specs=[pl.BlockSpec(memory_space=pltpu.HBM if name == "prepare" else pltpu.VMEM)] * len(args),
        out_specs=[pl.BlockSpec(memory_space=pltpu.VMEM)] * len(outs),
        scratch_shapes=[
            pltpu.SemaphoreType.DMA((s,)) if isinstance(s, int) else pltpu.VMEM(*s) for s in scratch
        ],
        compiler_params=pltpu.CompilerParams(vmem_limit_bytes=48 * 1024 * 1024),
    )(*args)


def paired(chi, inducing, record_dest, record_cell, record_value):
    n_gy = lax.axis_size("gy")
    everyone = ("gx", "gy", "gz")
    window = (ROWS, 16, 256)
    big = [(window, F32)]
    source, spill, message, kappa1 = call(
        prepare_kernel,
        "prepare",
        [(18, 24, 128), (24, 128), (64, 128), (32, 128)],
        [((128, 128), F32), ((16, 16, 128), F32), ((16, 16, 128), F32), ((3, 16, 16, 128), F32)]
        + [((8, 128), jnp.int32)] * 2
        + [((8, 128), F32), 5],
        chi,
        inducing,
        record_dest.reshape(8, 128),
        record_cell.reshape(8, 128),
        record_value.reshape(8, 128),
    )
    got = lax.ppermute(message, "gz", [(0, 1), (1, 0)])
    own, sent = call(
        deposit_kernel,
        "deposit",
        [(36, 16, 128)] * 2,
        [((36, 24, 128), F32)] + [((256, 2048), BF16)] * 4,
        source,
        spill,
        chi,
        message,
        got,
    )
    swap = [(0, 1), (1, 0), (2, 3), (3, 2)]
    got = lax.ppermute(sent, "gx", swap)
    held = [(ROWS, 16, 128), (ROWS, 16, 128), (3, 16, 128)]
    *fields, message = call(pair_kernel, "pair", held + [(9, 16, 128)], [], own, got)
    got = lax.ppermute(message, "gx", [(0, 2), (2, 0), (1, 3), (3, 1)])
    *fields, message = call(across_kernel, "across", held + [(PLANES + 3, 8, 128)], [], *fields, got)
    turns = []
    for p in range(2):
        for b in range(n_gy - 1):
            low, high = (2 * p + 1) * n_gy + b, 2 * p * n_gy + b + 1
            turns += [(low, high), (high, low)]
    for low, high in ((0, 2 * n_gy), (2 * n_gy - 1, 4 * n_gy - 1)):
        turns += [(low, high), (high, low)]
    got = lax.ppermute(message, ("gx", "gy"), turns)
    rhs, kappa, v2, message = call(
        functools.partial(down_kernel, n_gy),
        "down",
        [window, window, window, (4 * n_gy, 64, 128)],
        big * 6 + [((256, 128), F32), ((3, 16, 128), F32)],
        *fields,
        got,
        kappa1,
    )
    n = 2 * n_gy
    groups = [[(2 * p + c) * n + g for p in range(2) for g in range(n)] for c in range(2)]
    mine = lax.all_to_all(
        message, everyone, split_axis=0, concat_axis=0, tiled=True, axis_index_groups=groups
    )
    other = lax.ppermute(mine, "gx", swap)
    level1 = (34, 8 * n_gy, 128)
    (e,) = call(
        functools.partial(coarse_kernel, n_gy),
        "coarse",
        [level1],
        [(level1, F32)] * 9 + [((128 * n_gy, 128), F32)],
        mine,
        other,
    )
    (out,) = call(
        functools.partial(up_kernel, n_gy),
        "up",
        [(32, 8, 128)],
        big * 7 + [((18, 16 * n_gy + 8, 128), F32)],
        e,
        rhs,
        kappa,
        v2,
    )
    c = lax.axis_index("gx") & 1
    keep = lax.dynamic_slice_in_dim(out, 16 * c, 16, axis=0)
    give = lax.dynamic_slice_in_dim(out, 16 - 16 * c, 16, axis=0)
    got = lax.ppermute(give, "gx", swap)
    return jnp.where(
        c == 0, jnp.concatenate([keep, got], axis=1), jnp.concatenate([got, keep], axis=1)
    )


def solution(mesh):
    placed = (
        P("gx", "gy", "gz"),
        P(None, "gx", "gy", "gz"),
        P("gx", "gy", "gz", None, None),
        P("gx", "gy", "gz", None),
        P("gx", "gy", "gz", None),
    )
    small = mesh.shape["gx"] == 4 and mesh.shape["gz"] == 2 and mesh.shape["gy"] <= 4
    return jax.shard_map(
        paired if small else general,
        mesh=mesh,
        in_specs=placed,
        out_specs=P("gx", "gy", "gz"),
        check_vma=False,
    )
```

```python
import functools

import jax
import jax.numpy as jnp
from jax import lax
from jax.experimental import pallas as pl
from jax.experimental.pallas import tpu as pltpu
from jax.sharding import PartitionSpec as P

SMOOTH = 2
LEVELS = 3
COARSE_SWEEPS = 8
CAP = 640


OMEGA = 0.8


def padded_2(cells, sides, width):
    for axis, dim in sides:
        count = lax.axis_size(axis)
        ends = count - 1
        head = lax.slice_in_dim(cells, 0, width, axis=dim)
        tail = lax.slice_in_dim(cells, cells.shape[dim] - width, cells.shape[dim], axis=dim)
        cells = jnp.concatenate(
            [
                lax.ppermute(tail, axis, [(i, (i + 1) % count) for i in range(ends)]),
                cells,
                lax.ppermute(head, axis, [((i + 1) % count, i) for i in range(ends)]),
            ],
            axis=dim,
        )
    return cells


def restrict(x):
    s = x.shape
    return x.reshape(s[0] // 2, 2, s[1] // 2, 2, s[2] // 2, 2).mean(axis=(1, 3, 5))


def prolong(e):
    return jnp.repeat(jnp.repeat(jnp.repeat(e, 2, 0), 2, 1), 2, 2)


def neighbours(padded):
    return [
        padded[2:, 1:-1, 1:-1],
        padded[:-2, 1:-1, 1:-1],
        padded[1:-1, 2:, 1:-1],
        padded[1:-1, :-2, 1:-1],
        padded[1:-1, 1:-1, 2:],
        padded[1:-1, 1:-1, :-2],
    ]


def face_pad(x):
    return padded_2(x, (("gx", 0), ("gy", 1), ("gz", 2)), 1)


def coefficients(kappa):
    return [0.5 * (kappa + other) for other in neighbours(face_pad(kappa))]


def apply_op(v, coefs, scale):
    total = jnp.zeros_like(v)
    for coef, other in zip(coefs, neighbours(face_pad(v))):
        total = total + coef * (v - other)
    return scale * total


def cycle(level, rhs, kappa):
    scale = 0.25**level
    coefs = coefficients(kappa)
    diag = scale * (coefs[0] + coefs[1] + coefs[2] + coefs[3] + coefs[4] + coefs[5])
    v = OMEGA * rhs / diag
    for sweep in range((COARSE_SWEEPS if level == LEVELS else SMOOTH) - 1):
        v = v + OMEGA * (rhs - apply_op(v, coefs, scale)) / diag
    if level == LEVELS:
        return v
    resid = rhs - apply_op(v, coefs, scale)
    corr = cycle(level + 1, restrict(resid), restrict(kappa))
    v = v + prolong(corr)
    for sweep in range(SMOOTH):
        v = v + OMEGA * (rhs - apply_op(v, coefs, scale)) / diag
    return v


def general(chi, inducing, record_dest, record_cell, record_value):
    n_gz = lax.axis_size("gz")
    dest = record_dest[0, 0, 0, :, 0]
    cells = record_cell[0, 0, 0]
    values = record_value[0, 0, 0]
    onehot = (dest[:, None] == jnp.arange(n_gz, dtype=jnp.int32)[None, :]).astype(jnp.int32)
    ranks = jnp.sum((jnp.cumsum(onehot, axis=0) - 1) * onehot, axis=1)
    outgoing = jnp.zeros((n_gz, 2, CAP), jnp.float32)
    outgoing = outgoing.at[dest, 0, ranks].set(values)
    outgoing = outgoing.at[dest, 1, ranks].set(cells.astype(jnp.float32))
    incoming = lax.all_to_all(outgoing, "gz", split_axis=0, concat_axis=0, tiled=True)
    in_values = incoming[:, 0].reshape(-1)
    in_cells = incoming[:, 1].reshape(-1).astype(jnp.int32)
    moment_x = face_pad(chi * inducing[0])
    moment_y = face_pad(chi * inducing[1])
    moment_z = face_pad(chi * inducing[2])
    source = -0.5 * (
        moment_x[2:, 1:-1, 1:-1]
        - moment_x[:-2, 1:-1, 1:-1]
        + (moment_y[1:-1, 2:, 1:-1] - moment_y[1:-1, :-2, 1:-1])
        + (moment_z[1:-1, 1:-1, 2:] - moment_z[1:-1, 1:-1, :-2])
    )
    rhs = source.reshape(-1).at[in_cells].add(in_values).reshape(source.shape)
    return cycle(0, rhs, 1.0 + chi)


F32 = jnp.float32
BF16 = jnp.bfloat16
ROWS = 42
PLANES = 36
SIZE = 4


def iota(shape, dim):
    return lax.broadcasted_iota(jnp.int32, shape, dim)


def roll(x, shift, axis):
    shift = shift % x.shape[axis]
    return pltpu.roll(x, shift, axis) if shift else x


def pick(flag, first, second):
    return jnp.where(jnp.full(first.shape, flag, jnp.int32) == 0, first, second)


def dot(a, b):
    total = 0.0
    for _ in range(3):
        part = a.astype(BF16)
        total = total + jnp.dot(part, b.astype(BF16), preferred_element_type=F32)
        a = a - part.astype(F32)
    return total


def halving(offset, factor):
    shape = (128, 128)
    return jnp.where((iota(shape, 0) >> 1) + offset == iota(shape, 1), factor, 0.0).astype(F32)


def place():
    gx, gy, gz = lax.axis_index("gx"), lax.axis_index("gy"), lax.axis_index("gz")
    return gx >> 1, gx & 1, gy, gz


def stretch(x):
    return roll(jnp.concatenate([x, jnp.zeros((8, x.shape[1]), F32)], 0), 4, 0)


def message_kernel(*refs):
    given, (chi, inducing, message, spill), (dest, cell, value, done) = refs[:5], refs[5:9], refs[9:]
    _, _, _, t = place()
    held = (chi, inducing, dest, cell, value)
    copies = [pltpu.make_async_copy(a, b, done.at[i]) for i, (a, b) in enumerate(zip(given, held))]
    for copy in copies:
        copy.start()
    for copy in copies:
        copy.wait()
    lane = iota((16, 128), 1)
    turn = 4 - 3 * t
    wanted = pick(t, (lane < 4).astype(jnp.int32), ((lane >= 1) & (lane < 5)).astype(jnp.int32)) > 0
    k, mx, my, mz = [jnp.zeros((16, 128), F32) for _ in range(4)]
    for x in range(16):
        near = jnp.where(wanted, pltpu.roll(chi[x], turn, 1), 0.0)
        parts = [near * pltpu.roll(inducing[d, x], turn, 1) for d in range(3)]
        one = jnp.where(wanted, 1.0 + near, 0.0)
        k, mx, my, mz = [total + roll(part, 8 * x, 1) for total, part in zip((k, mx, my, mz), [one] + parts)]
    dx = jnp.where(lane < 120, roll(mx, -8, 1), 0.0) - jnp.where(lane >= 8, roll(mx, 8, 1), 0.0)
    y = stretch(my)
    dz = roll(mz, -1, 1) - roll(mz, 1, 1)
    body = -0.5 * (stretch(dx + dz) + (roll(y, -1, 0) - roll(y, 1, 0)))
    lane = iota((24, 128), 1)
    slot = lane & 7
    ends = 0.5 * (jnp.where((lane >= 8) & (lane < 16), roll(stretch(mx), 16, 1), 0.0) - jnp.where(lane < 8, stretch(mx), 0.0))

    def four(tile):
        tile = pick(t, roll(tile, -1, 1), tile)
        return jnp.where(slot < 4, tile, 0.0)

    own = pick(t, jnp.where(slot == 4, body, 0.0), jnp.where(slot == 0, body, 0.0))
    spill[...] = pick(t, roll(own, -3, 1), roll(own, 2, 1))
    message[0:24] = four(body) + jnp.where(slot >= 4, stretch(pick(t, roll(k, 4, 1), roll(k, 3, 1))), 0.0)
    message[24:48] = four(ends)
    message[48:56] = value[...]
    message[56:64] = (dest[...] * 32768 + cell[...]).astype(F32)


def spread_records(records, t, at_row, hi, mid, lo):
    spot = iota((256, 128), 0)
    for j in range(8):
        value = records[48 + j : 49 + j, :]
        code = records[56 + j : 57 + j, :].astype(jnp.int32)
        cells = code & 32767
        z = ((code >> 15) - t) * 128 + (cells & 127)
        far = z - 128 + 131 * t
        column = jnp.where((far >= 0) & (far < 3), z + 1 + 130 * t, 255)
        column = jnp.where((z >= 0) & (z < 128), z, column)
        cut = slice(128 * j, 128 * (j + 1))
        at_row[:, cut] = jnp.where(spot == (cells >> 7), 1.0, 0.0).astype(BF16)
        here = spot == column
        for part in (hi, mid, lo):
            short = value.astype(BF16).astype(F32)
            part[:, cut] = jnp.where(here, short, 0.0).astype(BF16)
            value = value - short
    total = jnp.zeros((256, 256), F32)
    for part in (lo, mid, hi):
        total = total + lax.dot_general(
            at_row[...], part[...], (((1,), (1,)), ((), ())), preferred_element_type=F32
        )
    return total


def source_kernel(chi, inducing, records, source, total, coarse, sums, at_row, hi, mid, lo):
    _, _, _, t = place()
    lane = iota((16, 128), 1)
    zero = jnp.zeros((16, 128), F32)
    mx = [zero, zero] + [chi[x] * inducing[0, x] for x in range(16)] + [zero, zero]
    for i in range(18):
        flat = mx[i + 2] - mx[i]
        if 1 <= i <= 16:
            my, mz = chi[i - 1] * inducing[1, i - 1], chi[i - 1] * inducing[2, i - 1]
            flat = flat + (jnp.where(lane == 127, 0.0, roll(mz, -1, 1)) - jnp.where(lane == 0, 0.0, roll(mz, 1, 1)))
            y = stretch(my)
            source[i] = -0.5 * (stretch(flat) + (roll(y, -1, 0) - roll(y, 1, 0)))
        else:
            source[i] = -0.5 * stretch(flat)
    total[...] = spread_records(records, t, at_row, hi, mid, lo)
    sums[...] = pair_sums(1.0 + chi[...]).reshape(128, 128)
    halves = sums[pl.ds(0, 64, stride=2), :] + sums[pl.ds(1, 64, stride=2), :]
    coarse[...] = dot(halves[:32], halving(0, 0.125)) + dot(halves[32:], halving(64, 0.125))


def deposit_kernel(source, spill, chi, mine, other, own, sent, all_, at_row, hi, mid, lo):
    _, c, _, t = place()
    total = mine[...] + spread_records(other, t, at_row, hi, mid, lo)
    lane = iota((24, 128), 1)
    halo = other[0:24] + spill[...]
    for i in range(18):
        if 1 <= i <= 16:
            at = 16 * (i - 1)
            got = stretch(total[at : at + 16, 128:])
            halo = halo + roll(jnp.where(lane < 4, got, 0.0), 8 * (i - 1), 1)
            add = stretch(total[at : at + 16, :128])
            near = pick(t, roll(other[0:24], 127 - 8 * (i - 1), 1), roll(other[0:24], -3 - 8 * (i - 1), 1))
        else:
            add = jnp.zeros((24, 128), F32)
            by = 0 if i == 0 else -8
            near = pick(t, roll(other[24:48], 127 + by, 1), roll(other[24:48], -3 + by, 1))
        all_[i] = source[i] + add + jnp.where(lane == 127 - 127 * t, near, 0.0)
    for i in range(16):
        all_[18 + i] = stretch(1.0 + chi[i])
    all_[34] = halo
    all_[35] = other[24:48]
    keep, give = pl.multiple_of(8 * c, 8), pl.multiple_of(8 - 8 * c, 8)
    own[...] = all_[:, pl.ds(keep, 16), :]
    sent[...] = all_[:, pl.ds(give, 16), :]


def pair_kernel(own, other, source, kappa, halo, message):
    p, c, _, _ = place()
    source[...] = jnp.zeros_like(source)
    kappa[...] = jnp.zeros_like(kappa)
    source[pl.ds(4 + 16 * c, 18)] = own[0:18]
    low = 4 + 16 * (1 - c)
    source[pl.ds(low, 18)] = source[pl.ds(low, 18)] + other[0:18]
    kappa[pl.ds(5 + 16 * c, 16)] = own[18:34]
    kappa[pl.ds(low + 1, 16)] = other[18:34]
    lane = iota((16, 128), 1)
    tiles = [jnp.zeros((16, 128), F32)] * 3
    for side in range(2):
        cells = roll(pick(c ^ side, own[34], other[34]), 40, 1)
        ends = pick(c ^ side, own[35], other[35])
        before, after = jnp.where(lane < 4, ends, 0.0), jnp.where((lane >= 8) & (lane < 12), ends, 0.0)
        tiles[side] = tiles[side] + jnp.where(lane >= 40, cells, 0.0) + roll(before, 32, 1)
        tiles[side + 1] = tiles[side + 1] + jnp.where(lane < 40, cells, 0.0) + roll(after, 32, 1)
    for i in range(3):
        halo[i] = tiles[i]
    message[0:4] = source[pl.ds(34 - 30 * p, 4)]
    message[4:8] = kappa[pl.ds(33 - 28 * p, 4)]
    message[8] = jnp.where(lane < 40, pick(p, roll(tiles[2], -8, 1), roll(tiles[0], -32, 1)), 0.0)


def across_kernel(source_in, kappa_in, halo_in, other, source, kappa, halo, message):
    p, c, _, _ = place()
    source[...] = source_in[...]
    kappa[...] = kappa_in[...]
    at = 36 - 34 * p
    source[pl.ds(at, 4)] = source[pl.ds(at, 4)] + other[0:4]
    kappa[pl.ds(37 - 36 * p, 4)] = other[4:8]
    zero = jnp.zeros((16, 128), F32)
    halo[0] = halo_in[0] + pick(p, zero, roll(other[8], 8, 1))
    halo[1] = halo_in[1]
    halo[2] = halo_in[2] + pick(p, roll(other[8], 32, 1), zero)
    first = 5 - 4 * p

    def cut(s, k):
        s = pick(c, roll(s, -3, 1)[:, :8], roll(s, -9, 1)[:, :8])
        k = pick(c, k[:, :8], roll(k, -4, 1)[:, :8])
        return jnp.where(iota(s.shape, 1) < 4, s, k)

    def body(i):
        message[pl.ds(i, SIZE)] = cut(source[pl.ds(first + i, SIZE)], kappa[pl.ds(first + i, SIZE)])

    chunked(PLANES, body, SIZE)
    message[PLANES:] = cut(halo[...], halo[...])


def chunked(count, body, size=4):
    def step(i, _):
        body(i * size)
        return 0

    lax.fori_loop(0, count // size, step, 0)


def faces(kap, cx, cy, cz, weight, diag, first, count, scale, closed):
    n = SIZE
    shape = (n,) + kap.shape[1:]
    last_y = iota(shape, 1) == shape[1] - 1
    first_y = iota(shape, 1) == 0
    last_z = iota(shape, 2) == shape[2] - 1
    first_z = iota(shape, 2) == 0

    def body(i):
        r = first + i
        near = kap[pl.ds(r - 1, n + 2)]
        k, up, down = near[1 : n + 1], near[2:], near[:n]
        yu, yd, zu, zd = roll(k, -1, 1), roll(k, 1, 1), roll(k, -1, 2), roll(k, 1, 2)
        if closed:
            yu, yd = jnp.where(last_y, 0.0, yu), jnp.where(first_y, 0.0, yd)
            zu, zd = jnp.where(last_z, 0.0, zu), jnp.where(first_z, 0.0, zd)
        half = 0.5 * scale
        total = half * (6.0 * k + ((up + down) + (yu + yd) + (zu + zd)))
        fy, fz = half * (k + yu), half * (k + zu)
        if closed:
            fy, fz = jnp.where(last_y, 0.0, fy), jnp.where(last_z, 0.0, fz)
        cx[pl.ds(r, n)] = half * (k + up)
        cy[pl.ds(r, n)] = fy
        cz[pl.ds(r, n)] = fz
        diag[pl.ds(r, n)] = total
        weight[pl.ds(r, n)] = jnp.where(k > 0.0, OMEGA / jnp.where(k > 0.0, total, 1.0), 0.0)

    chunked(count, body, n)


def around(v, cx, cy, cz, r, n):
    near, fx = v[pl.ds(r - 1, n + 2)], cx[pl.ds(r - 1, n + 1)]
    here, fy, fz = near[1 : n + 1], cy[pl.ds(r, n)], cz[pl.ds(r, n)]
    return here, (
        (fx[1:] * near[2:] + fx[:n] * near[:n])
        + (fy * roll(here, -1, 1) + roll(fy * here, 1, 1))
        + (fz * roll(here, -1, 2) + roll(fz * here, 1, 2))
    )


def sweep(v, out, rhs, cx, cy, cz, weight, first, count):
    def body(i):
        r = first + i
        here, total = around(v, cx, cy, cz, r, SIZE)
        out[pl.ds(r, SIZE)] = (1.0 - OMEGA) * here + weight[pl.ds(r, SIZE)] * (rhs[pl.ds(r, SIZE)] + total)

    chunked(count, body, SIZE)


def resid(v, rhs, cx, cy, cz, diag, r):
    here, total = around(v, cx, cy, cz, r, SIZE)
    return rhs[pl.ds(r, SIZE)] + total - diag[pl.ds(r, SIZE)] * here


def pair_sums(x):
    x = x.reshape((x.shape[0] // 2, 2) + x.shape[1:])
    return x[:, 0] + x[:, 1]


def down_kernel(
    n_gy, source_in, kappa_in, halo_in, other, kappa1, rhs, kappa, weight, v2, message,
    cx, cy, cz, diag, v1, sums, halo,
):
    p, c, b, t = place()
    first = 5 - 4 * p
    edge = jnp.where(c == 0, b == 0, b == n_gy - 1).astype(jnp.int32)
    for ref in (kappa, cx, weight, v1, v2, rhs):
        ref[0:5] = jnp.zeros((5, 16, 256), F32)
        ref[37:42] = jnp.zeros((5, 16, 256), F32)

    def merge(got):
        n = got.shape[0]
        got = jnp.concatenate([got, jnp.zeros((n, 8, 128), F32)], 1)
        got = pick(edge, got, jnp.zeros_like(got))
        top = iota(got.shape, 1) < 4
        s, k = jnp.where(top, got, 0.0), jnp.where(top, 0.0, got)
        return pick(c, roll(s, 1, 1), roll(s, 11, 1)), pick(c, roll(k, -4, 1), roll(k, 8, 1))

    s, k = merge(other[PLANES:])
    halo[...] = halo_in[...] + jnp.where((iota(s.shape, 2) & 7) < 4, s, k)
    lane = iota((16, 128), 1)
    s_lanes = pick(t, (lane < 3).astype(jnp.int32), (lane >= 125).astype(jnp.int32)) > 0
    k_lanes = pick(t, (lane < 4).astype(jnp.int32), (lane >= 124).astype(jnp.int32)) > 0

    def enter(i):
        r = first + i
        rows = pl.ds(r, SIZE)
        s, k = merge(other[pl.ds(i, SIZE)])
        far_s, far_k = [], []
        for j in range(SIZE):
            tile = halo[(r + j) >> 4]
            by = 8 * ((r + j) & 15)
            far_s.append(jnp.where(s_lanes, pltpu.roll(tile, (127 - by - 2 * t) & 127, 1), 0.0)[None])
            far_k.append(jnp.where(k_lanes, pltpu.roll(tile, (124 - by - 4 * t) & 127, 1), 0.0)[None])
        rhs[rows] = jnp.concatenate([source_in[rows] + s, jnp.concatenate(far_s, 0)], 2)
        kappa[rows] = jnp.concatenate([kappa_in[rows] + k, jnp.concatenate(far_k, 0)], 2)

    chunked(PLANES, enter, SIZE)
    faces(kappa, cx, cy, cz, weight, diag, first, PLANES, 1.0, False)

    def start(i):
        r = pl.ds(first + i, SIZE)
        v1[r] = weight[r] * rhs[r]

    chunked(PLANES, start, SIZE)
    sweep(v1, v2, rhs, cx, cy, cz, weight, first, PLANES)

    def pair(i):
        two = pair_sums(resid(v2, rhs, cx, cy, cz, diag, 5 + i))
        sums[pl.ds(pl.multiple_of(8 * i, 16), 8 * SIZE), :] = two[:, :, :128].reshape(8 * SIZE, 128)

    chunked(32, pair, SIZE)
    halves = sums[pl.ds(0, 128, stride=2), :] + sums[pl.ds(1, 128, stride=2), :]
    packed = dot(halves[:64], halving(0, 0.125)) + dot(halves[64:], halving(64, 0.125))
    low = iota((8, 128), 0) < 4
    for j in range(4):
        even, odd = packed[16 * j : 16 * j + 8], packed[16 * j + 8 : 16 * j + 16]
        tile = jnp.where(low, roll(even, -2, 0), roll(odd, 2, 0))
        for d in range(message.shape[0]):
            message[d, 8 * j : 8 * j + 8, :] = tile
            message[d, 32 + 8 * j : 40 + 8 * j, :] = kappa1[8 * j : 8 * j + 8, :]


def shift(x, by, axis):
    if axis == 0:
        zero = jnp.zeros((1,) + x.shape[1:], x.dtype)
        return jnp.concatenate([x[1:], zero] if by > 0 else [zero, x[:-1]], 0)
    return roll(x, -by, axis)


SIDES = [(axis, by) for axis in range(3) for by in (1, -1)]


class Level:
    def __init__(self, kappa, scale):
        half = 0.5 * scale
        at = iota(kappa.shape, 1)
        ends = {1: at == kappa.shape[1] - 1, -1: at == 0}
        near = [shift(kappa, by, axis) for axis, by in SIDES]
        near[2:4] = [jnp.where(ends[by], 0.0, k) for by, k in zip((1, -1), near[2:4])]
        self.diag = half * (6.0 * kappa + (near[0] + near[1]) + (near[2] + near[3]) + (near[4] + near[5]))
        self.faces = [half * (kappa + other) for other in near]
        self.faces[2:4] = [jnp.where(ends[by], 0.0, f) for by, f in zip((1, -1), self.faces[2:4])]
        inside = kappa > 0.0
        self.weight = jnp.where(inside, OMEGA / jnp.where(inside, self.diag, 1.0), 0.0)

    def around(self, v):
        terms = [f * shift(v, by, axis) for f, (axis, by) in zip(self.faces, SIDES)]
        return (terms[0] + terms[1]) + (terms[2] + terms[3]) + (terms[4] + terms[5])

    def sweep(self, v, rhs):
        return (1.0 - OMEGA) * v + self.weight * (rhs + self.around(v))

    def resid(self, v, rhs):
        return rhs + self.around(v) - self.diag * v


def halved(x, scratch):
    nx, ny = x.shape[0] // 2, x.shape[1] // 2
    pairs = x.reshape(nx, 2, 2 * ny, 128)
    scratch[0 : 2 * nx * ny, :] = (pairs[:, 0] + pairs[:, 1]).reshape(2 * nx * ny, 128)
    return halved_yz(scratch, nx, ny)


def halved_yz(scratch, nx, ny):
    halves = scratch[pl.ds(0, nx * ny, stride=2), :] + scratch[pl.ds(1, nx * ny, stride=2), :]
    return dot(halves, halving(0, 0.125)).reshape(nx, ny, 128)


def doubling():
    shape = (128, 128)
    return jnp.where((iota(shape, 1) >> 1) == iota(shape, 0), 1.0, 0.0).astype(F32)


def doubled_yz(e, scratch):
    nx, ny, _ = e.shape
    wide = dot(e.reshape(nx * ny, 128), doubling())
    scratch[pl.ds(0, nx * ny, stride=2), :] = wide
    scratch[pl.ds(1, nx * ny, stride=2), :] = wide
    return scratch[0 : 2 * nx * ny, :].reshape(nx, 2 * ny, 128)


def doubled(e, scratch):
    e = doubled_yz(e, scratch)
    nx, ny, _ = e.shape
    return jnp.broadcast_to(e[:, None], (nx, 2, ny, 128)).reshape(2 * nx, ny, 128)


def coarse_kernel(n_gy, mine, other, e_out, k1, r1, cx, cy, cz, weight, diag, va, vb, sums):
    p, c, b, t = place()
    n_y = 8 * n_gy
    for ref in (k1, cx, va, vb):
        ref[0] = jnp.zeros((n_y, 128), F32)
        ref[33] = jnp.zeros((n_y, 128), F32)
    left = iota((8, 128), 1) < 64
    top = iota((8, 128), 0) < 4
    for gx in range(4):
        for gy in range(n_gy):
            for x in range(4):
                cut = slice(32 + 8 * x, 40 + 8 * x)
                both = [[ref[((gx >> 1) * n_gy + gy) * 2 + gz, cut, :] for ref in (mine, other)] for gz in range(2)]
                near, far = [pick(c ^ (gx & 1), a, o) for a, o in both]
                spot = slice(8 * gy, 8 * gy + 8)
                k1[1 + 8 * gx + x, spot, :] = jnp.where(left, near, roll(far, 64, 1))
                k1[1 + 8 * gx + 4 + x, spot, :] = jnp.where(left, roll(near, 64, 1), far)
    for pp in range(2):
        for gy in range(n_gy):
            for j in range(4):
                cut = slice(8 * j, 8 * j + 8)
                evens, odds = [], []
                for gz in range(2):
                    a = mine[(pp * n_gy + gy) * 2 + gz, cut, :]
                    o = other[(pp * n_gy + gy) * 2 + gz, cut, :]
                    first, second = pick(c, a, o), pick(c, o, a)
                    evens.append(jnp.where(top, first, roll(second, 4, 0)))
                    odds.append(jnp.where(top, roll(first, 4, 0), second))
                spot = slice(8 * gy, 8 * gy + 8)
                for odd, (near, far) in enumerate((evens, odds)):
                    r1[1 + 16 * pp + 2 * j + odd, spot, :] = jnp.where(left, near, roll(far, 64, 1))
                    r1[1 + 16 * pp + 8 + 2 * j + odd, spot, :] = jnp.where(left, roll(near, 64, 1), far)
    faces(k1, cx, cy, cz, weight, diag, 1, 32, 0.25, True)

    def start(i):
        r = pl.ds(1 + i, SIZE)
        va[r] = weight[r] * r1[r]

    chunked(32, start, SIZE)
    sweep(va, vb, r1, cx, cy, cz, weight, 1, 32)
    step = n_y * SIZE // 2

    def pair(i):
        two = pair_sums(resid(vb, r1, cx, cy, cz, diag, 1 + i))
        sums[pl.ds(pl.multiple_of(n_y // 2 * i, 8), step), :] = two.reshape(step, 128)

    chunked(32, pair, SIZE)
    r2 = halved_yz(sums, 16, n_y // 2)

    def kappa_pair(i):
        two = pair_sums(k1[pl.ds(1 + i, SIZE)])
        sums[pl.ds(pl.multiple_of(n_y // 2 * i, 8), step), :] = two.reshape(step, 128)

    chunked(32, kappa_pair, SIZE)
    k2 = halved_yz(sums, 16, n_y // 2)
    middle = Level(k2, 0.0625)
    v2 = middle.weight * r2
    v2 = middle.sweep(v2, r2)
    r3 = halved(middle.resid(v2, r2), sums)
    bottom = Level(halved(k2, sums), 0.015625)
    v3 = bottom.weight * r3
    for _ in range(COARSE_SWEEPS - 1):
        v3 = bottom.sweep(v3, r3)
    v2 = v2 + doubled(v3, sums)
    for _ in range(SMOOTH):
        v2 = middle.sweep(v2, r2)
    e1 = doubled_yz(v2, sums)
    for i in range(16):
        vb[1 + 2 * i] = vb[1 + 2 * i] + e1[i]
        vb[2 + 2 * i] = vb[2 + 2 * i] + e1[i]
    sweep(vb, va, r1, cx, cy, cz, weight, 1, 32)
    sweep(va, vb, r1, cx, cy, cz, weight, 1, 32)
    e_out[...] = vb[...]


def up_kernel(n_gy, e_in, rhs, kappa, weight, v2, out, cx, cy, cz, va, vb, tall):
    p, c, b, t = place()
    first = 5 - 4 * p
    n_y = 8 * n_gy
    for ref in (va, vb, cx):
        ref[0:5] = jnp.zeros((5, 16, 256), F32)
        ref[37:42] = jnp.zeros((5, 16, 256), F32)

    def face(i):
        near = kappa[pl.ds(first + i, SIZE + 1)]
        r, k = pl.ds(first + i, SIZE), near[:SIZE]
        cx[r] = 0.5 * (k + near[1:])
        cy[r] = 0.5 * (k + roll(k, -1, 1))
        cz[r] = 0.5 * (k + roll(k, -1, 2))

    chunked(PLANES, face, SIZE)
    tall[:, 0:8, :] = jnp.zeros((18, 8, 128), F32)
    tall[:, 2 * n_y : 2 * n_y + 8, :] = jnp.zeros((18, 8, 128), F32)
    for k in range(18):
        e = e_in[16 * p + k]
        tall[k, pl.ds(4, n_y, stride=2), :] = e
        tall[k, pl.ds(5, n_y, stride=2), :] = e
    window = tall[:, pl.ds(pl.multiple_of(16 * b + 8 * c, 8), 16), :]
    shape = (128, 256)
    z = iota(shape, 1)
    z = jnp.where(z < 192, z, z - 256)
    spread = jnp.where(64 * t + (z >> 1) == iota(shape, 0), 1.0, 0.0).astype(F32)
    e = dot(window.reshape(288, 128), spread).reshape(18, 16, 256)
    for k in range(18):
        for r in (2 * k + 3, 2 * k + 4):
            va[r] = v2[r] + jnp.where(weight[r] > 0.0, e[k], 0.0)
    sweep(va, vb, rhs, cx, cy, cz, weight, first, PLANES)

    def last(i):
        r = pl.ds(5 + i, SIZE)
        here, total = around(vb, cx, cy, cz, 5 + i, SIZE)
        done = (1.0 - OMEGA) * here + weight[r] * (rhs[r] + total)
        out[pl.ds(i, SIZE)] = roll(done[:, :, :128], -4, 1)[:, :8]

    chunked(32, last, SIZE)


def call(kernel, name, outs, scratch, *args):
    where = pltpu.HBM if name == "message" else pltpu.VMEM
    if name == "message":
        args = [pltpu.with_memory_space_constraint(a, pltpu.HBM) for a in args]
    return pl.pallas_call(
        kernel,
        name=name,
        out_shape=[jax.ShapeDtypeStruct(s, F32) for s in outs],
        in_specs=[pl.BlockSpec(memory_space=where)] * len(args),
        out_specs=[pl.BlockSpec(memory_space=pltpu.VMEM)] * len(outs),
        scratch_shapes=[
            pltpu.SemaphoreType.DMA((s,)) if isinstance(s, int) else pltpu.VMEM(*s) for s in scratch
        ],
        compiler_params=pltpu.CompilerParams(vmem_limit_bytes=16 * 1024 * 1024),
        cost_estimate=pl.CostEstimate(flops=10**7, bytes_accessed=4 * 10**6, transcendentals=0),
    )(*args)


def paired(chi, inducing, record_dest, record_cell, record_value):
    n_gy = lax.axis_size("gy")
    everyone = ("gx", "gy", "gz")
    window = (ROWS, 16, 256)
    big = [(window, F32)]
    chi, inducing, message, spill = call(
        message_kernel,
        "message",
        [(16, 16, 128), (3, 16, 16, 128), (64, 128), (24, 128)],
        [((8, 128), jnp.int32)] * 2 + [((8, 128), F32), 5],
        chi,
        inducing,
        record_dest.reshape(8, 128),
        record_cell.reshape(8, 128),
        record_value.reshape(8, 128),
    )
    got = lax.ppermute(message, "gz", [(0, 1), (1, 0)])
    spread = [((256, 1024), BF16)] * 4
    source, total, kappa1 = call(
        source_kernel,
        "source",
        [(18, 24, 128), (256, 256), (32, 128)],
        [((128, 128), F32)] + spread,
        chi,
        inducing,
        message,
    )
    own, sent = call(
        deposit_kernel,
        "deposit",
        [(36, 16, 128)] * 2,
        [((36, 24, 128), F32)] + spread,
        source,
        spill,
        chi,
        total,
        got,
    )
    swap = [(0, 1), (1, 0), (2, 3), (3, 2)]
    got = lax.ppermute(sent, "gx", swap)
    held = [(ROWS, 16, 128), (ROWS, 16, 128), (3, 16, 128)]
    *fields, message = call(pair_kernel, "pair", held + [(9, 16, 128)], [], own, got)
    got = lax.ppermute(message, "gx", [(0, 2), (2, 0), (1, 3), (3, 1)])
    *fields, message = call(across_kernel, "across", held + [(PLANES + 3, 8, 128)], [], *fields, got)
    turns = []
    for p in range(2):
        for b in range(n_gy - 1):
            low, high = (2 * p + 1) * n_gy + b, 2 * p * n_gy + b + 1
            turns += [(low, high), (high, low)]
    for low, high in ((0, 2 * n_gy), (2 * n_gy - 1, 4 * n_gy - 1)):
        turns += [(low, high), (high, low)]
    got = lax.ppermute(message, ("gx", "gy"), turns)
    *fine, message = call(
        functools.partial(down_kernel, n_gy),
        "down",
        [window] * 4 + [(4 * n_gy, 64, 128)],
        big * 5 + [((256, 128), F32), ((3, 16, 128), F32)],
        *fields,
        got,
        kappa1,
    )
    n = 2 * n_gy
    groups = [[(2 * p + c) * n + g for p in range(2) for g in range(n)] for c in range(2)]
    mine = lax.all_to_all(
        message, everyone, split_axis=0, concat_axis=0, tiled=True, axis_index_groups=groups
    )
    other = lax.ppermute(mine, "gx", swap)
    level1 = (34, 8 * n_gy, 128)
    (e,) = call(
        functools.partial(coarse_kernel, n_gy),
        "coarse",
        [level1],
        [(level1, F32)] * 9 + [((128 * n_gy, 128), F32)],
        mine,
        other,
    )
    (out,) = call(
        functools.partial(up_kernel, n_gy),
        "up",
        [(32, 8, 128)],
        big * 5 + [((18, 16 * n_gy + 8, 128), F32)],
        e,
        *fine,
    )
    c = lax.axis_index("gx") & 1
    keep = lax.dynamic_slice_in_dim(out, 16 * c, 16, axis=0)
    give = lax.dynamic_slice_in_dim(out, 16 - 16 * c, 16, axis=0)
    got = lax.ppermute(give, "gx", swap)
    return jnp.where(
        c == 0, jnp.concatenate([keep, got], axis=1), jnp.concatenate([got, keep], axis=1)
    )


def solution(mesh):
    placed = (
        P("gx", "gy", "gz"),
        P(None, "gx", "gy", "gz"),
        P("gx", "gy", "gz", None, None),
        P("gx", "gy", "gz", None),
        P("gx", "gy", "gz", None),
    )
    small = mesh.shape["gx"] == 4 and mesh.shape["gz"] == 2 and mesh.shape["gy"] <= 4
    return jax.shard_map(
        paired if small else general,
        mesh=mesh,
        in_specs=placed,
        out_specs=P("gx", "gy", "gz"),
        check_vma=False,
    )
```

```python
import functools

import jax
import jax.numpy as jnp
from jax import lax
from jax.experimental import pallas as pl
from jax.experimental.pallas import tpu as pltpu
from jax.sharding import PartitionSpec as P

SMOOTH = 2
LEVELS = 3
COARSE_SWEEPS = 8
CAP = 640


OMEGA = 0.8


def padded_2(cells, sides, width):
    for axis, dim in sides:
        count = lax.axis_size(axis)
        ends = count - 1
        head = lax.slice_in_dim(cells, 0, width, axis=dim)
        tail = lax.slice_in_dim(cells, cells.shape[dim] - width, cells.shape[dim], axis=dim)
        cells = jnp.concatenate(
            [
                lax.ppermute(tail, axis, [(i, (i + 1) % count) for i in range(ends)]),
                cells,
                lax.ppermute(head, axis, [((i + 1) % count, i) for i in range(ends)]),
            ],
            axis=dim,
        )
    return cells


def restrict(x):
    s = x.shape
    return x.reshape(s[0] // 2, 2, s[1] // 2, 2, s[2] // 2, 2).mean(axis=(1, 3, 5))


def prolong(e):
    return jnp.repeat(jnp.repeat(jnp.repeat(e, 2, 0), 2, 1), 2, 2)


def neighbours(padded):
    return [
        padded[2:, 1:-1, 1:-1],
        padded[:-2, 1:-1, 1:-1],
        padded[1:-1, 2:, 1:-1],
        padded[1:-1, :-2, 1:-1],
        padded[1:-1, 1:-1, 2:],
        padded[1:-1, 1:-1, :-2],
    ]


def face_pad(x):
    return padded_2(x, (("gx", 0), ("gy", 1), ("gz", 2)), 1)


def coefficients(kappa):
    return [0.5 * (kappa + other) for other in neighbours(face_pad(kappa))]


def apply_op(v, coefs, scale):
    total = jnp.zeros_like(v)
    for coef, other in zip(coefs, neighbours(face_pad(v))):
        total = total + coef * (v - other)
    return scale * total


def cycle(level, rhs, kappa):
    scale = 0.25**level
    coefs = coefficients(kappa)
    diag = scale * (coefs[0] + coefs[1] + coefs[2] + coefs[3] + coefs[4] + coefs[5])
    v = OMEGA * rhs / diag
    for sweep in range((COARSE_SWEEPS if level == LEVELS else SMOOTH) - 1):
        v = v + OMEGA * (rhs - apply_op(v, coefs, scale)) / diag
    if level == LEVELS:
        return v
    resid = rhs - apply_op(v, coefs, scale)
    corr = cycle(level + 1, restrict(resid), restrict(kappa))
    v = v + prolong(corr)
    for sweep in range(SMOOTH):
        v = v + OMEGA * (rhs - apply_op(v, coefs, scale)) / diag
    return v


def general(chi, inducing, record_dest, record_cell, record_value):
    n_gz = lax.axis_size("gz")
    dest = record_dest[0, 0, 0, :, 0]
    cells = record_cell[0, 0, 0]
    values = record_value[0, 0, 0]
    onehot = (dest[:, None] == jnp.arange(n_gz, dtype=jnp.int32)[None, :]).astype(jnp.int32)
    ranks = jnp.sum((jnp.cumsum(onehot, axis=0) - 1) * onehot, axis=1)
    outgoing = jnp.zeros((n_gz, 2, CAP), jnp.float32)
    outgoing = outgoing.at[dest, 0, ranks].set(values)
    outgoing = outgoing.at[dest, 1, ranks].set(cells.astype(jnp.float32))
    incoming = lax.all_to_all(outgoing, "gz", split_axis=0, concat_axis=0, tiled=True)
    in_values = incoming[:, 0].reshape(-1)
    in_cells = incoming[:, 1].reshape(-1).astype(jnp.int32)
    moment_x = face_pad(chi * inducing[0])
    moment_y = face_pad(chi * inducing[1])
    moment_z = face_pad(chi * inducing[2])
    source = -0.5 * (
        moment_x[2:, 1:-1, 1:-1]
        - moment_x[:-2, 1:-1, 1:-1]
        + (moment_y[1:-1, 2:, 1:-1] - moment_y[1:-1, :-2, 1:-1])
        + (moment_z[1:-1, 1:-1, 2:] - moment_z[1:-1, 1:-1, :-2])
    )
    rhs = source.reshape(-1).at[in_cells].add(in_values).reshape(source.shape)
    return cycle(0, rhs, 1.0 + chi)


F32 = jnp.float32
BF16 = jnp.bfloat16
ROWS = 42
PLANES = 36
SIZE = 12


def iota(shape, dim):
    return lax.broadcasted_iota(jnp.int32, shape, dim)


def roll(x, shift, axis):
    shift = shift % x.shape[axis]
    return pltpu.roll(x, shift, axis) if shift else x


def pick(flag, first, second):
    return jnp.where(jnp.full(first.shape, flag, jnp.int32) == 0, first, second)


def dot(a, b):
    total = 0.0
    for _ in range(3):
        part = a.astype(BF16)
        total = total + jnp.dot(part, b.astype(BF16), preferred_element_type=F32)
        a = a - part.astype(F32)
    return total


def halving(offset, factor):
    shape = (128, 128)
    return jnp.where((iota(shape, 0) >> 1) + offset == iota(shape, 1), factor, 0.0).astype(F32)


def place():
    gx, gy, gz = lax.axis_index("gx"), lax.axis_index("gy"), lax.axis_index("gz")
    return gx >> 1, gx & 1, gy, gz


def stretch(x):
    return roll(jnp.concatenate([x, jnp.zeros((8, x.shape[1]), F32)], 0), 4, 0)


def message_kernel(*refs):
    given, (chi, inducing, message, spill), (dest, cell, value, done) = refs[:5], refs[5:9], refs[9:]
    _, _, _, t = place()
    held = (chi, inducing, dest, cell, value)
    copies = [pltpu.make_async_copy(a, b, done.at[i]) for i, (a, b) in enumerate(zip(given, held))]
    for copy in copies:
        copy.start()
    for copy in copies:
        copy.wait()
    lane = iota((16, 128), 1)
    turn = 4 - 3 * t
    wanted = pick(t, (lane < 4).astype(jnp.int32), ((lane >= 1) & (lane < 5)).astype(jnp.int32)) > 0
    k, mx, my, mz = [jnp.zeros((16, 128), F32) for _ in range(4)]
    for x in range(16):
        near = jnp.where(wanted, pltpu.roll(chi[x], turn, 1), 0.0)
        parts = [near * pltpu.roll(inducing[d, x], turn, 1) for d in range(3)]
        one = jnp.where(wanted, 1.0 + near, 0.0)
        k, mx, my, mz = [total + roll(part, 8 * x, 1) for total, part in zip((k, mx, my, mz), [one] + parts)]
    dx = jnp.where(lane < 120, roll(mx, -8, 1), 0.0) - jnp.where(lane >= 8, roll(mx, 8, 1), 0.0)
    y = stretch(my)
    dz = roll(mz, -1, 1) - roll(mz, 1, 1)
    body = -0.5 * (stretch(dx + dz) + (roll(y, -1, 0) - roll(y, 1, 0)))
    lane = iota((24, 128), 1)
    slot = lane & 7
    ends = 0.5 * (jnp.where((lane >= 8) & (lane < 16), roll(stretch(mx), 16, 1), 0.0) - jnp.where(lane < 8, stretch(mx), 0.0))

    def four(tile):
        tile = pick(t, roll(tile, -1, 1), tile)
        return jnp.where(slot < 4, tile, 0.0)

    own = pick(t, jnp.where(slot == 4, body, 0.0), jnp.where(slot == 0, body, 0.0))
    spill[...] = pick(t, roll(own, -3, 1), roll(own, 2, 1))
    message[0:24] = four(body) + jnp.where(slot >= 4, stretch(pick(t, roll(k, 4, 1), roll(k, 3, 1))), 0.0)
    message[24:48] = four(ends)
    message[48:56] = value[...]
    message[56:64] = (dest[...] * 32768 + cell[...]).astype(F32)


def spread_records(records, t, at_row, hi, mid, lo):
    spot = iota((256, 128), 0)
    for j in range(8):
        value = records[48 + j : 49 + j, :]
        code = records[56 + j : 57 + j, :].astype(jnp.int32)
        cells = code & 32767
        z = ((code >> 15) - t) * 128 + (cells & 127)
        far = z - 128 + 131 * t
        column = jnp.where((far >= 0) & (far < 3), z + 1 + 130 * t, 255)
        column = jnp.where((z >= 0) & (z < 128), z, column)
        cut = slice(128 * j, 128 * (j + 1))
        at_row[:, cut] = jnp.where(spot == (cells >> 7), 1.0, 0.0).astype(BF16)
        here = spot == column
        for part in (hi, mid, lo):
            short = value.astype(BF16).astype(F32)
            part[:, cut] = jnp.where(here, short, 0.0).astype(BF16)
            value = value - short
    total = jnp.zeros((256, 256), F32)
    for part in (lo, mid, hi):
        total = total + lax.dot_general(
            at_row[...], part[...], (((1,), (1,)), ((), ())), preferred_element_type=F32
        )
    return total


def source_kernel(chi, inducing, records, source, total, coarse, sums, at_row, hi, mid, lo):
    _, _, _, t = place()
    lane = iota((16, 128), 1)
    zero = jnp.zeros((16, 128), F32)
    mx = [zero, zero] + [chi[x] * inducing[0, x] for x in range(16)] + [zero, zero]
    for i in range(18):
        flat = mx[i + 2] - mx[i]
        if 1 <= i <= 16:
            my, mz = chi[i - 1] * inducing[1, i - 1], chi[i - 1] * inducing[2, i - 1]
            flat = flat + (jnp.where(lane == 127, 0.0, roll(mz, -1, 1)) - jnp.where(lane == 0, 0.0, roll(mz, 1, 1)))
            y = stretch(my)
            source[i] = -0.5 * (stretch(flat) + (roll(y, -1, 0) - roll(y, 1, 0)))
        else:
            source[i] = -0.5 * stretch(flat)
    total[...] = spread_records(records, t, at_row, hi, mid, lo)
    sums[...] = pair_sums(1.0 + chi[...]).reshape(128, 128)
    halves = sums[pl.ds(0, 64, stride=2), :] + sums[pl.ds(1, 64, stride=2), :]
    coarse[...] = dot(halves[:32], halving(0, 0.125)) + dot(halves[32:], halving(64, 0.125))


def deposit_kernel(source, spill, chi, mine, other, own, sent, all_, at_row, hi, mid, lo):
    _, c, _, t = place()
    total = mine[...] + spread_records(other, t, at_row, hi, mid, lo)
    lane = iota((24, 128), 1)
    halo = other[0:24] + spill[...]
    for i in range(18):
        if 1 <= i <= 16:
            at = 16 * (i - 1)
            got = stretch(total[at : at + 16, 128:])
            halo = halo + roll(jnp.where(lane < 4, got, 0.0), 8 * (i - 1), 1)
            add = stretch(total[at : at + 16, :128])
            near = pick(t, roll(other[0:24], 127 - 8 * (i - 1), 1), roll(other[0:24], -3 - 8 * (i - 1), 1))
        else:
            add = jnp.zeros((24, 128), F32)
            by = 0 if i == 0 else -8
            near = pick(t, roll(other[24:48], 127 + by, 1), roll(other[24:48], -3 + by, 1))
        all_[i] = source[i] + add + jnp.where(lane == 127 - 127 * t, near, 0.0)
    for i in range(16):
        all_[18 + i] = stretch(1.0 + chi[i])
    all_[34] = halo
    all_[35] = other[24:48]
    keep, give = pl.multiple_of(8 * c, 8), pl.multiple_of(8 - 8 * c, 8)
    own[...] = all_[:, pl.ds(keep, 16), :]
    sent[...] = all_[:, pl.ds(give, 16), :]


def pair_kernel(own, other, source, kappa, halo, message):
    p, c, _, _ = place()
    source[...] = jnp.zeros_like(source)
    kappa[...] = jnp.zeros_like(kappa)
    source[pl.ds(4 + 16 * c, 18)] = own[0:18]
    low = 4 + 16 * (1 - c)
    source[pl.ds(low, 18)] = source[pl.ds(low, 18)] + other[0:18]
    kappa[pl.ds(5 + 16 * c, 16)] = own[18:34]
    kappa[pl.ds(low + 1, 16)] = other[18:34]
    lane = iota((16, 128), 1)
    tiles = [jnp.zeros((16, 128), F32)] * 3
    for side in range(2):
        cells = roll(pick(c ^ side, own[34], other[34]), 40, 1)
        ends = pick(c ^ side, own[35], other[35])
        before, after = jnp.where(lane < 4, ends, 0.0), jnp.where((lane >= 8) & (lane < 12), ends, 0.0)
        tiles[side] = tiles[side] + jnp.where(lane >= 40, cells, 0.0) + roll(before, 32, 1)
        tiles[side + 1] = tiles[side + 1] + jnp.where(lane < 40, cells, 0.0) + roll(after, 32, 1)
    for i in range(3):
        halo[i] = tiles[i]
    message[0:4] = source[pl.ds(34 - 30 * p, 4)]
    message[4:8] = kappa[pl.ds(33 - 28 * p, 4)]
    message[8] = jnp.where(lane < 40, pick(p, roll(tiles[2], -8, 1), roll(tiles[0], -32, 1)), 0.0)


def across_kernel(source_in, kappa_in, halo_in, other, source, kappa, halo, message):
    p, c, _, _ = place()
    source[...] = source_in[...]
    kappa[...] = kappa_in[...]
    at = 36 - 34 * p
    source[pl.ds(at, 4)] = source[pl.ds(at, 4)] + other[0:4]
    kappa[pl.ds(37 - 36 * p, 4)] = other[4:8]
    zero = jnp.zeros((16, 128), F32)
    halo[0] = halo_in[0] + pick(p, zero, roll(other[8], 8, 1))
    halo[1] = halo_in[1]
    halo[2] = halo_in[2] + pick(p, roll(other[8], 32, 1), zero)
    first = 5 - 4 * p

    def cut(s, k):
        s = pick(c, roll(s, -3, 1)[:, :8], roll(s, -9, 1)[:, :8])
        k = pick(c, k[:, :8], roll(k, -4, 1)[:, :8])
        return jnp.where(iota(s.shape, 1) < 4, s, k)

    def body(i):
        message[pl.ds(i, SIZE)] = cut(source[pl.ds(first + i, SIZE)], kappa[pl.ds(first + i, SIZE)])

    chunked(PLANES, body, SIZE)
    message[PLANES:] = cut(halo[...], halo[...])


def chunked(count, body, size=4):
    def step(i, _):
        body(i * size)
        return 0

    lax.fori_loop(0, count // size, step, 0)


def faces(kap, cx, cy, cz, weight, diag, first, count, scale, closed, n):
    shape = (n,) + kap.shape[1:]
    last_y = iota(shape, 1) == shape[1] - 1
    first_y = iota(shape, 1) == 0
    last_z = iota(shape, 2) == shape[2] - 1
    first_z = iota(shape, 2) == 0

    def body(i):
        r = first + i
        near = kap[pl.ds(r - 1, n + 2)]
        k, up, down = near[1 : n + 1], near[2:], near[:n]
        yu, yd, zu, zd = roll(k, -1, 1), roll(k, 1, 1), roll(k, -1, 2), roll(k, 1, 2)
        if closed:
            yu, yd = jnp.where(last_y, 0.0, yu), jnp.where(first_y, 0.0, yd)
            zu, zd = jnp.where(last_z, 0.0, zu), jnp.where(first_z, 0.0, zd)
        half = 0.5 * scale
        total = half * (6.0 * k + ((up + down) + (yu + yd) + (zu + zd)))
        fy, fz = half * (k + yu), half * (k + zu)
        if closed:
            fy, fz = jnp.where(last_y, 0.0, fy), jnp.where(last_z, 0.0, fz)
        cx[pl.ds(r, n)] = half * (k + up)
        cy[pl.ds(r, n)] = fy
        cz[pl.ds(r, n)] = fz
        diag[pl.ds(r, n)] = total
        weight[pl.ds(r, n)] = jnp.where(k > 0.0, OMEGA / jnp.where(k > 0.0, total, 1.0), 0.0)

    chunked(count, body, n)


def around(v, cx, cy, cz, r, n):
    near, fx = v[pl.ds(r - 1, n + 2)], cx[pl.ds(r - 1, n + 1)]
    here, fy, fz = near[1 : n + 1], cy[pl.ds(r, n)], cz[pl.ds(r, n)]
    return here, (
        (fx[1:] * near[2:] + fx[:n] * near[:n])
        + (fy * roll(here, -1, 1) + roll(fy * here, 1, 1))
        + (fz * roll(here, -1, 2) + roll(fz * here, 1, 2))
    )


def sweep(v, out, rhs, cx, cy, cz, weight, first, count, n):
    def body(i):
        r = first + i
        here, total = around(v, cx, cy, cz, r, n)
        out[pl.ds(r, n)] = (1.0 - OMEGA) * here + weight[pl.ds(r, n)] * (rhs[pl.ds(r, n)] + total)

    chunked(count, body, n)


def resid(v, rhs, cx, cy, cz, diag, r, n):
    here, total = around(v, cx, cy, cz, r, n)
    return rhs[pl.ds(r, n)] + total - diag[pl.ds(r, n)] * here


def pair_sums(x):
    x = x.reshape((x.shape[0] // 2, 2) + x.shape[1:])
    return x[:, 0] + x[:, 1]


def down_kernel(
    n_gy, source_in, kappa_in, halo_in, other, kappa1, rhs, kappa, weight, v2, message,
    cx, cy, cz, diag, v1, sums, halo,
):
    p, c, b, t = place()
    first = 5 - 4 * p
    edge = jnp.where(c == 0, b == 0, b == n_gy - 1).astype(jnp.int32)
    for ref in (kappa, cx, weight, v1, v2, rhs):
        ref[0:5] = jnp.zeros((5, 16, 256), F32)
        ref[37:42] = jnp.zeros((5, 16, 256), F32)

    def merge(got):
        n = got.shape[0]
        got = jnp.concatenate([got, jnp.zeros((n, 8, 128), F32)], 1)
        got = pick(edge, got, jnp.zeros_like(got))
        top = iota(got.shape, 1) < 4
        s, k = jnp.where(top, got, 0.0), jnp.where(top, 0.0, got)
        return pick(c, roll(s, 1, 1), roll(s, 11, 1)), pick(c, roll(k, -4, 1), roll(k, 8, 1))

    s, k = merge(other[PLANES:])
    halo[...] = halo_in[...] + jnp.where((iota(s.shape, 2) & 7) < 4, s, k)
    lane = iota((16, 128), 1)
    s_lanes = pick(t, (lane < 3).astype(jnp.int32), (lane >= 125).astype(jnp.int32)) > 0
    k_lanes = pick(t, (lane < 4).astype(jnp.int32), (lane >= 124).astype(jnp.int32)) > 0

    def enter(i):
        r = first + i
        rows = pl.ds(r, SIZE)
        s, k = merge(other[pl.ds(i, SIZE)])
        far_s, far_k = [], []
        for j in range(SIZE):
            tile = halo[(r + j) >> 4]
            by = 8 * ((r + j) & 15)
            far_s.append(jnp.where(s_lanes, pltpu.roll(tile, (127 - by - 2 * t) & 127, 1), 0.0)[None])
            far_k.append(jnp.where(k_lanes, pltpu.roll(tile, (124 - by - 4 * t) & 127, 1), 0.0)[None])
        rhs[rows] = jnp.concatenate([source_in[rows] + s, jnp.concatenate(far_s, 0)], 2)
        kappa[rows] = jnp.concatenate([kappa_in[rows] + k, jnp.concatenate(far_k, 0)], 2)

    chunked(PLANES, enter, SIZE)
    faces(kappa, cx, cy, cz, weight, diag, first, PLANES, 1.0, False, PLANES)

    rows = pl.ds(first, PLANES)
    v1[rows] = weight[rows] * rhs[rows]
    sweep(v1, v2, rhs, cx, cy, cz, weight, first, PLANES, PLANES)

    two = pair_sums(resid(v2, rhs, cx, cy, cz, diag, 5, 32))
    sums[...] = two[:, :, :128].reshape(256, 128)
    halves = sums[pl.ds(0, 128, stride=2), :] + sums[pl.ds(1, 128, stride=2), :]
    packed = dot(halves[:64], halving(0, 0.125)) + dot(halves[64:], halving(64, 0.125))
    low = iota((8, 128), 0) < 4
    for j in range(4):
        even, odd = packed[16 * j : 16 * j + 8], packed[16 * j + 8 : 16 * j + 16]
        tile = jnp.where(low, roll(even, -2, 0), roll(odd, 2, 0))
        for d in range(message.shape[0]):
            message[d, 8 * j : 8 * j + 8, :] = tile
            message[d, 32 + 8 * j : 40 + 8 * j, :] = kappa1[8 * j : 8 * j + 8, :]


def shift(x, by, axis):
    if axis == 0:
        zero = jnp.zeros((1,) + x.shape[1:], x.dtype)
        return jnp.concatenate([x[1:], zero] if by > 0 else [zero, x[:-1]], 0)
    return roll(x, -by, axis)


SIDES = [(axis, by) for axis in range(3) for by in (1, -1)]


class Level:
    def __init__(self, kappa, scale):
        half = 0.5 * scale
        at = iota(kappa.shape, 1)
        ends = {1: at == kappa.shape[1] - 1, -1: at == 0}
        near = [shift(kappa, by, axis) for axis, by in SIDES]
        near[2:4] = [jnp.where(ends[by], 0.0, k) for by, k in zip((1, -1), near[2:4])]
        self.diag = half * (6.0 * kappa + (near[0] + near[1]) + (near[2] + near[3]) + (near[4] + near[5]))
        self.faces = [half * (kappa + other) for other in near]
        self.faces[2:4] = [jnp.where(ends[by], 0.0, f) for by, f in zip((1, -1), self.faces[2:4])]
        inside = kappa > 0.0
        self.weight = jnp.where(inside, OMEGA / jnp.where(inside, self.diag, 1.0), 0.0)

    def around(self, v):
        terms = [f * shift(v, by, axis) for f, (axis, by) in zip(self.faces, SIDES)]
        return (terms[0] + terms[1]) + (terms[2] + terms[3]) + (terms[4] + terms[5])

    def sweep(self, v, rhs):
        return (1.0 - OMEGA) * v + self.weight * (rhs + self.around(v))

    def resid(self, v, rhs):
        return rhs + self.around(v) - self.diag * v


def halved(x, scratch):
    nx, ny = x.shape[0] // 2, x.shape[1] // 2
    pairs = x.reshape(nx, 2, 2 * ny, 128)
    scratch[0 : 2 * nx * ny, :] = (pairs[:, 0] + pairs[:, 1]).reshape(2 * nx * ny, 128)
    return halved_yz(scratch, nx, ny)


def halved_yz(scratch, nx, ny):
    halves = scratch[pl.ds(0, nx * ny, stride=2), :] + scratch[pl.ds(1, nx * ny, stride=2), :]
    return dot(halves, halving(0, 0.125)).reshape(nx, ny, 128)


def doubling():
    shape = (128, 128)
    return jnp.where((iota(shape, 1) >> 1) == iota(shape, 0), 1.0, 0.0).astype(F32)


def doubled_yz(e, scratch):
    nx, ny, _ = e.shape
    wide = dot(e.reshape(nx * ny, 128), doubling())
    scratch[pl.ds(0, nx * ny, stride=2), :] = wide
    scratch[pl.ds(1, nx * ny, stride=2), :] = wide
    return scratch[0 : 2 * nx * ny, :].reshape(nx, 2 * ny, 128)


def doubled(e, scratch):
    e = doubled_yz(e, scratch)
    nx, ny, _ = e.shape
    return jnp.broadcast_to(e[:, None], (nx, 2, ny, 128)).reshape(2 * nx, ny, 128)


def coarse_kernel(n_gy, mine, other, e_out, k1, r1, cx, cy, cz, weight, diag, va, vb, sums):
    p, c, b, t = place()
    n_y = 8 * n_gy
    for ref in (k1, cx, va, vb):
        ref[0] = jnp.zeros((n_y, 128), F32)
        ref[33] = jnp.zeros((n_y, 128), F32)
    left = iota((8, 128), 1) < 64
    top = iota((8, 128), 0) < 4
    for gx in range(4):
        for gy in range(n_gy):
            for x in range(4):
                cut = slice(32 + 8 * x, 40 + 8 * x)
                both = [[ref[((gx >> 1) * n_gy + gy) * 2 + gz, cut, :] for ref in (mine, other)] for gz in range(2)]
                near, far = [pick(c ^ (gx & 1), a, o) for a, o in both]
                spot = slice(8 * gy, 8 * gy + 8)
                k1[1 + 8 * gx + x, spot, :] = jnp.where(left, near, roll(far, 64, 1))
                k1[1 + 8 * gx + 4 + x, spot, :] = jnp.where(left, roll(near, 64, 1), far)
    for pp in range(2):
        for gy in range(n_gy):
            for j in range(4):
                cut = slice(8 * j, 8 * j + 8)
                evens, odds = [], []
                for gz in range(2):
                    a = mine[(pp * n_gy + gy) * 2 + gz, cut, :]
                    o = other[(pp * n_gy + gy) * 2 + gz, cut, :]
                    first, second = pick(c, a, o), pick(c, o, a)
                    evens.append(jnp.where(top, first, roll(second, 4, 0)))
                    odds.append(jnp.where(top, roll(first, 4, 0), second))
                spot = slice(8 * gy, 8 * gy + 8)
                for odd, (near, far) in enumerate((evens, odds)):
                    r1[1 + 16 * pp + 2 * j + odd, spot, :] = jnp.where(left, near, roll(far, 64, 1))
                    r1[1 + 16 * pp + 8 + 2 * j + odd, spot, :] = jnp.where(left, roll(near, 64, 1), far)
    faces(k1, cx, cy, cz, weight, diag, 1, 32, 0.25, True, 32)

    va[1:33] = weight[1:33] * r1[1:33]
    sweep(va, vb, r1, cx, cy, cz, weight, 1, 32, 32)
    sums[...] = pair_sums(resid(vb, r1, cx, cy, cz, diag, 1, 32)).reshape(16 * n_y, 128)
    r2 = halved_yz(sums, 16, n_y // 2)

    sums[...] = pair_sums(k1[1:33]).reshape(16 * n_y, 128)
    k2 = halved_yz(sums, 16, n_y // 2)
    middle = Level(k2, 0.0625)
    v2 = middle.weight * r2
    v2 = middle.sweep(v2, r2)
    r3 = halved(middle.resid(v2, r2), sums)
    bottom = Level(halved(k2, sums), 0.015625)
    v3 = bottom.weight * r3
    for _ in range(COARSE_SWEEPS - 1):
        v3 = bottom.sweep(v3, r3)
    v2 = v2 + doubled(v3, sums)
    for _ in range(SMOOTH):
        v2 = middle.sweep(v2, r2)
    e1 = doubled_yz(v2, sums)
    for i in range(16):
        vb[1 + 2 * i] = vb[1 + 2 * i] + e1[i]
        vb[2 + 2 * i] = vb[2 + 2 * i] + e1[i]
    sweep(vb, va, r1, cx, cy, cz, weight, 1, 32, 32)
    sweep(va, vb, r1, cx, cy, cz, weight, 1, 32, 32)
    e_out[...] = vb[...]


def up_kernel(n_gy, e_in, rhs, kappa, weight, v2, out, cx, cy, cz, va, vb, tall):
    p, c, b, t = place()
    first = 5 - 4 * p
    n_y = 8 * n_gy
    for ref in (va, vb, cx):
        ref[0:5] = jnp.zeros((5, 16, 256), F32)
        ref[37:42] = jnp.zeros((5, 16, 256), F32)

    def face(i):
        near = kappa[pl.ds(first + i, PLANES + 1)]
        r, k = pl.ds(first + i, PLANES), near[:PLANES]
        cx[r] = 0.5 * (k + near[1:])
        cy[r] = 0.5 * (k + roll(k, -1, 1))
        cz[r] = 0.5 * (k + roll(k, -1, 2))

    face(0)
    tall[:, 0:8, :] = jnp.zeros((18, 8, 128), F32)
    tall[:, 2 * n_y : 2 * n_y + 8, :] = jnp.zeros((18, 8, 128), F32)
    for k in range(18):
        e = e_in[16 * p + k]
        tall[k, pl.ds(4, n_y, stride=2), :] = e
        tall[k, pl.ds(5, n_y, stride=2), :] = e
    window = tall[:, pl.ds(pl.multiple_of(16 * b + 8 * c, 8), 16), :]
    shape = (128, 256)
    z = iota(shape, 1)
    z = jnp.where(z < 192, z, z - 256)
    spread = jnp.where(64 * t + (z >> 1) == iota(shape, 0), 1.0, 0.0).astype(F32)
    e = dot(window.reshape(288, 128), spread).reshape(18, 16, 256)
    for k in range(18):
        for r in (2 * k + 3, 2 * k + 4):
            va[r] = v2[r] + jnp.where(weight[r] > 0.0, e[k], 0.0)
    sweep(va, vb, rhs, cx, cy, cz, weight, first, PLANES, PLANES)

    def last(i):
        r = pl.ds(5 + i, 32)
        here, total = around(vb, cx, cy, cz, 5 + i, 32)
        done = (1.0 - OMEGA) * here + weight[r] * (rhs[r] + total)
        out[...] = roll(done[:, :, :128], -4, 1)[:, :8]

    last(0)


def call(kernel, name, outs, scratch, *args):
    where = pltpu.HBM if name == "message" else pltpu.VMEM
    if name == "message":
        args = [pltpu.with_memory_space_constraint(a, pltpu.HBM) for a in args]
    return pl.pallas_call(
        kernel,
        name=name,
        out_shape=[jax.ShapeDtypeStruct(s, F32) for s in outs],
        in_specs=[pl.BlockSpec(memory_space=where)] * len(args),
        out_specs=[pl.BlockSpec(memory_space=pltpu.VMEM)] * len(outs),
        scratch_shapes=[
            pltpu.SemaphoreType.DMA((s,)) if isinstance(s, int) else pltpu.VMEM(*s) for s in scratch
        ],
        compiler_params=pltpu.CompilerParams(vmem_limit_bytes=16 * 1024 * 1024),
        cost_estimate=pl.CostEstimate(flops=10**7, bytes_accessed=4 * 10**6, transcendentals=0),
    )(*args)


def paired(chi, inducing, record_dest, record_cell, record_value):
    n_gy = lax.axis_size("gy")
    everyone = ("gx", "gy", "gz")
    window = (ROWS, 16, 256)
    big = [(window, F32)]
    chi, inducing, message, spill = call(
        message_kernel,
        "message",
        [(16, 16, 128), (3, 16, 16, 128), (64, 128), (24, 128)],
        [((8, 128), jnp.int32)] * 2 + [((8, 128), F32), 5],
        chi,
        inducing,
        record_dest.reshape(8, 128),
        record_cell.reshape(8, 128),
        record_value.reshape(8, 128),
    )
    got = lax.ppermute(message, "gz", [(0, 1), (1, 0)])
    spread = [((256, 1024), BF16)] * 4
    source, total, kappa1 = call(
        source_kernel,
        "source",
        [(18, 24, 128), (256, 256), (32, 128)],
        [((128, 128), F32)] + spread,
        chi,
        inducing,
        message,
    )
    own, sent = call(
        deposit_kernel,
        "deposit",
        [(36, 16, 128)] * 2,
        [((36, 24, 128), F32)] + spread,
        source,
        spill,
        chi,
        total,
        got,
    )
    swap = [(0, 1), (1, 0), (2, 3), (3, 2)]
    got = lax.ppermute(sent, "gx", swap)
    held = [(ROWS, 16, 128), (ROWS, 16, 128), (3, 16, 128)]
    *fields, message = call(pair_kernel, "pair", held + [(9, 16, 128)], [], own, got)
    got = lax.ppermute(message, "gx", [(0, 2), (2, 0), (1, 3), (3, 1)])
    *fields, message = call(across_kernel, "across", held + [(PLANES + 3, 8, 128)], [], *fields, got)
    turns = []
    for p in range(2):
        for b in range(n_gy - 1):
            low, high = (2 * p + 1) * n_gy + b, 2 * p * n_gy + b + 1
            turns += [(low, high), (high, low)]
    for low, high in ((0, 2 * n_gy), (2 * n_gy - 1, 4 * n_gy - 1)):
        turns += [(low, high), (high, low)]
    got = lax.ppermute(message, ("gx", "gy"), turns)
    *fine, message = call(
        functools.partial(down_kernel, n_gy),
        "down",
        [window] * 4 + [(4 * n_gy, 64, 128)],
        big * 5 + [((256, 128), F32), ((3, 16, 128), F32)],
        *fields,
        got,
        kappa1,
    )
    n = 2 * n_gy
    groups = [[(2 * p + c) * n + g for p in range(2) for g in range(n)] for c in range(2)]
    mine = lax.all_to_all(
        message, everyone, split_axis=0, concat_axis=0, tiled=True, axis_index_groups=groups
    )
    other = lax.ppermute(mine, "gx", swap)
    level1 = (34, 8 * n_gy, 128)
    (e,) = call(
        functools.partial(coarse_kernel, n_gy),
        "coarse",
        [level1],
        [(level1, F32)] * 9 + [((128 * n_gy, 128), F32)],
        mine,
        other,
    )
    (out,) = call(
        functools.partial(up_kernel, n_gy),
        "up",
        [(32, 8, 128)],
        big * 5 + [((18, 16 * n_gy + 8, 128), F32)],
        e,
        *fine,
    )
    c = lax.axis_index("gx") & 1
    keep = lax.dynamic_slice_in_dim(out, 16 * c, 16, axis=0)
    give = lax.dynamic_slice_in_dim(out, 16 - 16 * c, 16, axis=0)
    got = lax.ppermute(give, "gx", swap)
    return jnp.where(
        c == 0, jnp.concatenate([keep, got], axis=1), jnp.concatenate([got, keep], axis=1)
    )


def solution(mesh):
    placed = (
        P("gx", "gy", "gz"),
        P(None, "gx", "gy", "gz"),
        P("gx", "gy", "gz", None, None),
        P("gx", "gy", "gz", None),
        P("gx", "gy", "gz", None),
    )
    small = mesh.shape["gx"] == 4 and mesh.shape["gz"] == 2 and mesh.shape["gy"] <= 4
    return jax.shard_map(
        paired if small else general,
        mesh=mesh,
        in_specs=placed,
        out_specs=P("gx", "gy", "gz"),
        check_vma=False,
    )
```

```python
import functools

import jax
import jax.numpy as jnp
from jax import lax
from jax.experimental import pallas as pl
from jax.experimental.pallas import tpu as pltpu
from jax.sharding import PartitionSpec as P

SMOOTH = 2
LEVELS = 3
COARSE_SWEEPS = 8
CAP = 640


OMEGA = 0.8


def padded_2(cells, sides, width):
    for axis, dim in sides:
        count = lax.axis_size(axis)
        ends = count - 1
        head = lax.slice_in_dim(cells, 0, width, axis=dim)
        tail = lax.slice_in_dim(cells, cells.shape[dim] - width, cells.shape[dim], axis=dim)
        cells = jnp.concatenate(
            [
                lax.ppermute(tail, axis, [(i, (i + 1) % count) for i in range(ends)]),
                cells,
                lax.ppermute(head, axis, [((i + 1) % count, i) for i in range(ends)]),
            ],
            axis=dim,
        )
    return cells


def restrict(x):
    s = x.shape
    return x.reshape(s[0] // 2, 2, s[1] // 2, 2, s[2] // 2, 2).mean(axis=(1, 3, 5))


def prolong(e):
    return jnp.repeat(jnp.repeat(jnp.repeat(e, 2, 0), 2, 1), 2, 2)


def neighbours(padded):
    return [
        padded[2:, 1:-1, 1:-1],
        padded[:-2, 1:-1, 1:-1],
        padded[1:-1, 2:, 1:-1],
        padded[1:-1, :-2, 1:-1],
        padded[1:-1, 1:-1, 2:],
        padded[1:-1, 1:-1, :-2],
    ]


def face_pad(x):
    return padded_2(x, (("gx", 0), ("gy", 1), ("gz", 2)), 1)


def coefficients(kappa):
    return [0.5 * (kappa + other) for other in neighbours(face_pad(kappa))]


def apply_op(v, coefs, scale):
    total = jnp.zeros_like(v)
    for coef, other in zip(coefs, neighbours(face_pad(v))):
        total = total + coef * (v - other)
    return scale * total


def cycle(level, rhs, kappa):
    scale = 0.25**level
    coefs = coefficients(kappa)
    diag = scale * (coefs[0] + coefs[1] + coefs[2] + coefs[3] + coefs[4] + coefs[5])
    v = OMEGA * rhs / diag
    for sweep in range((COARSE_SWEEPS if level == LEVELS else SMOOTH) - 1):
        v = v + OMEGA * (rhs - apply_op(v, coefs, scale)) / diag
    if level == LEVELS:
        return v
    resid = rhs - apply_op(v, coefs, scale)
    corr = cycle(level + 1, restrict(resid), restrict(kappa))
    v = v + prolong(corr)
    for sweep in range(SMOOTH):
        v = v + OMEGA * (rhs - apply_op(v, coefs, scale)) / diag
    return v


def general(chi, inducing, record_dest, record_cell, record_value):
    n_gz = lax.axis_size("gz")
    dest = record_dest[0, 0, 0, :, 0]
    cells = record_cell[0, 0, 0]
    values = record_value[0, 0, 0]
    onehot = (dest[:, None] == jnp.arange(n_gz, dtype=jnp.int32)[None, :]).astype(jnp.int32)
    ranks = jnp.sum((jnp.cumsum(onehot, axis=0) - 1) * onehot, axis=1)
    outgoing = jnp.zeros((n_gz, 2, CAP), jnp.float32)
    outgoing = outgoing.at[dest, 0, ranks].set(values)
    outgoing = outgoing.at[dest, 1, ranks].set(cells.astype(jnp.float32))
    incoming = lax.all_to_all(outgoing, "gz", split_axis=0, concat_axis=0, tiled=True)
    in_values = incoming[:, 0].reshape(-1)
    in_cells = incoming[:, 1].reshape(-1).astype(jnp.int32)
    moment_x = face_pad(chi * inducing[0])
    moment_y = face_pad(chi * inducing[1])
    moment_z = face_pad(chi * inducing[2])
    source = -0.5 * (
        moment_x[2:, 1:-1, 1:-1]
        - moment_x[:-2, 1:-1, 1:-1]
        + (moment_y[1:-1, 2:, 1:-1] - moment_y[1:-1, :-2, 1:-1])
        + (moment_z[1:-1, 1:-1, 2:] - moment_z[1:-1, 1:-1, :-2])
    )
    rhs = source.reshape(-1).at[in_cells].add(in_values).reshape(source.shape)
    return cycle(0, rhs, 1.0 + chi)


F32 = jnp.float32
BF16 = jnp.bfloat16
ROWS = 42
PLANES = 36
SIZE = 12


def iota(shape, dim):
    return lax.broadcasted_iota(jnp.int32, shape, dim)


def roll(x, shift, axis):
    shift = shift % x.shape[axis]
    return pltpu.roll(x, shift, axis) if shift else x


def pick(flag, first, second):
    return jnp.where(jnp.full(first.shape, flag, jnp.int32) == 0, first, second)


def dot(a, b):
    total = 0.0
    for _ in range(3):
        part = a.astype(BF16)
        total = total + jnp.dot(part, b.astype(BF16), preferred_element_type=F32)
        a = a - part.astype(F32)
    return total


def halving(lanes):
    shape = (lanes, 128)
    return jnp.where((iota(shape, 0) >> 1) == iota(shape, 1), 0.125, 0.0).astype(F32)


def place():
    gx, gy, gz = lax.axis_index("gx"), lax.axis_index("gy"), lax.axis_index("gz")
    return gx >> 1, gx & 1, gy, gz


def stretch(x):
    return roll(jnp.concatenate([x, jnp.zeros((8, x.shape[1]), F32)], 0), 4, 0)


def message_kernel(*refs):
    given, (chi, inducing, message, spill), (dest, cell, value, done) = refs[:5], refs[5:9], refs[9:]
    _, _, _, t = place()
    held = (chi, inducing, dest, cell, value)
    copies = [pltpu.make_async_copy(a, b, done.at[i]) for i, (a, b) in enumerate(zip(given, held))]
    for copy in copies:
        copy.start()
    for copy in copies:
        copy.wait()
    lane = iota((16, 128), 1)
    turn = 11 - 10 * t
    wanted = pick(t, (lane < 11).astype(jnp.int32), ((lane >= 1) & (lane < 12)).astype(jnp.int32)) > 0
    packs = [[jnp.zeros((16, 128), F32)] * 2 for _ in range(4)]
    for x in range(16):
        near = jnp.where(wanted, pltpu.roll(chi[x], turn, 1), 0.0)
        parts = [jnp.where(wanted, 1.0 + near, 0.0)]
        parts += [near * pltpu.roll(inducing[d, x], turn, 1) for d in range(3)]
        for pack, part in zip(packs, parts):
            pack[x // 8] = pack[x // 8] + roll(part, 16 * (x % 8), 1)
    k, mx, my, mz = [jnp.concatenate(pack, 1) for pack in packs]
    lane = iota((16, 256), 1)
    dx = jnp.where(lane < 240, roll(mx, -16, 1), 0.0) - jnp.where(lane >= 16, roll(mx, 16, 1), 0.0)
    y = stretch(my)
    dz = roll(mz, -1, 1) - roll(mz, 1, 1)
    body = -0.5 * (stretch(dx + dz) + (roll(y, -1, 0) - roll(y, 1, 0)))
    lane = iota((24, 128), 1)
    before, after = stretch(mx[:, :128]), stretch(mx[:, 128:])
    ends = 0.5 * (jnp.where((lane >= 16) & (lane < 32), roll(after, 32, 1), 0.0) - jnp.where(lane < 16, before, 0.0))

    def eleven(tile):
        tile = pick(t, roll(tile, -1, 1), tile)
        return jnp.where((iota(tile.shape, 1) & 15) < 11, tile, 0.0)

    slot = iota((24, 256), 1) & 15
    own = pick(t, jnp.where(slot == 11, body, 0.0), jnp.where(slot == 0, body, 0.0))
    own = pick(t, roll(own, -10, 1), roll(own, 9, 1))
    body = eleven(body)
    k = pick(t, k, roll(k, -1, 1))
    for i in range(2):
        cut = slice(128 * i, 128 * (i + 1))
        spill[24 * i : 24 * (i + 1)] = own[:, cut]
        message[24 * i : 24 * (i + 1)] = body[:, cut]
        message[72 + 16 * i : 88 + 16 * i] = k[:, cut]
    message[48:72] = eleven(ends)
    message[104:112] = value[...]
    message[112:120] = (dest[...] * 32768 + cell[...]).astype(F32)


def spread_records(records, t, at_row, hi, mid, lo):
    spot = iota((256, 128), 0)
    for j in range(8):
        value = records[104 + j : 105 + j, :]
        code = records[112 + j : 113 + j, :].astype(jnp.int32)
        cells = code & 32767
        z = ((code >> 15) - t) * 128 + (cells & 127)
        far = z - 128 + 138 * t
        column = jnp.where((far >= 0) & (far < 10), z + 1 + 137 * t, 255)
        column = jnp.where((z >= 0) & (z < 128), z, column)
        cut = slice(128 * j, 128 * (j + 1))
        at_row[:, cut] = jnp.where(spot == (cells >> 7), 1.0, 0.0).astype(BF16)
        here = spot == column
        for part in (hi, mid, lo):
            short = value.astype(BF16).astype(F32)
            part[:, cut] = jnp.where(here, short, 0.0).astype(BF16)
            value = value - short
    total = jnp.zeros((256, 256), F32)
    for part in (lo, mid, hi):
        total = total + lax.dot_general(
            at_row[...], part[...], (((1,), (1,)), ((), ())), preferred_element_type=F32
        )
    return total


def source_kernel(chi, inducing, records, source, total, at_row, hi, mid, lo):
    _, _, _, t = place()
    lane = iota((16, 128), 1)
    zero = jnp.zeros((16, 128), F32)
    mx = [zero, zero] + [chi[x] * inducing[0, x] for x in range(16)] + [zero, zero]
    for i in range(18):
        flat = mx[i + 2] - mx[i]
        if 1 <= i <= 16:
            my, mz = chi[i - 1] * inducing[1, i - 1], chi[i - 1] * inducing[2, i - 1]
            flat = flat + (jnp.where(lane == 127, 0.0, roll(mz, -1, 1)) - jnp.where(lane == 0, 0.0, roll(mz, 1, 1)))
            y = stretch(my)
            source[i] = -0.5 * (stretch(flat) + (roll(y, -1, 0) - roll(y, 1, 0)))
        else:
            source[i] = -0.5 * stretch(flat)
    total[...] = spread_records(records, t, at_row, hi, mid, lo)


def deposit_kernel(source, spill, chi, mine, other, own, sent, all_, at_row, hi, mid, lo):
    _, c, _, t = place()
    total = mine[...] + spread_records(other, t, at_row, hi, mid, lo)
    lane = iota((24, 128), 1)
    halo = [other[24 * i : 24 * (i + 1)] + spill[24 * i : 24 * (i + 1)] for i in range(2)]
    for i in range(18):
        x = i - 1
        if 0 <= x < 16:
            got = stretch(total[16 * x : 16 * x + 16, 128:])
            halo[x // 8] = halo[x // 8] + roll(jnp.where(lane < 16, got, 0.0), 16 * (x % 8), 1)
            add = stretch(total[16 * x : 16 * x + 16, :128])
            tile, by = other[24 * (x // 8) : 24 * (x // 8) + 24], 16 * (x % 8)
        else:
            add = jnp.zeros((24, 128), F32)
            tile, by = other[48:72], 0 if i == 0 else 16
        near = pick(t, roll(tile, 127 - by, 1), roll(tile, -10 - by, 1))
        all_[i] = source[i] + add + jnp.where(lane == 127 - 127 * t, near, 0.0)
    for i in range(16):
        all_[18 + i] = stretch(1.0 + chi[i])
    for i in range(2):
        all_[34 + i] = halo[i]
        all_[37 + i] = stretch(other[72 + 16 * i : 88 + 16 * i])
    all_[36] = other[48:72]
    keep, give = pl.multiple_of(8 * c, 8), pl.multiple_of(8 - 8 * c, 8)
    own[...] = all_[:, pl.ds(keep, 16), :]
    sent[...] = all_[:, pl.ds(give, 16), :]


def pair_kernel(own, other, source, kappa, halo, message):
    p, c, _, _ = place()
    source[...] = jnp.zeros_like(source)
    kappa[...] = jnp.zeros_like(kappa)
    source[pl.ds(4 + 16 * c, 18)] = own[0:18]
    low = 4 + 16 * (1 - c)
    source[pl.ds(low, 18)] = source[pl.ds(low, 18)] + other[0:18]
    kappa[pl.ds(5 + 16 * c, 16)] = own[18:34]
    kappa[pl.ds(low + 1, 16)] = other[18:34]
    lane = iota((16, 128), 1)
    tiles = [jnp.zeros((16, 128), F32)] * 12
    for side in range(2):
        for start, at in ((34, 0), (37, 6)):
            for i in range(2):
                cells = roll(pick(c ^ side, own[start + i], other[start + i]), 80, 1)
                n = at + 2 * side + i
                tiles[n] = tiles[n] + jnp.where(lane >= 80, cells, 0.0)
                tiles[n + 1] = tiles[n + 1] + jnp.where(lane < 80, cells, 0.0)
        ends = roll(pick(c ^ side, own[36], other[36]), 64, 1)
        n = 2 * side
        tiles[n] = tiles[n] + jnp.where((lane >= 64) & (lane < 80), ends, 0.0)
        tiles[n + 2] = tiles[n + 2] + jnp.where((lane >= 80) & (lane < 96), ends, 0.0)
    for i in range(12):
        halo[i] = tiles[i]
    message[0:4] = source[pl.ds(34 - 30 * p, 4)]
    message[4:8] = kappa[pl.ds(33 - 28 * p, 4)]
    for i in range(2):
        low = jnp.where(lane < 64, roll(tiles[6 * i], -64, 1), roll(tiles[6 * i + 1], 64, 1))
        message[8 + i] = jnp.where(lane < 80, pick(p, roll(tiles[6 * i + 4], -16, 1), low), 0.0)


def across_kernel(source_in, kappa_in, halo_in, other, source, kappa, halo, message):
    p, c, _, _ = place()
    source[...] = source_in[...]
    kappa[...] = kappa_in[...]
    at = 36 - 34 * p
    source[pl.ds(at, 4)] = source[pl.ds(at, 4)] + other[0:4]
    kappa[pl.ds(37 - 36 * p, 4)] = other[4:8]
    zero = jnp.zeros((16, 128), F32)
    lane = iota((16, 128), 1)
    halo[...] = halo_in[...]
    for i in range(2):
        got = other[8 + i]
        wide = roll(got, 64, 1)
        halo[6 * i] = halo[6 * i] + pick(p, zero, roll(got, 16, 1))
        halo[6 * i + 4] = halo[6 * i + 4] + pick(p, jnp.where(lane >= 64, wide, 0.0), zero)
        halo[6 * i + 5] = halo[6 * i + 5] + pick(p, jnp.where(lane < 16, wide, 0.0), zero)
    first = 5 - 4 * p

    def cut(s, k):
        s = pick(c, roll(s, -3, 1)[:, :8], roll(s, -9, 1)[:, :8])
        k = pick(c, k[:, :8], roll(k, -4, 1)[:, :8])
        return jnp.where(iota(s.shape, 1) < 4, s, k)

    def body(i):
        message[pl.ds(i, SIZE)] = cut(source[pl.ds(first + i, SIZE)], kappa[pl.ds(first + i, SIZE)])

    chunked(PLANES, body, SIZE)
    message[PLANES:] = cut(halo[0:6], halo[6:12])


def chunked(count, body, size=4):
    def step(i, _):
        body(i * size)
        return 0

    lax.fori_loop(0, count // size, step, 0)


def faces(kap, cx, cy, cz, weight, diag, first, count, scale, closed, n):
    shape = (n,) + kap.shape[1:]
    last_y = iota(shape, 1) == shape[1] - 1
    first_y = iota(shape, 1) == 0
    last_z = iota(shape, 2) == shape[2] - 1
    first_z = iota(shape, 2) == 0

    def body(i):
        r = first + i
        near = kap[pl.ds(r - 1, n + 2)]
        k, up, down = near[1 : n + 1], near[2:], near[:n]
        yu, yd, zu, zd = roll(k, -1, 1), roll(k, 1, 1), roll(k, -1, 2), roll(k, 1, 2)
        if closed:
            yu, yd = jnp.where(last_y, 0.0, yu), jnp.where(first_y, 0.0, yd)
            zu, zd = jnp.where(last_z, 0.0, zu), jnp.where(first_z, 0.0, zd)
        half = 0.5 * scale
        total = half * (6.0 * k + ((up + down) + (yu + yd) + (zu + zd)))
        fy, fz = half * (k + yu), half * (k + zu)
        if closed:
            fy, fz = jnp.where(last_y, 0.0, fy), jnp.where(last_z, 0.0, fz)
        cx[pl.ds(r, n)] = half * (k + up)
        cy[pl.ds(r, n)] = fy
        cz[pl.ds(r, n)] = fz
        diag[pl.ds(r, n)] = total
        weight[pl.ds(r, n)] = jnp.where(k > 0.0, OMEGA / jnp.where(k > 0.0, total, 1.0), 0.0)

    chunked(count, body, n)


def around(v, cx, cy, cz, r, n):
    near, fx = v[pl.ds(r - 1, n + 2)], cx[pl.ds(r - 1, n + 1)]
    here, fy, fz = near[1 : n + 1], cy[pl.ds(r, n)], cz[pl.ds(r, n)]
    return here, (
        (fx[1:] * near[2:] + fx[:n] * near[:n])
        + (fy * roll(here, -1, 1) + roll(fy * here, 1, 1))
        + (fz * roll(here, -1, 2) + roll(fz * here, 1, 2))
    )


def sweep(v, out, rhs, cx, cy, cz, weight, first, count, n):
    def body(i):
        r = first + i
        here, total = around(v, cx, cy, cz, r, n)
        out[pl.ds(r, n)] = (1.0 - OMEGA) * here + weight[pl.ds(r, n)] * (rhs[pl.ds(r, n)] + total)

    chunked(count, body, n)


def resid(v, rhs, cx, cy, cz, diag, r, n):
    here, total = around(v, cx, cy, cz, r, n)
    return rhs[pl.ds(r, n)] + total - diag[pl.ds(r, n)] * here


def pair_sums(x):
    x = x.reshape((x.shape[0] // 2, 2) + x.shape[1:])
    return x[:, 0] + x[:, 1]


def down_kernel(
    n_gy, source_in, kappa_in, halo_in, other, left, kappa, weight, v, along, beside, message,
    rhs, cx, cy, cz, diag, v1, v2, sums, halo,
):
    p, c, b, t = place()
    first = 5 - 4 * p
    edge = jnp.where(c == 0, b == 0, b == n_gy - 1).astype(jnp.int32)
    for ref in (kappa, cx, weight, v1, v2, left):
        ref[0:5] = jnp.zeros((5, 16, 256), F32)
        ref[37:42] = jnp.zeros((5, 16, 256), F32)

    def merge(got):
        n = got.shape[0]
        got = jnp.concatenate([got, jnp.zeros((n, 8, 128), F32)], 1)
        got = pick(edge, got, jnp.zeros_like(got))
        top = iota(got.shape, 1) < 4
        s, k = jnp.where(top, got, 0.0), jnp.where(top, 0.0, got)
        return pick(c, roll(s, 1, 1), roll(s, 11, 1)), pick(c, roll(k, -4, 1), roll(k, 8, 1))

    s, k = merge(other[PLANES:])
    halo[0:6] = halo_in[0:6] + s
    halo[6:12] = halo_in[6:12] + k
    lane = iota((16, 128), 1)
    s_lanes = pick(t, (lane < 10).astype(jnp.int32), (lane >= 118).astype(jnp.int32)) > 0
    k_lanes = pick(t, (lane < 11).astype(jnp.int32), (lane >= 117).astype(jnp.int32)) > 0

    def enter(i):
        r = first + i
        rows = pl.ds(r, SIZE)
        s, k = merge(other[pl.ds(i, SIZE)])
        far_s, far_k = [], []
        for j in range(SIZE):
            tile, by = (r + j) >> 3, 16 * ((r + j) & 7)
            far_s.append(jnp.where(s_lanes, pltpu.roll(halo[tile], (127 - by - 9 * t) & 127, 1), 0.0)[None])
            far_k.append(jnp.where(k_lanes, pltpu.roll(halo[6 + tile], (128 - by - 11 * t) & 127, 1), 0.0)[None])
        rhs[rows] = jnp.concatenate([source_in[rows] + s, jnp.concatenate(far_s, 0)], 2)
        kappa[rows] = jnp.concatenate([kappa_in[rows] + k, jnp.concatenate(far_k, 0)], 2)

    chunked(PLANES, enter, SIZE)
    faces(kappa, cx, cy, cz, weight, diag, first, PLANES, 1.0, False, PLANES)

    def coarse(fine):
        two = pair_sums(fine)
        n = 16 * two.shape[0]
        two = two.reshape(n, 256)
        halves = []
        for i in range(2):
            at = 288 * i
            sums[at : at + n] = two[:, 128 * i : 128 * (i + 1)]
            halves.append(sums[pl.ds(at, n // 2, stride=2), :] + sums[pl.ds(at + 1, n // 2, stride=2), :])
        return dot(jnp.concatenate(halves, 1), halving(256)).reshape(n // 16, 8, 128)

    rows = pl.ds(first, PLANES)
    v1[rows] = weight[rows] * rhs[rows]
    sweep(v1, v2, rhs, cx, cy, cz, weight, first, PLANES, PLANES)
    left[rows] = resid(v2, rhs, cx, cy, cz, diag, first, PLANES)
    v[...] = roll(v2[5:37, :, :128], -4, 1)[:, :8]
    r1 = coarse(left[5:37])
    k1 = coarse(kappa[3:39])
    k = k1[1:17]
    total = (k1[2:] + k1[:16]) + (roll(k, -1, 1) + roll(k, 1, 1)) + (roll(k, -1, 2) + roll(k, 1, 2))
    v1c = jnp.where(k > 0.0, OMEGA / jnp.where(k > 0.0, 0.125 * (6.0 * k + total), 1.0), 0.0) * r1
    tiles = jnp.where(iota(r1.shape, 1) < 4, roll(r1, -2, 1), roll(k, 2, 1))
    along[0:16] = tiles
    beside[0:16] = tiles
    sub = iota((8, 128), 0)
    for i in range(2):
        far, near = jnp.zeros((8, 128), F32), jnp.zeros((8, 128), F32)
        for j in range(8):
            cells = v1c[8 * i + j]
            last, start = roll(cells, j - 5, 0), roll(cells, j - 2, 0)
            far = jnp.where(sub == j, pick(c, last, start), far)
            near = jnp.where(sub == j, pick(c, start, last), near)
        along[16 + i] = far
        beside[16 + i] = near
    message[0:4] = along[pl.ds(12 - 12 * p, 4)]
    message[4] = roll(pick(p, v1c[12], v1c[3]), -2, 0)
    message[5] = roll(pick(p, v1c[15], v1c[0]), -2, 0)


def middle_kernel(n_gy, mine, across, got, other, r1, k1, weight, v2, message, cx, cy, cz, diag, v1, sums, flat):
    p, c, b, t = place()
    edge = jnp.where(c == 0, b == 0, b == n_gy - 1).astype(jnp.int32)
    for ref in (r1, k1, cx, weight, v1, v2):
        ref[...] = jnp.zeros_like(ref)
    sub = iota((8, 128), 0)
    zero = jnp.zeros((8, 128), F32)
    middle = (sub >= 2) & (sub < 6)

    def around_mine(at):
        s, g = other[at], pick(edge, got[at], zero)
        return pick(c, g, s), pick(c, s, g)

    def joined(low, o, high):
        first = jnp.where(middle, roll(low, 2, 0), jnp.where(sub >= 6, roll(o, 6, 0), 0.0))
        return first, jnp.where(sub < 2, roll(o, -2, 0), jnp.where(middle, roll(high, 2, 0), 0.0))

    for j in range(20):
        row = 6 + j if j < 16 else 6 + j - 20 * p
        o = mine[j] if j < 16 else across[j - 16]
        low, high = around_mine(j if j < 16 else j + 2)
        r1[row, 0:8], r1[row, 8:16] = joined(low, o, high)
        k1[row, 0:8], k1[row, 8:16] = joined(*[roll(tile, 4, 0) for tile in (low, o, high)])
    first = 6 - 4 * p
    faces(k1, cx, cy, cz, weight, diag, first, 20, 0.25, False, 20)
    rows = pl.ds(first, 20)
    v1[rows] = weight[rows] * r1[rows]
    ends = []
    for i in range(2):
        low, high = around_mine(16 + i)
        ends += [(6 + 8 * i + j, roll(low, 2 - j, 0), roll(high, 5 - j, 0)) for j in range(8)]
    low, high = around_mine(23)
    ends.append((22 - 17 * p, roll(low, 2, 0), roll(high, 2, 0)))
    for r, low, high in ends:
        v1[r, 0:8] = jnp.where(sub == 2, low, v1[r, 0:8])
        v1[r, 8:16] = jnp.where(sub == 5, high, v1[r, 8:16])
    low, high = around_mine(22)
    r = 25 - 23 * p
    v1[r, 0:8], v1[r, 8:16] = joined(low, across[4], high)
    sweep(v1, v2, r1, cx, cy, cz, weight, first, 20, 20)
    lane = iota((8, 128), 1)
    tile = zero
    for i, fine in enumerate((resid(v2, r1, cx, cy, cz, diag, 6, 16), k1[6:22])):
        sums[...] = pair_sums(fine).reshape(128, 128)
        flat[...] = dot(sums[pl.ds(0, 64, stride=2), :] + sums[pl.ds(1, 64, stride=2), :], halving(128))
        for y in range(2):
            part = jnp.where(lane < 32, flat[pl.ds(3 + y, 8, stride=8), :], 0.0)
            tile = tile + roll(part, 64 * i + 32 * y, 1)
    for d in range(message.shape[0]):
        message[d] = tile


def shift(x, by, axis):
    if axis == 0:
        zero = jnp.zeros((1,) + x.shape[1:], x.dtype)
        return jnp.concatenate([x[1:], zero] if by > 0 else [zero, x[:-1]], 0)
    return roll(x, -by, axis)


SIDES = [(axis, by) for axis in range(3) for by in (1, -1)]


class Level:
    def __init__(self, kappa, scale):
        half = 0.5 * scale
        at = iota(kappa.shape, 1)
        ends = {1: at == kappa.shape[1] - 1, -1: at == 0}
        near = [shift(kappa, by, axis) for axis, by in SIDES]
        near[2:4] = [jnp.where(ends[by], 0.0, k) for by, k in zip((1, -1), near[2:4])]
        self.diag = half * (6.0 * kappa + (near[0] + near[1]) + (near[2] + near[3]) + (near[4] + near[5]))
        self.faces = [half * (kappa + other) for other in near]
        self.faces[2:4] = [jnp.where(ends[by], 0.0, f) for by, f in zip((1, -1), self.faces[2:4])]
        inside = kappa > 0.0
        self.weight = jnp.where(inside, OMEGA / jnp.where(inside, self.diag, 1.0), 0.0)

    def around(self, v):
        terms = [f * shift(v, by, axis) for f, (axis, by) in zip(self.faces, SIDES)]
        return (terms[0] + terms[1]) + (terms[2] + terms[3]) + (terms[4] + terms[5])

    def sweep(self, v, rhs):
        return (1.0 - OMEGA) * v + self.weight * (rhs + self.around(v))

    def resid(self, v, rhs):
        return rhs + self.around(v) - self.diag * v


def halved(x, scratch):
    nx, ny = x.shape[0] // 2, x.shape[1] // 2
    pairs = x.reshape(nx, 2, 2 * ny, 128)
    scratch[0 : 2 * nx * ny, :] = (pairs[:, 0] + pairs[:, 1]).reshape(2 * nx * ny, 128)
    return halved_yz(scratch, nx, ny)


def halved_yz(scratch, nx, ny):
    halves = scratch[pl.ds(0, nx * ny, stride=2), :] + scratch[pl.ds(1, nx * ny, stride=2), :]
    return dot(halves, halving(128)).reshape(nx, ny, 128)


def doubling():
    shape = (128, 128)
    return jnp.where((iota(shape, 1) >> 1) == iota(shape, 0), 1.0, 0.0).astype(F32)


def doubled_yz(e, scratch):
    nx, ny, _ = e.shape
    wide = dot(e.reshape(nx * ny, 128), doubling())
    scratch[pl.ds(0, nx * ny, stride=2), :] = wide
    scratch[pl.ds(1, nx * ny, stride=2), :] = wide
    return scratch[0 : 2 * nx * ny, :].reshape(nx, 2 * ny, 128)


def doubled(e, scratch):
    e = doubled_yz(e, scratch)
    nx, ny, _ = e.shape
    return jnp.broadcast_to(e[:, None], (nx, 2, ny, 128)).reshape(2 * nx, ny, 128)


def up_kernel(
    n_gy, blocks, r1, k1, w1, v21, left, kappa, weight, v2, out,
    r2, k2, tall, flat, sums, fx, fy, fz, ua, ub, cx, cy, cz, va, vb,
):
    p, c, b, t = place()
    first = 5 - 4 * p
    n_y = 4 * n_gy
    for ref in (va, vb, cx):
        ref[0:5] = jnp.zeros((5, 16, 256), F32)
        ref[37:42] = jnp.zeros((5, 16, 256), F32)
    for ref in (fx, ua, ub):
        ref[...] = jnp.zeros_like(ref)

    lane = iota((8, 128), 1)
    for y in range(n_y):
        gy, gc, low = y // 4, y // 2 % 2, y % 2
        for gp in range(2):
            at = ((2 * gp + gc) * n_gy + gy) * 2
            near, far = blocks[at], blocks[at + 1]
            for ref, start in ((r2, 32 * low), (k2, 64 + 32 * low)):
                cells = jnp.where(lane < 64, roll(far, 32 - start, 1), 0.0)
                ref[y, 8 * gp : 8 * gp + 8, :] = jnp.where(lane < 32, roll(near, -start, 1), cells)
    middle, rhs2 = Level(k2[...], 0.0625), r2[...]
    m2 = middle.weight * rhs2
    m2 = middle.sweep(m2, rhs2)
    rhs3 = halved(middle.resid(m2, rhs2), sums)
    bottom = Level(halved(k2[...], sums), 0.015625)
    m3 = bottom.weight * rhs3
    for _ in range(COARSE_SWEEPS - 1):
        m3 = bottom.sweep(m3, rhs3)
    m2 = m2 + doubled(m3, sums)
    for _ in range(SMOOTH):
        m2 = middle.sweep(m2, rhs2)

    shape = (128, 128)
    z = iota(shape, 1)
    z = jnp.where(z < 96, z, z - 128)
    spread = jnp.where(32 * t + (z >> 1) == iota(shape, 0), 1.0, 0.0).astype(F32)
    tall[...] = jnp.zeros_like(tall)
    tall[4 : 4 + n_y, 8:24, :] = dot(m2.reshape(16 * n_y, 128), spread).reshape(n_y, 16, 128)
    for j in range(8):
        cells = tall[4 * b + 2 * c + 1 + j]
        flat[64 * j : 64 * j + 32, :] = cells
        flat[64 * j + 32 : 64 * j + 64, :] = cells
    for i in range(14):
        e = pick(p, flat[pl.ds(5 + i, 16, stride=32), :], flat[pl.ds(13 + i, 16, stride=32), :])
        for r in (2 * i, 2 * i + 1):
            ua[r] = v21[r] + jnp.where(w1[r] > 0.0, e, 0.0)
    at = 6 - 4 * p
    rows = pl.ds(at, 20)
    near = k1[pl.ds(at, 21)]
    k = near[:20]
    fx[rows] = 0.125 * (k + near[1:])
    fy[rows] = 0.125 * (k + roll(k, -1, 1))
    fz[rows] = 0.125 * (k + roll(k, -1, 2))
    sweep(ua, ub, r1, fx, fy, fz, w1, at, 20, 20)
    sweep(ub, ua, r1, fx, fy, fz, w1, at, 20, 20)

    e = roll(ua[5:23], -4, 1)[:, :8].reshape(144, 128)
    flat[pl.ds(0, 144, stride=2), :] = e
    flat[pl.ds(1, 144, stride=2), :] = e
    shape = (128, 256)
    spread = jnp.where((iota(shape, 1) >> 1) == iota(shape, 0), 1.0, 0.0).astype(F32)
    e = dot(flat[0:288, :], spread).reshape(18, 16, 256)
    for k in range(18):
        for r in (2 * k + 3, 2 * k + 4):
            va[r] = jnp.where(weight[r] > 0.0, e[k], 0.0)
    rows = pl.ds(first, PLANES)
    near = kappa[pl.ds(first, PLANES + 1)]
    k = near[:PLANES]
    cx[rows] = 0.5 * (k + near[1:])
    cy[rows] = 0.5 * (k + roll(k, -1, 1))
    cz[rows] = 0.5 * (k + roll(k, -1, 2))
    sweep(va, vb, left, cx, cy, cz, weight, first, PLANES, PLANES)
    here, total = around(vb, cx, cy, cz, 5, 32)
    done = (1.0 - OMEGA) * here + weight[5:37] * (left[5:37] + total)
    out[...] = v2[...] + roll(done[:, :, :128], -4, 1)[:, :8]


def call(kernel, name, outs, scratch, *args):
    where = pltpu.HBM if name == "message" else pltpu.VMEM
    if name == "message":
        args = [pltpu.with_memory_space_constraint(a, pltpu.HBM) for a in args]
    return pl.pallas_call(
        kernel,
        name=name,
        out_shape=[jax.ShapeDtypeStruct(s, F32) for s in outs],
        in_specs=[pl.BlockSpec(memory_space=where)] * len(args),
        out_specs=[pl.BlockSpec(memory_space=pltpu.VMEM)] * len(outs),
        scratch_shapes=[
            pltpu.SemaphoreType.DMA((s,)) if isinstance(s, int) else pltpu.VMEM(*s) for s in scratch
        ],
        compiler_params=pltpu.CompilerParams(vmem_limit_bytes=16 * 1024 * 1024),
        cost_estimate=pl.CostEstimate(flops=10**7, bytes_accessed=4 * 10**6, transcendentals=0),
    )(*args)


def paired(chi, inducing, record_dest, record_cell, record_value):
    n_gy = lax.axis_size("gy")
    everyone = ("gx", "gy", "gz")
    window = (ROWS, 16, 256)
    big = [(window, F32)]
    chi, inducing, message, spill = call(
        message_kernel,
        "message",
        [(16, 16, 128), (3, 16, 16, 128), (120, 128), (48, 128)],
        [((8, 128), jnp.int32)] * 2 + [((8, 128), F32), 5],
        chi,
        inducing,
        record_dest.reshape(8, 128),
        record_cell.reshape(8, 128),
        record_value.reshape(8, 128),
    )
    got = lax.ppermute(message, "gz", [(0, 1), (1, 0)])
    spread = [((256, 1024), BF16)] * 4
    source, total = call(
        source_kernel,
        "source",
        [(18, 24, 128), (256, 256)],
        spread,
        chi,
        inducing,
        message,
    )
    own, sent = call(
        deposit_kernel,
        "deposit",
        [(39, 16, 128)] * 2,
        [((39, 24, 128), F32)] + spread,
        source,
        spill,
        chi,
        total,
        got,
    )
    swap = [(0, 1), (1, 0), (2, 3), (3, 2)]
    got = lax.ppermute(sent, "gx", swap)
    held = [(ROWS, 16, 128), (ROWS, 16, 128), (12, 16, 128)]
    *fields, message = call(pair_kernel, "pair", held + [(10, 16, 128)], [], own, got)
    cross = [(0, 2), (2, 0), (1, 3), (3, 1)]
    got = lax.ppermute(message, "gx", cross)
    *fields, message = call(across_kernel, "across", held + [(PLANES + 6, 8, 128)], [], *fields, got)
    turns = []
    for p in range(2):
        for b in range(n_gy - 1):
            low, high = (2 * p + 1) * n_gy + b, 2 * p * n_gy + b + 1
            turns += [(low, high), (high, low)]
    for low, high in ((0, 2 * n_gy), (2 * n_gy - 1, 4 * n_gy - 1)):
        turns += [(low, high), (high, low)]
    got = lax.ppermute(message, ("gx", "gy"), turns)
    *fine, along, beside, message = call(
        functools.partial(down_kernel, n_gy),
        "down",
        [window] * 3 + [(32, 8, 128), (18, 8, 128), (18, 8, 128), (6, 8, 128)],
        big * 7 + [((576, 128), F32), ((12, 16, 128), F32)],
        *fields,
        got,
    )
    across = lax.ppermute(message, "gx", cross)
    got = lax.ppermute(jnp.concatenate([along, across]), ("gx", "gy"), turns)
    other = lax.ppermute(jnp.concatenate([beside, across]), "gx", swap)
    window1 = (28, 16, 128)
    big1 = [(window1, F32)]
    *coarse, message = call(
        functools.partial(middle_kernel, n_gy),
        "middle",
        [window1] * 4 + [(8 * n_gy, 8, 128)],
        big1 * 5 + [((128, 128), F32), ((64, 128), F32)],
        beside,
        across,
        got,
        other,
    )
    blocks = lax.all_to_all(message, ("gx", "gy", "gz"), split_axis=0, concat_axis=0, tiled=True)
    level2 = ((4 * n_gy, 16, 128), F32)
    (out,) = call(
        functools.partial(up_kernel, n_gy),
        "up",
        [(32, 8, 128)],
        [level2] * 2
        + [((4 * n_gy + 8, 32, 128), F32), ((512, 128), F32), ((64 * n_gy, 128), F32)]
        + big1 * 5
        + big * 5,
        blocks,
        *coarse,
        *fine,
    )
    c = lax.axis_index("gx") & 1
    keep = lax.dynamic_slice_in_dim(out, 16 * c, 16, axis=0)
    give = lax.dynamic_slice_in_dim(out, 16 - 16 * c, 16, axis=0)
    got = lax.ppermute(give, "gx", swap)
    return jnp.where(
        c == 0, jnp.concatenate([keep, got], axis=1), jnp.concatenate([got, keep], axis=1)
    )


def solution(mesh):
    placed = (
        P("gx", "gy", "gz"),
        P(None, "gx", "gy", "gz"),
        P("gx", "gy", "gz", None, None),
        P("gx", "gy", "gz", None),
        P("gx", "gy", "gz", None),
    )
    small = mesh.shape["gx"] == 4 and mesh.shape["gz"] == 2 and mesh.shape["gy"] <= 4
    return jax.shard_map(
        paired if small else general,
        mesh=mesh,
        in_specs=placed,
        out_specs=P("gx", "gy", "gz"),
        check_vma=False,
    )
```

```python
import functools

import jax
import jax.numpy as jnp
from jax import lax
from jax.experimental import pallas as pl
from jax.experimental.pallas import tpu as pltpu
from jax.sharding import PartitionSpec as P

SMOOTH = 2
LEVELS = 3
COARSE_SWEEPS = 8
CAP = 640


OMEGA = 0.8


def padded_2(cells, sides, width):
    for axis, dim in sides:
        count = lax.axis_size(axis)
        ends = count - 1
        head = lax.slice_in_dim(cells, 0, width, axis=dim)
        tail = lax.slice_in_dim(cells, cells.shape[dim] - width, cells.shape[dim], axis=dim)
        cells = jnp.concatenate(
            [
                lax.ppermute(tail, axis, [(i, (i + 1) % count) for i in range(ends)]),
                cells,
                lax.ppermute(head, axis, [((i + 1) % count, i) for i in range(ends)]),
            ],
            axis=dim,
        )
    return cells


def restrict(x):
    s = x.shape
    return x.reshape(s[0] // 2, 2, s[1] // 2, 2, s[2] // 2, 2).mean(axis=(1, 3, 5))


def prolong(e):
    return jnp.repeat(jnp.repeat(jnp.repeat(e, 2, 0), 2, 1), 2, 2)


def neighbours(padded):
    return [
        padded[2:, 1:-1, 1:-1],
        padded[:-2, 1:-1, 1:-1],
        padded[1:-1, 2:, 1:-1],
        padded[1:-1, :-2, 1:-1],
        padded[1:-1, 1:-1, 2:],
        padded[1:-1, 1:-1, :-2],
    ]


def face_pad(x):
    return padded_2(x, (("gx", 0), ("gy", 1), ("gz", 2)), 1)


def coefficients(kappa):
    return [0.5 * (kappa + other) for other in neighbours(face_pad(kappa))]


def apply_op(v, coefs, scale):
    total = jnp.zeros_like(v)
    for coef, other in zip(coefs, neighbours(face_pad(v))):
        total = total + coef * (v - other)
    return scale * total


def cycle(level, rhs, kappa):
    scale = 0.25**level
    coefs = coefficients(kappa)
    diag = scale * (coefs[0] + coefs[1] + coefs[2] + coefs[3] + coefs[4] + coefs[5])
    v = OMEGA * rhs / diag
    for sweep in range((COARSE_SWEEPS if level == LEVELS else SMOOTH) - 1):
        v = v + OMEGA * (rhs - apply_op(v, coefs, scale)) / diag
    if level == LEVELS:
        return v
    resid = rhs - apply_op(v, coefs, scale)
    corr = cycle(level + 1, restrict(resid), restrict(kappa))
    v = v + prolong(corr)
    for sweep in range(SMOOTH):
        v = v + OMEGA * (rhs - apply_op(v, coefs, scale)) / diag
    return v


def general(chi, inducing, record_dest, record_cell, record_value):
    n_gz = lax.axis_size("gz")
    dest = record_dest[0, 0, 0, :, 0]
    cells = record_cell[0, 0, 0]
    values = record_value[0, 0, 0]
    onehot = (dest[:, None] == jnp.arange(n_gz, dtype=jnp.int32)[None, :]).astype(jnp.int32)
    ranks = jnp.sum((jnp.cumsum(onehot, axis=0) - 1) * onehot, axis=1)
    outgoing = jnp.zeros((n_gz, 2, CAP), jnp.float32)
    outgoing = outgoing.at[dest, 0, ranks].set(values)
    outgoing = outgoing.at[dest, 1, ranks].set(cells.astype(jnp.float32))
    incoming = lax.all_to_all(outgoing, "gz", split_axis=0, concat_axis=0, tiled=True)
    in_values = incoming[:, 0].reshape(-1)
    in_cells = incoming[:, 1].reshape(-1).astype(jnp.int32)
    moment_x = face_pad(chi * inducing[0])
    moment_y = face_pad(chi * inducing[1])
    moment_z = face_pad(chi * inducing[2])
    source = -0.5 * (
        moment_x[2:, 1:-1, 1:-1]
        - moment_x[:-2, 1:-1, 1:-1]
        + (moment_y[1:-1, 2:, 1:-1] - moment_y[1:-1, :-2, 1:-1])
        + (moment_z[1:-1, 1:-1, 2:] - moment_z[1:-1, 1:-1, :-2])
    )
    rhs = source.reshape(-1).at[in_cells].add(in_values).reshape(source.shape)
    return cycle(0, rhs, 1.0 + chi)


F32 = jnp.float32
BF16 = jnp.bfloat16
ROWS = 42
PLANES = 36
SIZE = 12


def iota(shape, dim):
    return lax.broadcasted_iota(jnp.int32, shape, dim)


def roll(x, shift, axis):
    shift = shift % x.shape[axis]
    return pltpu.roll(x, shift, axis) if shift else x


def pick(flag, first, second):
    return jnp.where(jnp.full(first.shape, flag, jnp.int32) == 0, first, second)


def dot(a, b):
    total = 0.0
    for _ in range(3):
        part = a.astype(BF16)
        total = total + jnp.dot(part, b.astype(BF16), preferred_element_type=F32)
        a = a - part.astype(F32)
    return total


def halving(lanes):
    shape = (lanes, 128)
    return jnp.where((iota(shape, 0) >> 1) == iota(shape, 1), 0.125, 0.0).astype(F32)


def place():
    gx, gy, gz = lax.axis_index("gx"), lax.axis_index("gy"), lax.axis_index("gz")
    return gx >> 1, gx & 1, gy, gz


def stretch(x):
    return roll(jnp.concatenate([x, jnp.zeros((8, x.shape[1]), F32)], 0), 4, 0)


def message_kernel(*refs):
    given, (chi, inducing, message, spill), (dest, cell, value, done) = refs[:5], refs[5:9], refs[9:]
    _, _, _, t = place()
    held = (chi, inducing, dest, cell, value)
    copies = [pltpu.make_async_copy(a, b, done.at[i]) for i, (a, b) in enumerate(zip(given, held))]
    for copy in copies:
        copy.start()
    for copy in copies:
        copy.wait()
    lane = iota((16, 128), 1)
    turn = 11 - 10 * t
    wanted = pick(t, (lane < 11).astype(jnp.int32), ((lane >= 1) & (lane < 12)).astype(jnp.int32)) > 0
    packs = [[jnp.zeros((16, 128), F32)] * 2 for _ in range(4)]
    for x in range(16):
        near = jnp.where(wanted, pltpu.roll(chi[x], turn, 1), 0.0)
        parts = [jnp.where(wanted, 1.0 + near, 0.0)]
        parts += [near * pltpu.roll(inducing[d, x], turn, 1) for d in range(3)]
        for pack, part in zip(packs, parts):
            pack[x // 8] = pack[x // 8] + roll(part, 16 * (x % 8), 1)
    k, mx, my, mz = [jnp.concatenate(pack, 1) for pack in packs]
    lane = iota((16, 256), 1)
    dx = jnp.where(lane < 240, roll(mx, -16, 1), 0.0) - jnp.where(lane >= 16, roll(mx, 16, 1), 0.0)
    y = stretch(my)
    dz = roll(mz, -1, 1) - roll(mz, 1, 1)
    body = -0.5 * (stretch(dx + dz) + (roll(y, -1, 0) - roll(y, 1, 0)))
    lane = iota((24, 128), 1)
    before, after = stretch(mx[:, :128]), stretch(mx[:, 128:])
    ends = 0.5 * (jnp.where((lane >= 16) & (lane < 32), roll(after, 32, 1), 0.0) - jnp.where(lane < 16, before, 0.0))

    def eleven(tile):
        tile = pick(t, roll(tile, -1, 1), tile)
        return jnp.where((iota(tile.shape, 1) & 15) < 11, tile, 0.0)

    slot = iota((24, 256), 1) & 15
    own = pick(t, jnp.where(slot == 11, body, 0.0), jnp.where(slot == 0, body, 0.0))
    own = pick(t, roll(own, -10, 1), roll(own, 9, 1))
    body = eleven(body)
    k = pick(t, k, roll(k, -1, 1))
    for i in range(2):
        cut = slice(128 * i, 128 * (i + 1))
        spill[24 * i : 24 * (i + 1)] = own[:, cut]
        message[24 * i : 24 * (i + 1)] = body[:, cut]
        message[72 + 16 * i : 88 + 16 * i] = k[:, cut]
    message[48:72] = eleven(ends)
    message[104:112] = value[...]
    message[112:120] = (dest[...] * 32768 + cell[...]).astype(F32)


def spread_records(records, t, at_row, hi, mid, lo):
    spot = iota((256, 128), 0)
    for j in range(8):
        value = records[104 + j : 105 + j, :]
        code = records[112 + j : 113 + j, :].astype(jnp.int32)
        cells = code & 32767
        z = ((code >> 15) - t) * 128 + (cells & 127)
        far = z - 128 + 138 * t
        column = jnp.where((far >= 0) & (far < 10), z + 1 + 137 * t, 255)
        column = jnp.where((z >= 0) & (z < 128), z, column)
        cut = slice(128 * j, 128 * (j + 1))
        at_row[:, cut] = jnp.where(spot == (cells >> 7), 1.0, 0.0).astype(BF16)
        here = spot == column
        for part in (hi, mid, lo):
            short = value.astype(BF16).astype(F32)
            part[:, cut] = jnp.where(here, short, 0.0).astype(BF16)
            value = value - short
    total = jnp.zeros((256, 256), F32)
    for part in (lo, mid, hi):
        total = total + lax.dot_general(
            at_row[...], part[...], (((1,), (1,)), ((), ())), preferred_element_type=F32
        )
    return total


def source_kernel(chi, inducing, records, source, total, at_row, hi, mid, lo):
    _, _, _, t = place()
    lane = iota((16, 128), 1)
    zero = jnp.zeros((16, 128), F32)
    mx = [zero, zero] + [chi[x] * inducing[0, x] for x in range(16)] + [zero, zero]
    for i in range(18):
        flat = mx[i + 2] - mx[i]
        if 1 <= i <= 16:
            my, mz = chi[i - 1] * inducing[1, i - 1], chi[i - 1] * inducing[2, i - 1]
            flat = flat + (jnp.where(lane == 127, 0.0, roll(mz, -1, 1)) - jnp.where(lane == 0, 0.0, roll(mz, 1, 1)))
            y = stretch(my)
            source[i] = -0.5 * (stretch(flat) + (roll(y, -1, 0) - roll(y, 1, 0)))
        else:
            source[i] = -0.5 * stretch(flat)
    total[...] = spread_records(records, t, at_row, hi, mid, lo)


def deposit_kernel(source, spill, chi, mine, other, own, sent, all_, at_row, hi, mid, lo):
    _, c, _, t = place()
    total = mine[...] + spread_records(other, t, at_row, hi, mid, lo)
    lane = iota((24, 128), 1)
    halo = [other[24 * i : 24 * (i + 1)] + spill[24 * i : 24 * (i + 1)] for i in range(2)]
    for i in range(18):
        x = i - 1
        if 0 <= x < 16:
            got = stretch(total[16 * x : 16 * x + 16, 128:])
            halo[x // 8] = halo[x // 8] + roll(jnp.where(lane < 16, got, 0.0), 16 * (x % 8), 1)
            add = stretch(total[16 * x : 16 * x + 16, :128])
            tile, by = other[24 * (x // 8) : 24 * (x // 8) + 24], 16 * (x % 8)
        else:
            add = jnp.zeros((24, 128), F32)
            tile, by = other[48:72], 0 if i == 0 else 16
        near = pick(t, roll(tile, 127 - by, 1), roll(tile, -10 - by, 1))
        all_[i] = source[i] + add + jnp.where(lane == 127 - 127 * t, near, 0.0)
    for i in range(16):
        all_[18 + i] = stretch(1.0 + chi[i])
    for i in range(2):
        all_[34 + i] = halo[i]
        all_[37 + i] = stretch(other[72 + 16 * i : 88 + 16 * i])
    all_[36] = other[48:72]
    keep, give = pl.multiple_of(8 * c, 8), pl.multiple_of(8 - 8 * c, 8)
    own[...] = all_[:, pl.ds(keep, 16), :]
    sent[...] = all_[:, pl.ds(give, 16), :]


def pair_kernel(own, other, source, kappa, halo, message):
    p, c, _, _ = place()
    source[...] = jnp.zeros_like(source)
    kappa[...] = jnp.zeros_like(kappa)
    source[pl.ds(4 + 16 * c, 18)] = own[0:18]
    low = 4 + 16 * (1 - c)
    source[pl.ds(low, 18)] = source[pl.ds(low, 18)] + other[0:18]
    kappa[pl.ds(5 + 16 * c, 16)] = own[18:34]
    kappa[pl.ds(low + 1, 16)] = other[18:34]
    lane = iota((16, 128), 1)
    tiles = [jnp.zeros((16, 128), F32)] * 12
    for side in range(2):
        for start, at in ((34, 0), (37, 6)):
            for i in range(2):
                cells = roll(pick(c ^ side, own[start + i], other[start + i]), 80, 1)
                n = at + 2 * side + i
                tiles[n] = tiles[n] + jnp.where(lane >= 80, cells, 0.0)
                tiles[n + 1] = tiles[n + 1] + jnp.where(lane < 80, cells, 0.0)
        ends = roll(pick(c ^ side, own[36], other[36]), 64, 1)
        n = 2 * side
        tiles[n] = tiles[n] + jnp.where((lane >= 64) & (lane < 80), ends, 0.0)
        tiles[n + 2] = tiles[n + 2] + jnp.where((lane >= 80) & (lane < 96), ends, 0.0)
    for i in range(12):
        halo[i] = tiles[i]
    message[0:4] = source[pl.ds(34 - 30 * p, 4)]
    message[4:8] = kappa[pl.ds(33 - 28 * p, 4)]
    for i in range(2):
        low = jnp.where(lane < 64, roll(tiles[6 * i], -64, 1), roll(tiles[6 * i + 1], 64, 1))
        message[8 + i] = jnp.where(lane < 80, pick(p, roll(tiles[6 * i + 4], -16, 1), low), 0.0)


def across_kernel(source_in, kappa_in, halo_in, other, source, kappa, halo, message):
    p, c, _, _ = place()
    source[...] = source_in[...]
    kappa[...] = kappa_in[...]
    at = 36 - 34 * p
    source[pl.ds(at, 4)] = source[pl.ds(at, 4)] + other[0:4]
    kappa[pl.ds(37 - 36 * p, 4)] = other[4:8]
    zero = jnp.zeros((16, 128), F32)
    lane = iota((16, 128), 1)
    halo[...] = halo_in[...]
    for i in range(2):
        got = other[8 + i]
        wide = roll(got, 64, 1)
        halo[6 * i] = halo[6 * i] + pick(p, zero, roll(got, 16, 1))
        halo[6 * i + 4] = halo[6 * i + 4] + pick(p, jnp.where(lane >= 64, wide, 0.0), zero)
        halo[6 * i + 5] = halo[6 * i + 5] + pick(p, jnp.where(lane < 16, wide, 0.0), zero)
    first = 5 - 4 * p

    def cut(s, k):
        s = pick(c, roll(s, -3, 1)[:, :8], roll(s, -9, 1)[:, :8])
        k = pick(c, k[:, :8], roll(k, -4, 1)[:, :8])
        return jnp.where(iota(s.shape, 1) < 4, s, k)

    def body(i):
        message[pl.ds(i, SIZE)] = cut(source[pl.ds(first + i, SIZE)], kappa[pl.ds(first + i, SIZE)])

    chunked(PLANES, body, SIZE)
    message[PLANES:] = cut(halo[0:6], halo[6:12])


def chunked(count, body, size=4):
    def step(i, _):
        body(i * size)
        return 0

    lax.fori_loop(0, count // size, step, 0)


def faces(kap, cx, cy, cz, weight, diag, first, count, scale, closed, n):
    shape = (n,) + kap.shape[1:]
    last_y = iota(shape, 1) == shape[1] - 1
    first_y = iota(shape, 1) == 0
    last_z = iota(shape, 2) == shape[2] - 1
    first_z = iota(shape, 2) == 0

    def body(i):
        r = first + i
        near = kap[pl.ds(r - 1, n + 2)]
        k, up, down = near[1 : n + 1], near[2:], near[:n]
        yu, yd, zu, zd = roll(k, -1, 1), roll(k, 1, 1), roll(k, -1, 2), roll(k, 1, 2)
        if closed:
            yu, yd = jnp.where(last_y, 0.0, yu), jnp.where(first_y, 0.0, yd)
            zu, zd = jnp.where(last_z, 0.0, zu), jnp.where(first_z, 0.0, zd)
        half = 0.5 * scale
        total = half * (6.0 * k + ((up + down) + (yu + yd) + (zu + zd)))
        fy, fz = half * (k + yu), half * (k + zu)
        if closed:
            fy, fz = jnp.where(last_y, 0.0, fy), jnp.where(last_z, 0.0, fz)
        cx[pl.ds(r, n)] = half * (k + up)
        cy[pl.ds(r, n)] = fy
        cz[pl.ds(r, n)] = fz
        diag[pl.ds(r, n)] = total
        weight[pl.ds(r, n)] = jnp.where(k > 0.0, OMEGA / jnp.where(k > 0.0, total, 1.0), 0.0)

    chunked(count, body, n)


def around(v, cx, cy, cz, r, n):
    near, fx = v[pl.ds(r - 1, n + 2)], cx[pl.ds(r - 1, n + 1)]
    here, fy, fz = near[1 : n + 1], cy[pl.ds(r, n)], cz[pl.ds(r, n)]
    return here, (
        (fx[1:] * near[2:] + fx[:n] * near[:n])
        + (fy * roll(here, -1, 1) + roll(fy * here, 1, 1))
        + (fz * roll(here, -1, 2) + roll(fz * here, 1, 2))
    )


def sweep(v, out, rhs, cx, cy, cz, weight, first, count, n):
    def body(i):
        r = first + i
        here, total = around(v, cx, cy, cz, r, n)
        out[pl.ds(r, n)] = (1.0 - OMEGA) * here + weight[pl.ds(r, n)] * (rhs[pl.ds(r, n)] + total)

    chunked(count, body, n)


def resid(v, rhs, cx, cy, cz, diag, r, n):
    here, total = around(v, cx, cy, cz, r, n)
    return rhs[pl.ds(r, n)] + total - diag[pl.ds(r, n)] * here


def pair_sums(x):
    x = x.reshape((x.shape[0] // 2, 2) + x.shape[1:])
    return x[:, 0] + x[:, 1]


def down_kernel(
    n_gy, source_in, kappa_in, halo_in, other, left, kappa, weight, v, along, beside, message, parts,
    rhs, cx, cy, cz, diag, v1, v2, sums, flat, halo,
):
    p, c, b, t = place()
    first = 5 - 4 * p
    edge = jnp.where(c == 0, b == 0, b == n_gy - 1).astype(jnp.int32)
    for ref in (kappa, cx, weight, v1, v2, left):
        ref[0:5] = jnp.zeros((5, 16, 256), F32)
        ref[37:42] = jnp.zeros((5, 16, 256), F32)

    def merge(got):
        n = got.shape[0]
        got = jnp.concatenate([got, jnp.zeros((n, 8, 128), F32)], 1)
        got = pick(edge, got, jnp.zeros_like(got))
        top = iota(got.shape, 1) < 4
        s, k = jnp.where(top, got, 0.0), jnp.where(top, 0.0, got)
        return pick(c, roll(s, 1, 1), roll(s, 11, 1)), pick(c, roll(k, -4, 1), roll(k, 8, 1))

    s, k = merge(other[PLANES:])
    halo[0:6] = halo_in[0:6] + s
    halo[6:12] = halo_in[6:12] + k
    lane = iota((16, 128), 1)
    s_lanes = pick(t, (lane < 10).astype(jnp.int32), (lane >= 118).astype(jnp.int32)) > 0
    k_lanes = pick(t, (lane < 11).astype(jnp.int32), (lane >= 117).astype(jnp.int32)) > 0

    def enter(i):
        r = first + i
        rows = pl.ds(r, SIZE)
        s, k = merge(other[pl.ds(i, SIZE)])
        far_s, far_k = [], []
        for j in range(SIZE):
            tile, by = (r + j) >> 3, 16 * ((r + j) & 7)
            far_s.append(jnp.where(s_lanes, pltpu.roll(halo[tile], (127 - by - 9 * t) & 127, 1), 0.0)[None])
            far_k.append(jnp.where(k_lanes, pltpu.roll(halo[6 + tile], (128 - by - 11 * t) & 127, 1), 0.0)[None])
        rhs[rows] = jnp.concatenate([source_in[rows] + s, jnp.concatenate(far_s, 0)], 2)
        kappa[rows] = jnp.concatenate([kappa_in[rows] + k, jnp.concatenate(far_k, 0)], 2)

    chunked(PLANES, enter, SIZE)
    faces(kappa, cx, cy, cz, weight, diag, first, PLANES, 1.0, False, PLANES)

    def coarse(fine):
        two = pair_sums(fine)
        n = 16 * two.shape[0]
        two = two.reshape(n, 256)
        halves = []
        for i in range(2):
            at = 320 * i
            sums[at : at + n] = two[:, 128 * i : 128 * (i + 1)]
            halves.append(sums[pl.ds(at, n // 2, stride=2), :] + sums[pl.ds(at + 1, n // 2, stride=2), :])
        return dot(jnp.concatenate(halves, 1), halving(256)).reshape(n // 16, 8, 128)

    rows = pl.ds(first, PLANES)
    v1[rows] = weight[rows] * rhs[rows]
    sweep(v1, v2, rhs, cx, cy, cz, weight, first, PLANES, PLANES)
    left[rows] = resid(v2, rhs, cx, cy, cz, diag, first, PLANES)
    v[...] = roll(v2[5:37, :, :128], -4, 1)[:, :8]
    k1 = coarse(kappa[1:41])
    r1 = coarse(left[5:37])
    edge = jnp.zeros((2, 8, 128), F32)
    at = iota(r1.shape, 1)
    part = jnp.concatenate([edge, jnp.where((at >= 2) & (at < 6), r1, 0.0), edge], 0)
    level = Level(k1, 0.25, closed=False)
    u1 = level.weight * part
    u2 = level.sweep(u1, part)
    sub, lane = iota((8, 128), 0), iota((8, 128), 1)

    def means(fine):
        n = 2 * fine.shape[0]
        sums[0 : 2 * n] = pair_sums(fine).reshape(2 * n, 128)
        return dot(sums[pl.ds(0, n, stride=2), :] + sums[pl.ds(1, n, stride=2), :], halving(128))

    flat[0:40, :] = means(level.resid(u2, part))
    tile = jnp.zeros((8, 128), F32)
    for y in range(4):
        tile = tile + roll(jnp.where(lane < 32, flat[pl.ds(4 + y, 8, stride=4), :], 0.0), 32 * y, 1)
    beyond = jnp.where((sub < 4) & (lane < 32), pick(p, flat[36:44, :], flat[0:8, :]), 0.0)
    second = roll(beyond, 64, 1)
    flat[0:40, :] = means(k1)
    for y in range(2):
        second = second + roll(jnp.where(lane < 32, flat[pl.ds(5 + y, 8, stride=4), :], 0.0), 32 * y, 1)
    for d in range(parts.shape[0]):
        parts[d, 0:8] = tile
        parts[d, 8:16] = second
    k = k1[2:18]
    v1c = level.weight[2:18] * r1
    tiles = jnp.where(iota(r1.shape, 1) < 4, roll(r1, -2, 1), roll(k, 2, 1))
    along[0:16] = tiles
    beside[0:16] = tiles
    for i in range(2):
        far, near = jnp.zeros((8, 128), F32), jnp.zeros((8, 128), F32)
        for j in range(8):
            cells = v1c[8 * i + j]
            last, start = roll(cells, j - 5, 0), roll(cells, j - 2, 0)
            far = jnp.where(sub == j, pick(c, last, start), far)
            near = jnp.where(sub == j, pick(c, start, last), near)
        along[16 + i] = far
        beside[16 + i] = near
    message[0:4] = along[pl.ds(12 - 12 * p, 4)]
    message[4] = roll(pick(p, v1c[12], v1c[3]), -2, 0)
    message[5] = roll(pick(p, v1c[15], v1c[0]), -2, 0)


def middle_kernel(n_gy, mine, across, both, r1, k1, weight, v2, cx, cy, cz, diag, v1):
    p, c, b, t = place()
    edge = jnp.where(c == 0, b == 0, b == n_gy - 1).astype(jnp.int32)
    for ref in (r1, k1, cx, weight, v1, v2):
        ref[...] = jnp.zeros_like(ref)
    sub = iota((8, 128), 0)
    zero = jnp.zeros((8, 128), F32)
    middle = (sub >= 2) & (sub < 6)

    def around_mine(at):
        s, g = both[24 + at], pick(edge, both[at], zero)
        return pick(c, g, s), pick(c, s, g)

    def joined(low, o, high):
        first = jnp.where(middle, roll(low, 2, 0), jnp.where(sub >= 6, roll(o, 6, 0), 0.0))
        return first, jnp.where(sub < 2, roll(o, -2, 0), jnp.where(middle, roll(high, 2, 0), 0.0))

    for j in range(20):
        row = 6 + j if j < 16 else 6 + j - 20 * p
        o = mine[j] if j < 16 else across[j - 16]
        low, high = around_mine(j if j < 16 else j + 2)
        r1[row, 0:8], r1[row, 8:16] = joined(low, o, high)
        k1[row, 0:8], k1[row, 8:16] = joined(*[roll(tile, 4, 0) for tile in (low, o, high)])
    first = 6 - 4 * p
    faces(k1, cx, cy, cz, weight, diag, first, 20, 0.25, False, 20)
    rows = pl.ds(first, 20)
    v1[rows] = weight[rows] * r1[rows]
    ends = []
    for i in range(2):
        low, high = around_mine(16 + i)
        ends += [(6 + 8 * i + j, roll(low, 2 - j, 0), roll(high, 5 - j, 0)) for j in range(8)]
    low, high = around_mine(23)
    ends.append((22 - 17 * p, roll(low, 2, 0), roll(high, 2, 0)))
    for r, low, high in ends:
        v1[r, 0:8] = jnp.where(sub == 2, low, v1[r, 0:8])
        v1[r, 8:16] = jnp.where(sub == 5, high, v1[r, 8:16])
    low, high = around_mine(22)
    r = 25 - 23 * p
    v1[r, 0:8], v1[r, 8:16] = joined(low, across[4], high)
    sweep(v1, v2, r1, cx, cy, cz, weight, first, 20, 20)


def shift(x, by, axis):
    if axis == 0:
        zero = jnp.zeros((1,) + x.shape[1:], x.dtype)
        return jnp.concatenate([x[1:], zero] if by > 0 else [zero, x[:-1]], 0)
    return roll(x, -by, axis)


SIDES = [(axis, by) for axis in range(3) for by in (1, -1)]


class Level:
    def __init__(self, kappa, scale, closed=True):
        half = 0.5 * scale
        at = iota(kappa.shape, 1)
        ends = {1: at == kappa.shape[1] - 1, -1: at == 0}
        near = [shift(kappa, by, axis) for axis, by in SIDES]
        if closed:
            near[2:4] = [jnp.where(ends[by], 0.0, k) for by, k in zip((1, -1), near[2:4])]
        self.diag = half * (6.0 * kappa + (near[0] + near[1]) + (near[2] + near[3]) + (near[4] + near[5]))
        self.faces = [half * (kappa + other) for other in near]
        if closed:
            self.faces[2:4] = [jnp.where(ends[by], 0.0, f) for by, f in zip((1, -1), self.faces[2:4])]
        inside = kappa > 0.0
        self.weight = jnp.where(inside, OMEGA / jnp.where(inside, self.diag, 1.0), 0.0)

    def around(self, v):
        terms = [f * shift(v, by, axis) for f, (axis, by) in zip(self.faces, SIDES)]
        return (terms[0] + terms[1]) + (terms[2] + terms[3]) + (terms[4] + terms[5])

    def sweep(self, v, rhs):
        return (1.0 - OMEGA) * v + self.weight * (rhs + self.around(v))

    def resid(self, v, rhs):
        return rhs + self.around(v) - self.diag * v


def halved(x, scratch):
    nx, ny = x.shape[0] // 2, x.shape[1] // 2
    pairs = x.reshape(nx, 2, 2 * ny, 128)
    scratch[0 : 2 * nx * ny, :] = (pairs[:, 0] + pairs[:, 1]).reshape(2 * nx * ny, 128)
    return halved_yz(scratch, nx, ny)


def halved_yz(scratch, nx, ny):
    halves = scratch[pl.ds(0, nx * ny, stride=2), :] + scratch[pl.ds(1, nx * ny, stride=2), :]
    return dot(halves, halving(128)).reshape(nx, ny, 128)


def doubling():
    shape = (128, 128)
    return jnp.where((iota(shape, 1) >> 1) == iota(shape, 0), 1.0, 0.0).astype(F32)


def doubled_yz(e, scratch):
    nx, ny, _ = e.shape
    wide = dot(e.reshape(nx * ny, 128), doubling())
    scratch[pl.ds(0, nx * ny, stride=2), :] = wide
    scratch[pl.ds(1, nx * ny, stride=2), :] = wide
    return scratch[0 : 2 * nx * ny, :].reshape(nx, 2 * ny, 128)


def doubled(e, scratch):
    e = doubled_yz(e, scratch)
    nx, ny, _ = e.shape
    return jnp.broadcast_to(e[:, None], (nx, 2, ny, 128)).reshape(2 * nx, ny, 128)


def up_kernel(
    n_gy, blocks, r1, k1, w1, v21, left, kappa, weight, v2, out,
    r2, k2, tall, flat, sums, fx, fy, fz, ua, ub, cx, cy, cz, va, vb,
):
    p, c, b, t = place()
    first = 5 - 4 * p
    n_y = 4 * n_gy
    for ref in (va, vb, cx):
        ref[0:5] = jnp.zeros((5, 16, 256), F32)
        ref[37:42] = jnp.zeros((5, 16, 256), F32)
    for ref in (fx, ua, ub):
        ref[...] = jnp.zeros_like(ref)

    lane, sub = iota((8, 128), 1), iota((8, 128), 0)
    cells = {(y, gp): jnp.zeros((8, 128), F32) for y in range(-1, n_y + 1) for gp in range(2)}
    pairs = n_y // 2

    def block(gp, q, gz):
        return ((2 * gp + q % 2) * n_gy + q // 2) * 2 + gz

    for gp in range(2):
        for q in range(pairs):
            whole = []
            for gz in range(2):
                ends = jnp.zeros((8, 128), F32)
                if q + 1 < pairs:
                    ends = jnp.where(lane < 32, blocks[block(gp, q + 1, gz), 0:8, :], ends)
                if q > 0:
                    ends = jnp.where(lane >= 96, blocks[block(gp, q - 1, gz), 0:8, :], ends)
                whole.append(blocks[block(gp, q, gz), 0:8, :] + roll(ends, 64, 1))
            near, far = whole
            near2, far2 = [blocks[block(gp, q, gz), 8:16, :] for gz in range(2)]
            for y in range(2):
                high = jnp.where(lane < 64, roll(far, -32 * y, 1), 0.0)
                own = jnp.where(lane < 32, roll(near, -32 * (y + 1), 1), high)
                cells[2 * q + y, gp] = cells[2 * q + y, gp] + own
                high = jnp.where(lane < 64, roll(far2, 32 * (1 - y), 1), 0.0)
                k2[2 * q + y, 8 * gp : 8 * gp + 8, :] = jnp.where(lane < 32, roll(near2, -32 * y, 1), high)
            high = jnp.where(lane < 64, roll(far2, -32, 1), 0.0)
            beyond = jnp.where(lane < 32, roll(near2, -64, 1), high)
            goal = 0 if gp == 0 else 7
            for y in range(-1, 3):
                spot = 2 * q + y, 1 - gp
                cells[spot] = cells[spot] + jnp.where(sub == goal, roll(beyond, goal - y - 1, 0), 0.0)
    for y in range(n_y):
        for gp in range(2):
            r2[y, 8 * gp : 8 * gp + 8, :] = cells[y, gp]
    middle, rhs2 = Level(k2[...], 0.0625), r2[...]
    m2 = middle.weight * rhs2
    m2 = middle.sweep(m2, rhs2)
    rhs3 = halved(middle.resid(m2, rhs2), sums)
    bottom = Level(halved(k2[...], sums), 0.015625)
    m3 = bottom.weight * rhs3
    for _ in range(COARSE_SWEEPS - 1):
        m3 = bottom.sweep(m3, rhs3)
    m2 = m2 + doubled(m3, sums)
    for _ in range(SMOOTH):
        m2 = middle.sweep(m2, rhs2)

    shape = (128, 128)
    z = iota(shape, 1)
    z = jnp.where(z < 96, z, z - 128)
    spread = jnp.where(32 * t + (z >> 1) == iota(shape, 0), 1.0, 0.0).astype(F32)
    tall[...] = jnp.zeros_like(tall)
    tall[4 : 4 + n_y, 8:24, :] = dot(m2.reshape(16 * n_y, 128), spread).reshape(n_y, 16, 128)
    for j in range(8):
        cells = tall[4 * b + 2 * c + 1 + j]
        flat[64 * j : 64 * j + 32, :] = cells
        flat[64 * j + 32 : 64 * j + 64, :] = cells
    for i in range(14):
        e = pick(p, flat[pl.ds(5 + i, 16, stride=32), :], flat[pl.ds(13 + i, 16, stride=32), :])
        for r in (2 * i, 2 * i + 1):
            ua[r] = v21[r] + jnp.where(w1[r] > 0.0, e, 0.0)
    at = 6 - 4 * p
    rows = pl.ds(at, 20)
    near = k1[pl.ds(at, 21)]
    k = near[:20]
    fx[rows] = 0.125 * (k + near[1:])
    fy[rows] = 0.125 * (k + roll(k, -1, 1))
    fz[rows] = 0.125 * (k + roll(k, -1, 2))
    sweep(ua, ub, r1, fx, fy, fz, w1, at, 20, 20)
    sweep(ub, ua, r1, fx, fy, fz, w1, at, 20, 20)

    e = roll(ua[5:23], -4, 1)[:, :8].reshape(144, 128)
    flat[pl.ds(0, 144, stride=2), :] = e
    flat[pl.ds(1, 144, stride=2), :] = e
    shape = (128, 256)
    spread = jnp.where((iota(shape, 1) >> 1) == iota(shape, 0), 1.0, 0.0).astype(F32)
    e = dot(flat[0:288, :], spread).reshape(18, 16, 256)
    for k in range(18):
        for r in (2 * k + 3, 2 * k + 4):
            va[r] = jnp.where(weight[r] > 0.0, e[k], 0.0)
    rows = pl.ds(first, PLANES)
    near = kappa[pl.ds(first, PLANES + 1)]
    k = near[:PLANES]
    cx[rows] = 0.5 * (k + near[1:])
    cy[rows] = 0.5 * (k + roll(k, -1, 1))
    cz[rows] = 0.5 * (k + roll(k, -1, 2))
    sweep(va, vb, left, cx, cy, cz, weight, first, PLANES, PLANES)
    here, total = around(vb, cx, cy, cz, 5, 32)
    done = (1.0 - OMEGA) * here + weight[5:37] * (left[5:37] + total)
    out[...] = v2[...] + roll(done[:, :, :128], -4, 1)[:, :8]


def call(kernel, name, outs, scratch, *args):
    where = pltpu.HBM if name == "message" else pltpu.VMEM
    if name == "message":
        args = [pltpu.with_memory_space_constraint(a, pltpu.HBM) for a in args]
    return pl.pallas_call(
        kernel,
        name=name,
        out_shape=[jax.ShapeDtypeStruct(s, F32) for s in outs],
        in_specs=[pl.BlockSpec(memory_space=where)] * len(args),
        out_specs=[pl.BlockSpec(memory_space=pltpu.VMEM)] * len(outs),
        scratch_shapes=[
            pltpu.SemaphoreType.DMA((s,)) if isinstance(s, int) else pltpu.VMEM(*s) for s in scratch
        ],
        compiler_params=pltpu.CompilerParams(vmem_limit_bytes=16 * 1024 * 1024),
        cost_estimate=pl.CostEstimate(flops=10**7, bytes_accessed=4 * 10**6, transcendentals=0),
    )(*args)


def paired(chi, inducing, record_dest, record_cell, record_value):
    n_gy = lax.axis_size("gy")
    everyone = ("gx", "gy", "gz")
    window = (ROWS, 16, 256)
    big = [(window, F32)]
    chi, inducing, message, spill = call(
        message_kernel,
        "message",
        [(16, 16, 128), (3, 16, 16, 128), (120, 128), (48, 128)],
        [((8, 128), jnp.int32)] * 2 + [((8, 128), F32), 5],
        chi,
        inducing,
        record_dest.reshape(8, 128),
        record_cell.reshape(8, 128),
        record_value.reshape(8, 128),
    )
    got = lax.ppermute(message, "gz", [(0, 1), (1, 0)])
    spread = [((256, 1024), BF16)] * 4
    source, total = call(
        source_kernel,
        "source",
        [(18, 24, 128), (256, 256)],
        spread,
        chi,
        inducing,
        message,
    )
    own, sent = call(
        deposit_kernel,
        "deposit",
        [(39, 16, 128)] * 2,
        [((39, 24, 128), F32)] + spread,
        source,
        spill,
        chi,
        total,
        got,
    )
    swap = [(0, 1), (1, 0), (2, 3), (3, 2)]
    got = lax.ppermute(sent, "gx", swap)
    held = [(ROWS, 16, 128), (ROWS, 16, 128), (12, 16, 128)]
    *fields, message = call(pair_kernel, "pair", held + [(10, 16, 128)], [], own, got)
    cross = [(0, 2), (2, 0), (1, 3), (3, 1)]
    got = lax.ppermute(message, "gx", cross)
    *fields, message = call(across_kernel, "across", held + [(PLANES + 6, 8, 128)], [], *fields, got)
    turns = []
    for p in range(2):
        for b in range(n_gy - 1):
            low, high = (2 * p + 1) * n_gy + b, 2 * p * n_gy + b + 1
            turns += [(low, high), (high, low)]
    for low, high in ((0, 2 * n_gy), (2 * n_gy - 1, 4 * n_gy - 1)):
        turns += [(low, high), (high, low)]
    got = lax.ppermute(message, ("gx", "gy"), turns)
    *fine, along, beside, message, parts = call(
        functools.partial(down_kernel, n_gy),
        "down",
        [window] * 3 + [(32, 8, 128), (18, 8, 128), (18, 8, 128), (6, 8, 128), (8 * n_gy, 16, 128)],
        big * 7 + [((640, 128), F32), ((48, 128), F32), ((12, 16, 128), F32)],
        *fields,
        got,
    )
    blocks = lax.all_to_all(parts, ("gx", "gy", "gz"), split_axis=0, concat_axis=0, tiled=True)
    across = lax.ppermute(message, "gx", cross)
    got = lax.ppermute(jnp.concatenate([along, across]), ("gx", "gy"), turns)
    other = lax.ppermute(jnp.concatenate([beside, across]), "gx", swap)
    window1 = (28, 16, 128)
    big1 = [(window1, F32)]
    coarse = call(
        functools.partial(middle_kernel, n_gy),
        "middle",
        [window1] * 4,
        big1 * 5,
        beside,
        across,
        jnp.concatenate([got, other]),
    )
    level2 = ((4 * n_gy, 16, 128), F32)
    (out,) = call(
        functools.partial(up_kernel, n_gy),
        "up",
        [(32, 8, 128)],
        [level2] * 2
        + [((4 * n_gy + 8, 32, 128), F32), ((512, 128), F32), ((64 * n_gy, 128), F32)]
        + big1 * 5
        + big * 5,
        blocks,
        *coarse,
        *fine,
    )
    c = lax.axis_index("gx") & 1
    keep = lax.dynamic_slice_in_dim(out, 16 * c, 16, axis=0)
    give = lax.dynamic_slice_in_dim(out, 16 - 16 * c, 16, axis=0)
    got = lax.ppermute(give, "gx", swap)
    return jnp.where(
        c == 0, jnp.concatenate([keep, got], axis=1), jnp.concatenate([got, keep], axis=1)
    )


def solution(mesh):
    placed = (
        P("gx", "gy", "gz"),
        P(None, "gx", "gy", "gz"),
        P("gx", "gy", "gz", None, None),
        P("gx", "gy", "gz", None),
        P("gx", "gy", "gz", None),
    )
    small = mesh.shape["gx"] == 4 and mesh.shape["gz"] == 2 and mesh.shape["gy"] <= 4
    return jax.shard_map(
        paired if small else general,
        mesh=mesh,
        in_specs=placed,
        out_specs=P("gx", "gy", "gz"),
        check_vma=False,
    )
```

```python
import functools

import jax
import jax.numpy as jnp
from jax import lax
from jax.experimental import pallas as pl
from jax.experimental.pallas import tpu as pltpu
from jax.sharding import PartitionSpec as P

SMOOTH = 2
LEVELS = 3
COARSE_SWEEPS = 8
CAP = 640


OMEGA = 0.8


def padded_2(cells, sides, width):
    for axis, dim in sides:
        count = lax.axis_size(axis)
        ends = count - 1
        head = lax.slice_in_dim(cells, 0, width, axis=dim)
        tail = lax.slice_in_dim(cells, cells.shape[dim] - width, cells.shape[dim], axis=dim)
        cells = jnp.concatenate(
            [
                lax.ppermute(tail, axis, [(i, (i + 1) % count) for i in range(ends)]),
                cells,
                lax.ppermute(head, axis, [((i + 1) % count, i) for i in range(ends)]),
            ],
            axis=dim,
        )
    return cells


def restrict(x):
    s = x.shape
    return x.reshape(s[0] // 2, 2, s[1] // 2, 2, s[2] // 2, 2).mean(axis=(1, 3, 5))


def prolong(e):
    return jnp.repeat(jnp.repeat(jnp.repeat(e, 2, 0), 2, 1), 2, 2)


def neighbours(padded):
    return [
        padded[2:, 1:-1, 1:-1],
        padded[:-2, 1:-1, 1:-1],
        padded[1:-1, 2:, 1:-1],
        padded[1:-1, :-2, 1:-1],
        padded[1:-1, 1:-1, 2:],
        padded[1:-1, 1:-1, :-2],
    ]


def face_pad(x):
    return padded_2(x, (("gx", 0), ("gy", 1), ("gz", 2)), 1)


def coefficients(kappa):
    return [0.5 * (kappa + other) for other in neighbours(face_pad(kappa))]


def apply_op(v, coefs, scale):
    total = jnp.zeros_like(v)
    for coef, other in zip(coefs, neighbours(face_pad(v))):
        total = total + coef * (v - other)
    return scale * total


def cycle(level, rhs, kappa):
    scale = 0.25**level
    coefs = coefficients(kappa)
    diag = scale * (coefs[0] + coefs[1] + coefs[2] + coefs[3] + coefs[4] + coefs[5])
    v = OMEGA * rhs / diag
    for sweep in range((COARSE_SWEEPS if level == LEVELS else SMOOTH) - 1):
        v = v + OMEGA * (rhs - apply_op(v, coefs, scale)) / diag
    if level == LEVELS:
        return v
    resid = rhs - apply_op(v, coefs, scale)
    corr = cycle(level + 1, restrict(resid), restrict(kappa))
    v = v + prolong(corr)
    for sweep in range(SMOOTH):
        v = v + OMEGA * (rhs - apply_op(v, coefs, scale)) / diag
    return v


def general(chi, inducing, record_dest, record_cell, record_value):
    n_gz = lax.axis_size("gz")
    dest = record_dest[0, 0, 0, :, 0]
    cells = record_cell[0, 0, 0]
    values = record_value[0, 0, 0]
    onehot = (dest[:, None] == jnp.arange(n_gz, dtype=jnp.int32)[None, :]).astype(jnp.int32)
    ranks = jnp.sum((jnp.cumsum(onehot, axis=0) - 1) * onehot, axis=1)
    outgoing = jnp.zeros((n_gz, 2, CAP), jnp.float32)
    outgoing = outgoing.at[dest, 0, ranks].set(values)
    outgoing = outgoing.at[dest, 1, ranks].set(cells.astype(jnp.float32))
    incoming = lax.all_to_all(outgoing, "gz", split_axis=0, concat_axis=0, tiled=True)
    in_values = incoming[:, 0].reshape(-1)
    in_cells = incoming[:, 1].reshape(-1).astype(jnp.int32)
    moment_x = face_pad(chi * inducing[0])
    moment_y = face_pad(chi * inducing[1])
    moment_z = face_pad(chi * inducing[2])
    source = -0.5 * (
        moment_x[2:, 1:-1, 1:-1]
        - moment_x[:-2, 1:-1, 1:-1]
        + (moment_y[1:-1, 2:, 1:-1] - moment_y[1:-1, :-2, 1:-1])
        + (moment_z[1:-1, 1:-1, 2:] - moment_z[1:-1, 1:-1, :-2])
    )
    rhs = source.reshape(-1).at[in_cells].add(in_values).reshape(source.shape)
    return cycle(0, rhs, 1.0 + chi)


F32 = jnp.float32
BF16 = jnp.bfloat16
ROWS = 42
PLANES = 36
SIZE = 12


def iota(shape, dim):
    return lax.broadcasted_iota(jnp.int32, shape, dim)


def roll(x, shift, axis):
    shift = shift % x.shape[axis]
    return pltpu.roll(x, shift, axis) if shift else x


def pick(flag, first, second):
    return jnp.where(jnp.full(first.shape, flag, jnp.int32) == 0, first, second)


def dot(a, b):
    total = 0.0
    for _ in range(3):
        part = a.astype(BF16)
        total = total + jnp.dot(part, b.astype(BF16), preferred_element_type=F32)
        a = a - part.astype(F32)
    return total


def halving(lanes):
    shape = (lanes, 128)
    return jnp.where((iota(shape, 0) >> 1) == iota(shape, 1), 0.125, 0.0).astype(F32)


def place():
    gx, gy, gz = lax.axis_index("gx"), lax.axis_index("gy"), lax.axis_index("gz")
    return gx >> 1, gx & 1, gy, gz


def stretch(x):
    return roll(jnp.concatenate([x, jnp.zeros((8, x.shape[1]), F32)], 0), 4, 0)


def message_kernel(*refs):
    given, (chi, inducing, message, spill), (dest, cell, value, done) = refs[:5], refs[5:9], refs[9:]
    _, _, _, t = place()
    held = (chi, inducing, dest, cell, value)
    copies = [pltpu.make_async_copy(a, b, done.at[i]) for i, (a, b) in enumerate(zip(given, held))]
    for copy in copies:
        copy.start()
    for copy in copies:
        copy.wait()
    lane = iota((16, 128), 1)
    turn = 11 - 10 * t
    wanted = pick(t, (lane < 11).astype(jnp.int32), ((lane >= 1) & (lane < 12)).astype(jnp.int32)) > 0
    packs = [[jnp.zeros((16, 128), F32)] * 2 for _ in range(4)]
    for x in range(16):
        near = jnp.where(wanted, pltpu.roll(chi[x], turn, 1), 0.0)
        parts = [jnp.where(wanted, 1.0 + near, 0.0)]
        parts += [near * pltpu.roll(inducing[d, x], turn, 1) for d in range(3)]
        for pack, part in zip(packs, parts):
            pack[x // 8] = pack[x // 8] + roll(part, 16 * (x % 8), 1)
    k, mx, my, mz = [jnp.concatenate(pack, 1) for pack in packs]
    lane = iota((16, 256), 1)
    dx = jnp.where(lane < 240, roll(mx, -16, 1), 0.0) - jnp.where(lane >= 16, roll(mx, 16, 1), 0.0)
    y = stretch(my)
    dz = roll(mz, -1, 1) - roll(mz, 1, 1)
    body = -0.5 * (stretch(dx + dz) + (roll(y, -1, 0) - roll(y, 1, 0)))
    lane = iota((24, 128), 1)
    before, after = stretch(mx[:, :128]), stretch(mx[:, 128:])
    ends = 0.5 * (jnp.where((lane >= 16) & (lane < 32), roll(after, 32, 1), 0.0) - jnp.where(lane < 16, before, 0.0))

    def eleven(tile):
        tile = pick(t, roll(tile, -1, 1), tile)
        return jnp.where((iota(tile.shape, 1) & 15) < 11, tile, 0.0)

    slot = iota((24, 256), 1) & 15
    own = pick(t, jnp.where(slot == 11, body, 0.0), jnp.where(slot == 0, body, 0.0))
    own = pick(t, roll(own, -10, 1), roll(own, 9, 1))
    body = eleven(body)
    k = pick(t, k, roll(k, -1, 1))
    for i in range(2):
        cut = slice(128 * i, 128 * (i + 1))
        spill[24 * i : 24 * (i + 1)] = own[:, cut]
        message[24 * i : 24 * (i + 1)] = body[:, cut]
        message[72 + 16 * i : 88 + 16 * i] = k[:, cut]
    message[48:72] = eleven(ends)
    message[104:112] = value[...]
    message[112:120] = (dest[...] * 32768 + cell[...]).astype(F32)


def spread_records(records, t, at_row, hi, mid, lo):
    spot = iota((256, 128), 0)
    for j in range(8):
        value = records[104 + j : 105 + j, :]
        code = records[112 + j : 113 + j, :].astype(jnp.int32)
        cells = code & 32767
        z = ((code >> 15) - t) * 128 + (cells & 127)
        far = z - 128 + 138 * t
        column = jnp.where((far >= 0) & (far < 10), z + 1 + 137 * t, 255)
        column = jnp.where((z >= 0) & (z < 128), z, column)
        cut = slice(128 * j, 128 * (j + 1))
        at_row[:, cut] = jnp.where(spot == (cells >> 7), 1.0, 0.0).astype(BF16)
        here = spot == column
        for part in (hi, mid, lo):
            short = value.astype(BF16).astype(F32)
            part[:, cut] = jnp.where(here, short, 0.0).astype(BF16)
            value = value - short
    total = jnp.zeros((256, 256), F32)
    for part in (lo, mid, hi):
        total = total + lax.dot_general(
            at_row[...], part[...], (((1,), (1,)), ((), ())), preferred_element_type=F32
        )
    return total


def source_kernel(chi, inducing, records, source, total, at_row, hi, mid, lo):
    _, _, _, t = place()
    lane = iota((16, 128), 1)
    zero = jnp.zeros((16, 128), F32)
    mx = [zero, zero] + [chi[x] * inducing[0, x] for x in range(16)] + [zero, zero]
    for i in range(18):
        flat = mx[i + 2] - mx[i]
        if 1 <= i <= 16:
            my, mz = chi[i - 1] * inducing[1, i - 1], chi[i - 1] * inducing[2, i - 1]
            flat = flat + (jnp.where(lane == 127, 0.0, roll(mz, -1, 1)) - jnp.where(lane == 0, 0.0, roll(mz, 1, 1)))
            y = stretch(my)
            source[i] = -0.5 * (stretch(flat) + (roll(y, -1, 0) - roll(y, 1, 0)))
        else:
            source[i] = -0.5 * stretch(flat)
    total[...] = spread_records(records, t, at_row, hi, mid, lo)


def deposit_kernel(source, spill, chi, mine, other, own, sent, all_, at_row, hi, mid, lo):
    _, c, _, t = place()
    total = mine[...] + spread_records(other, t, at_row, hi, mid, lo)
    lane = iota((24, 128), 1)
    halo = [other[24 * i : 24 * (i + 1)] + spill[24 * i : 24 * (i + 1)] for i in range(2)]
    for i in range(18):
        x = i - 1
        if 0 <= x < 16:
            got = stretch(total[16 * x : 16 * x + 16, 128:])
            halo[x // 8] = halo[x // 8] + roll(jnp.where(lane < 16, got, 0.0), 16 * (x % 8), 1)
            add = stretch(total[16 * x : 16 * x + 16, :128])
            tile, by = other[24 * (x // 8) : 24 * (x // 8) + 24], 16 * (x % 8)
        else:
            add = jnp.zeros((24, 128), F32)
            tile, by = other[48:72], 0 if i == 0 else 16
        near = pick(t, roll(tile, 127 - by, 1), roll(tile, -10 - by, 1))
        all_[i] = source[i] + add + jnp.where(lane == 127 - 127 * t, near, 0.0)
    for i in range(16):
        all_[18 + i] = stretch(1.0 + chi[i])
    for i in range(2):
        all_[34 + i] = halo[i]
        all_[37 + i] = stretch(other[72 + 16 * i : 88 + 16 * i])
    all_[36] = other[48:72]
    keep, give = pl.multiple_of(8 * c, 8), pl.multiple_of(8 - 8 * c, 8)
    own[...] = all_[:, pl.ds(keep, 16), :]
    sent[...] = all_[:, pl.ds(give, 16), :]


def pair_kernel(own, other, source, kappa, halo, message, strip, corner):
    p, c, _, _ = place()
    source[...] = jnp.zeros_like(source)
    kappa[...] = jnp.zeros_like(kappa)
    source[pl.ds(4 + 16 * c, 18)] = own[0:18]
    low = 4 + 16 * (1 - c)
    source[pl.ds(low, 18)] = source[pl.ds(low, 18)] + other[0:18]
    kappa[pl.ds(5 + 16 * c, 16)] = own[18:34]
    kappa[pl.ds(low + 1, 16)] = other[18:34]
    lane = iota((16, 128), 1)
    tiles = [jnp.zeros((16, 128), F32)] * 12
    for side in range(2):
        for start, at in ((34, 0), (37, 6)):
            for i in range(2):
                cells = roll(pick(c ^ side, own[start + i], other[start + i]), 80, 1)
                n = at + 2 * side + i
                tiles[n] = tiles[n] + jnp.where(lane >= 80, cells, 0.0)
                tiles[n + 1] = tiles[n + 1] + jnp.where(lane < 80, cells, 0.0)
        ends = roll(pick(c ^ side, own[36], other[36]), 64, 1)
        n = 2 * side
        tiles[n] = tiles[n] + jnp.where((lane >= 64) & (lane < 80), ends, 0.0)
        tiles[n + 2] = tiles[n + 2] + jnp.where((lane >= 80) & (lane < 96), ends, 0.0)
    for i in range(12):
        halo[i] = tiles[i]
    message[0:4] = source[pl.ds(34 - 30 * p, 4)]
    message[4:8] = kappa[pl.ds(33 - 28 * p, 4)]
    for i in range(2):
        low = jnp.where(lane < 64, roll(tiles[6 * i], -64, 1), roll(tiles[6 * i + 1], 64, 1))
        message[8 + i] = jnp.where(lane < 80, pick(p, roll(tiles[6 * i + 4], -16, 1), low), 0.0)

    def cut(s, k):
        s = pick(c, roll(s, -3, 1)[:, :8], roll(s, -9, 1)[:, :8])
        k = pick(c, k[:, :8], roll(k, -4, 1)[:, :8])
        return jnp.where(iota(s.shape, 1) < 4, s, k)

    first = 5 - 4 * p
    strip[0:PLANES] = cut(source[pl.ds(first, PLANES)], kappa[pl.ds(first, PLANES)])
    strip[PLANES:] = cut(halo[0:6], halo[6:12])
    first = 33 - 29 * p
    corner[0:5] = cut(source[pl.ds(first, 5)], kappa[pl.ds(first, 5)])
    corner[5:6] = cut(message[8:9], message[9:10])


def chunked(count, body, size=4):
    def step(i, _):
        body(i * size)
        return 0

    lax.fori_loop(0, count // size, step, 0)


def faces(kap, cx, cy, cz, weight, diag, first, count, scale, closed, n):
    shape = (n,) + kap.shape[1:]
    last_y = iota(shape, 1) == shape[1] - 1
    first_y = iota(shape, 1) == 0
    last_z = iota(shape, 2) == shape[2] - 1
    first_z = iota(shape, 2) == 0

    def body(i):
        r = first + i
        near = kap[pl.ds(r - 1, n + 2)]
        k, up, down = near[1 : n + 1], near[2:], near[:n]
        yu, yd, zu, zd = roll(k, -1, 1), roll(k, 1, 1), roll(k, -1, 2), roll(k, 1, 2)
        if closed:
            yu, yd = jnp.where(last_y, 0.0, yu), jnp.where(first_y, 0.0, yd)
            zu, zd = jnp.where(last_z, 0.0, zu), jnp.where(first_z, 0.0, zd)
        half = 0.5 * scale
        total = half * (6.0 * k + ((up + down) + (yu + yd) + (zu + zd)))
        fy, fz = half * (k + yu), half * (k + zu)
        if closed:
            fy, fz = jnp.where(last_y, 0.0, fy), jnp.where(last_z, 0.0, fz)
        cx[pl.ds(r, n)] = half * (k + up)
        cy[pl.ds(r, n)] = fy
        cz[pl.ds(r, n)] = fz
        diag[pl.ds(r, n)] = total
        weight[pl.ds(r, n)] = jnp.where(k > 0.0, OMEGA / jnp.where(k > 0.0, total, 1.0), 0.0)

    chunked(count, body, n)


def around(v, cx, cy, cz, r, n):
    near, fx = v[pl.ds(r - 1, n + 2)], cx[pl.ds(r - 1, n + 1)]
    here, fy, fz = near[1 : n + 1], cy[pl.ds(r, n)], cz[pl.ds(r, n)]
    return here, (
        (fx[1:] * near[2:] + fx[:n] * near[:n])
        + (fy * roll(here, -1, 1) + roll(fy * here, 1, 1))
        + (fz * roll(here, -1, 2) + roll(fz * here, 1, 2))
    )


def sweep(v, out, rhs, cx, cy, cz, weight, first, count, n):
    def body(i):
        r = first + i
        here, total = around(v, cx, cy, cz, r, n)
        out[pl.ds(r, n)] = (1.0 - OMEGA) * here + weight[pl.ds(r, n)] * (rhs[pl.ds(r, n)] + total)

    chunked(count, body, n)


def resid(v, rhs, cx, cy, cz, diag, r, n):
    here, total = around(v, cx, cy, cz, r, n)
    return rhs[pl.ds(r, n)] + total - diag[pl.ds(r, n)] * here


def pair_sums(x):
    x = x.reshape((x.shape[0] // 2, 2) + x.shape[1:])
    return x[:, 0] + x[:, 1]


def down_kernel(
    n_gy, source_in, kappa_in, halo_in, across, along_in, corner, left, kappa, weight, v, along, beside, message, parts,
    rhs, cx, cy, cz, diag, v1, v2, sums, flat, halo, source, kap, strip,
):
    p, c, b, t = place()
    first = 5 - 4 * p
    edge = jnp.where(c == 0, b == 0, b == n_gy - 1).astype(jnp.int32)
    for ref in (kappa, cx, weight, v1, v2, left):
        ref[0:5] = jnp.zeros((5, 16, 256), F32)
        ref[37:42] = jnp.zeros((5, 16, 256), F32)

    source[...] = source_in[...]
    kap[...] = kappa_in[...]
    strip[...] = along_in[...]
    at = 36 - 34 * p
    source[pl.ds(at, 4)] = source[pl.ds(at, 4)] + across[0:4]
    kap[pl.ds(37 - 36 * p, 4)] = across[4:8]
    at = 31 - 31 * p
    strip[pl.ds(at, 5)] = strip[pl.ds(at, 5)] + corner[0:5]

    def packed(got):
        lane = iota(got.shape, 1)
        wide, zero = roll(got, 64, 1), jnp.zeros_like(got)
        return (
            pick(p, zero, roll(got, 16, 1)),
            pick(p, jnp.where(lane >= 64, wide, 0.0), zero),
            pick(p, jnp.where(lane < 16, wide, 0.0), zero),
        )

    for i, part in zip((0, 4, 5), packed(corner[5])):
        strip[PLANES + i] = strip[PLANES + i] + part

    def merge(got):
        n = got.shape[0]
        got = jnp.concatenate([got, jnp.zeros((n, 8, 128), F32)], 1)
        got = pick(edge, got, jnp.zeros_like(got))
        top = iota(got.shape, 1) < 4
        s, k = jnp.where(top, got, 0.0), jnp.where(top, 0.0, got)
        return pick(c, roll(s, 1, 1), roll(s, 11, 1)), pick(c, roll(k, -4, 1), roll(k, 8, 1))

    s, k = merge(strip[PLANES:])
    halo[0:6] = halo_in[0:6] + s
    halo[6:12] = halo_in[6:12] + k
    for n in range(2):
        for i, part in zip((0, 4, 5), packed(across[8 + n])):
            halo[6 * n + i] = halo[6 * n + i] + part
    lane = iota((16, 128), 1)
    s_lanes = pick(t, (lane < 10).astype(jnp.int32), (lane >= 118).astype(jnp.int32)) > 0
    k_lanes = pick(t, (lane < 11).astype(jnp.int32), (lane >= 117).astype(jnp.int32)) > 0

    def enter(i):
        r = first + i
        rows = pl.ds(r, SIZE)
        s, k = merge(strip[pl.ds(i, SIZE)])
        far_s, far_k = [], []
        for j in range(SIZE):
            tile, by = (r + j) >> 3, 16 * ((r + j) & 7)
            far_s.append(jnp.where(s_lanes, pltpu.roll(halo[tile], (127 - by - 9 * t) & 127, 1), 0.0)[None])
            far_k.append(jnp.where(k_lanes, pltpu.roll(halo[6 + tile], (128 - by - 11 * t) & 127, 1), 0.0)[None])
        rhs[rows] = jnp.concatenate([source[rows] + s, jnp.concatenate(far_s, 0)], 2)
        kappa[rows] = jnp.concatenate([kap[rows] + k, jnp.concatenate(far_k, 0)], 2)

    chunked(PLANES, enter, SIZE)
    faces(kappa, cx, cy, cz, weight, diag, first, PLANES, 1.0, False, PLANES)

    def coarse(fine):
        two = pair_sums(fine)
        n = 16 * two.shape[0]
        two = two.reshape(n, 256)
        halves = []
        for i in range(2):
            at = 320 * i
            sums[at : at + n] = two[:, 128 * i : 128 * (i + 1)]
            halves.append(sums[pl.ds(at, n // 2, stride=2), :] + sums[pl.ds(at + 1, n // 2, stride=2), :])
        return dot(jnp.concatenate(halves, 1), halving(256)).reshape(n // 16, 8, 128)

    rows = pl.ds(first, PLANES)
    v1[rows] = weight[rows] * rhs[rows]
    sweep(v1, v2, rhs, cx, cy, cz, weight, first, PLANES, PLANES)
    left[rows] = resid(v2, rhs, cx, cy, cz, diag, first, PLANES)
    v[...] = roll(v2[5:37, :, :128], -4, 1)[:, :8]
    k1 = coarse(kappa[1:41])
    r1 = coarse(left[5:37])
    edge = jnp.zeros((2, 8, 128), F32)
    at = iota(r1.shape, 1)
    part = jnp.concatenate([edge, jnp.where((at >= 2) & (at < 6), r1, 0.0), edge], 0)
    level = Level(k1, 0.25, closed=False)
    u1 = level.weight * part
    u2 = level.sweep(u1, part)
    sub, lane = iota((8, 128), 0), iota((8, 128), 1)

    def means(fine):
        n = 2 * fine.shape[0]
        sums[0 : 2 * n] = pair_sums(fine).reshape(2 * n, 128)
        return dot(sums[pl.ds(0, n, stride=2), :] + sums[pl.ds(1, n, stride=2), :], halving(128))

    flat[0:40, :] = means(level.resid(u2, part))
    tile = jnp.zeros((8, 128), F32)
    for y in range(4):
        tile = tile + roll(jnp.where(lane < 32, flat[pl.ds(4 + y, 8, stride=4), :], 0.0), 32 * y, 1)
    beyond = jnp.where((sub < 4) & (lane < 32), pick(p, flat[36:44, :], flat[0:8, :]), 0.0)
    second = roll(beyond, 64, 1)
    flat[0:40, :] = means(k1)
    for y in range(2):
        second = second + roll(jnp.where(lane < 32, flat[pl.ds(5 + y, 8, stride=4), :], 0.0), 32 * y, 1)
    for d in range(parts.shape[0]):
        parts[d, 0:8] = tile
        parts[d, 8:16] = second
    k = k1[2:18]
    v1c = level.weight[2:18] * r1
    tiles = jnp.where(iota(r1.shape, 1) < 4, roll(r1, -2, 1), roll(k, 2, 1))
    along[0:16] = tiles
    beside[0:16] = tiles
    for i in range(2):
        far, near = jnp.zeros((8, 128), F32), jnp.zeros((8, 128), F32)
        for j in range(8):
            cells = v1c[8 * i + j]
            last, start = roll(cells, j - 5, 0), roll(cells, j - 2, 0)
            far = jnp.where(sub == j, pick(c, last, start), far)
            near = jnp.where(sub == j, pick(c, start, last), near)
        along[16 + i] = far
        beside[16 + i] = near
    message[0:4] = along[pl.ds(12 - 12 * p, 4)]
    message[4] = roll(pick(p, v1c[12], v1c[3]), -2, 0)
    message[5] = roll(pick(p, v1c[15], v1c[0]), -2, 0)


def middle_kernel(n_gy, mine, across, both, r1, k1, weight, v2, cx, cy, cz, diag, v1):
    p, c, b, t = place()
    edge = jnp.where(c == 0, b == 0, b == n_gy - 1).astype(jnp.int32)
    for ref in (r1, k1, cx, weight, v1, v2):
        ref[...] = jnp.zeros_like(ref)
    sub = iota((8, 128), 0)
    zero = jnp.zeros((8, 128), F32)
    middle = (sub >= 2) & (sub < 6)

    def around_mine(at):
        s, g = both[24 + at], pick(edge, both[at], zero)
        return pick(c, g, s), pick(c, s, g)

    def joined(low, o, high):
        first = jnp.where(middle, roll(low, 2, 0), jnp.where(sub >= 6, roll(o, 6, 0), 0.0))
        return first, jnp.where(sub < 2, roll(o, -2, 0), jnp.where(middle, roll(high, 2, 0), 0.0))

    for j in range(20):
        row = 6 + j if j < 16 else 6 + j - 20 * p
        o = mine[j] if j < 16 else across[j - 16]
        low, high = around_mine(j if j < 16 else j + 2)
        r1[row, 0:8], r1[row, 8:16] = joined(low, o, high)
        k1[row, 0:8], k1[row, 8:16] = joined(*[roll(tile, 4, 0) for tile in (low, o, high)])
    first = 6 - 4 * p
    faces(k1, cx, cy, cz, weight, diag, first, 20, 0.25, False, 20)
    rows = pl.ds(first, 20)
    v1[rows] = weight[rows] * r1[rows]
    ends = []
    for i in range(2):
        low, high = around_mine(16 + i)
        ends += [(6 + 8 * i + j, roll(low, 2 - j, 0), roll(high, 5 - j, 0)) for j in range(8)]
    low, high = around_mine(23)
    ends.append((22 - 17 * p, roll(low, 2, 0), roll(high, 2, 0)))
    for r, low, high in ends:
        v1[r, 0:8] = jnp.where(sub == 2, low, v1[r, 0:8])
        v1[r, 8:16] = jnp.where(sub == 5, high, v1[r, 8:16])
    low, high = around_mine(22)
    r = 25 - 23 * p
    v1[r, 0:8], v1[r, 8:16] = joined(low, across[4], high)
    sweep(v1, v2, r1, cx, cy, cz, weight, first, 20, 20)


def shift(x, by, axis):
    if axis == 0:
        zero = jnp.zeros((1,) + x.shape[1:], x.dtype)
        return jnp.concatenate([x[1:], zero] if by > 0 else [zero, x[:-1]], 0)
    return roll(x, -by, axis)


SIDES = [(axis, by) for axis in range(3) for by in (1, -1)]


class Level:
    def __init__(self, kappa, scale, closed=True):
        half = 0.5 * scale
        at = iota(kappa.shape, 1)
        ends = {1: at == kappa.shape[1] - 1, -1: at == 0}
        near = [shift(kappa, by, axis) for axis, by in SIDES]
        if closed:
            near[2:4] = [jnp.where(ends[by], 0.0, k) for by, k in zip((1, -1), near[2:4])]
        self.diag = half * (6.0 * kappa + (near[0] + near[1]) + (near[2] + near[3]) + (near[4] + near[5]))
        self.faces = [half * (kappa + other) for other in near]
        if closed:
            self.faces[2:4] = [jnp.where(ends[by], 0.0, f) for by, f in zip((1, -1), self.faces[2:4])]
        inside = kappa > 0.0
        self.weight = jnp.where(inside, OMEGA / jnp.where(inside, self.diag, 1.0), 0.0)

    def around(self, v):
        terms = [f * shift(v, by, axis) for f, (axis, by) in zip(self.faces, SIDES)]
        return (terms[0] + terms[1]) + (terms[2] + terms[3]) + (terms[4] + terms[5])

    def sweep(self, v, rhs):
        return (1.0 - OMEGA) * v + self.weight * (rhs + self.around(v))

    def resid(self, v, rhs):
        return rhs + self.around(v) - self.diag * v


def halved(x, scratch):
    nx, ny = x.shape[0] // 2, x.shape[1] // 2
    pairs = x.reshape(nx, 2, 2 * ny, 128)
    scratch[0 : 2 * nx * ny, :] = (pairs[:, 0] + pairs[:, 1]).reshape(2 * nx * ny, 128)
    return halved_yz(scratch, nx, ny)


def halved_yz(scratch, nx, ny):
    halves = scratch[pl.ds(0, nx * ny, stride=2), :] + scratch[pl.ds(1, nx * ny, stride=2), :]
    return dot(halves, halving(128)).reshape(nx, ny, 128)


def doubling():
    shape = (128, 128)
    return jnp.where((iota(shape, 1) >> 1) == iota(shape, 0), 1.0, 0.0).astype(F32)


def doubled_yz(e, scratch):
    nx, ny, _ = e.shape
    wide = dot(e.reshape(nx * ny, 128), doubling())
    scratch[pl.ds(0, nx * ny, stride=2), :] = wide
    scratch[pl.ds(1, nx * ny, stride=2), :] = wide
    return scratch[0 : 2 * nx * ny, :].reshape(nx, 2 * ny, 128)


def doubled(e, scratch):
    e = doubled_yz(e, scratch)
    nx, ny, _ = e.shape
    return jnp.broadcast_to(e[:, None], (nx, 2, ny, 128)).reshape(2 * nx, ny, 128)


def up_kernel(
    n_gy, blocks, r1, k1, w1, v21, left, kappa, weight, v2, out,
    r2, k2, tall, flat, sums, fx, fy, fz, ua, ub, cx, cy, cz, va, vb,
):
    p, c, b, t = place()
    first = 5 - 4 * p
    n_y = 4 * n_gy
    for ref in (va, vb, cx):
        ref[0:5] = jnp.zeros((5, 16, 256), F32)
        ref[37:42] = jnp.zeros((5, 16, 256), F32)
    for ref in (fx, ua, ub):
        ref[...] = jnp.zeros_like(ref)

    lane, sub = iota((8, 128), 1), iota((8, 128), 0)
    cells = {(y, gp): jnp.zeros((8, 128), F32) for y in range(-1, n_y + 1) for gp in range(2)}
    pairs = n_y // 2

    def block(gp, q, gz):
        return ((2 * gp + q % 2) * n_gy + q // 2) * 2 + gz

    for gp in range(2):
        for q in range(pairs):
            whole = []
            for gz in range(2):
                ends = jnp.zeros((8, 128), F32)
                if q + 1 < pairs:
                    ends = jnp.where(lane < 32, blocks[block(gp, q + 1, gz), 0:8, :], ends)
                if q > 0:
                    ends = jnp.where(lane >= 96, blocks[block(gp, q - 1, gz), 0:8, :], ends)
                whole.append(blocks[block(gp, q, gz), 0:8, :] + roll(ends, 64, 1))
            near, far = whole
            near2, far2 = [blocks[block(gp, q, gz), 8:16, :] for gz in range(2)]
            for y in range(2):
                high = jnp.where(lane < 64, roll(far, -32 * y, 1), 0.0)
                own = jnp.where(lane < 32, roll(near, -32 * (y + 1), 1), high)
                cells[2 * q + y, gp] = cells[2 * q + y, gp] + own
                high = jnp.where(lane < 64, roll(far2, 32 * (1 - y), 1), 0.0)
                k2[2 * q + y, 8 * gp : 8 * gp + 8, :] = jnp.where(lane < 32, roll(near2, -32 * y, 1), high)
            high = jnp.where(lane < 64, roll(far2, -32, 1), 0.0)
            beyond = jnp.where(lane < 32, roll(near2, -64, 1), high)
            goal = 0 if gp == 0 else 7
            for y in range(-1, 3):
                spot = 2 * q + y, 1 - gp
                cells[spot] = cells[spot] + jnp.where(sub == goal, roll(beyond, goal - y - 1, 0), 0.0)
    for y in range(n_y):
        for gp in range(2):
            r2[y, 8 * gp : 8 * gp + 8, :] = cells[y, gp]
    middle, rhs2 = Level(k2[...], 0.0625), r2[...]
    m2 = middle.weight * rhs2
    m2 = middle.sweep(m2, rhs2)
    rhs3 = halved(middle.resid(m2, rhs2), sums)
    bottom = Level(halved(k2[...], sums), 0.015625)
    m3 = bottom.weight * rhs3
    for _ in range(COARSE_SWEEPS - 1):
        m3 = bottom.sweep(m3, rhs3)
    m2 = m2 + doubled(m3, sums)
    for _ in range(SMOOTH):
        m2 = middle.sweep(m2, rhs2)

    shape = (128, 128)
    z = iota(shape, 1)
    z = jnp.where(z < 96, z, z - 128)
    spread = jnp.where(32 * t + (z >> 1) == iota(shape, 0), 1.0, 0.0).astype(F32)
    tall[...] = jnp.zeros_like(tall)
    tall[4 : 4 + n_y, 8:24, :] = dot(m2.reshape(16 * n_y, 128), spread).reshape(n_y, 16, 128)
    for j in range(8):
        cells = tall[4 * b + 2 * c + 1 + j]
        flat[64 * j : 64 * j + 32, :] = cells
        flat[64 * j + 32 : 64 * j + 64, :] = cells
    for i in range(14):
        e = pick(p, flat[pl.ds(5 + i, 16, stride=32), :], flat[pl.ds(13 + i, 16, stride=32), :])
        for r in (2 * i, 2 * i + 1):
            ua[r] = v21[r] + jnp.where(w1[r] > 0.0, e, 0.0)
    at = 6 - 4 * p
    rows = pl.ds(at, 20)
    near = k1[pl.ds(at, 21)]
    k = near[:20]
    fx[rows] = 0.125 * (k + near[1:])
    fy[rows] = 0.125 * (k + roll(k, -1, 1))
    fz[rows] = 0.125 * (k + roll(k, -1, 2))
    sweep(ua, ub, r1, fx, fy, fz, w1, at, 20, 20)
    sweep(ub, ua, r1, fx, fy, fz, w1, at, 20, 20)

    e = roll(ua[5:23], -4, 1)[:, :8].reshape(144, 128)
    flat[pl.ds(0, 144, stride=2), :] = e
    flat[pl.ds(1, 144, stride=2), :] = e
    shape = (128, 256)
    spread = jnp.where((iota(shape, 1) >> 1) == iota(shape, 0), 1.0, 0.0).astype(F32)
    e = dot(flat[0:288, :], spread).reshape(18, 16, 256)
    for k in range(18):
        for r in (2 * k + 3, 2 * k + 4):
            va[r] = jnp.where(weight[r] > 0.0, e[k], 0.0)
    rows = pl.ds(first, PLANES)
    near = kappa[pl.ds(first, PLANES + 1)]
    k = near[:PLANES]
    cx[rows] = 0.5 * (k + near[1:])
    cy[rows] = 0.5 * (k + roll(k, -1, 1))
    cz[rows] = 0.5 * (k + roll(k, -1, 2))
    sweep(va, vb, left, cx, cy, cz, weight, first, PLANES, PLANES)
    here, total = around(vb, cx, cy, cz, 5, 32)
    done = (1.0 - OMEGA) * here + weight[5:37] * (left[5:37] + total)
    out[...] = v2[...] + roll(done[:, :, :128], -4, 1)[:, :8]


def call(kernel, name, outs, scratch, *args):
    where = pltpu.HBM if name == "message" else pltpu.VMEM
    if name == "message":
        args = [pltpu.with_memory_space_constraint(a, pltpu.HBM) for a in args]
    return pl.pallas_call(
        kernel,
        name=name,
        out_shape=[jax.ShapeDtypeStruct(s, F32) for s in outs],
        in_specs=[pl.BlockSpec(memory_space=where)] * len(args),
        out_specs=[pl.BlockSpec(memory_space=pltpu.VMEM)] * len(outs),
        scratch_shapes=[
            pltpu.SemaphoreType.DMA((s,)) if isinstance(s, int) else pltpu.VMEM(*s) for s in scratch
        ],
        compiler_params=pltpu.CompilerParams(vmem_limit_bytes=16 * 1024 * 1024),
        cost_estimate=pl.CostEstimate(flops=10**7, bytes_accessed=4 * 10**6, transcendentals=0),
    )(*args)


def paired(chi, inducing, record_dest, record_cell, record_value):
    n_gy = lax.axis_size("gy")
    everyone = ("gx", "gy", "gz")
    window = (ROWS, 16, 256)
    big = [(window, F32)]
    chi, inducing, message, spill = call(
        message_kernel,
        "message",
        [(16, 16, 128), (3, 16, 16, 128), (120, 128), (48, 128)],
        [((8, 128), jnp.int32)] * 2 + [((8, 128), F32), 5],
        chi,
        inducing,
        record_dest.reshape(8, 128),
        record_cell.reshape(8, 128),
        record_value.reshape(8, 128),
    )
    got = lax.ppermute(message, "gz", [(0, 1), (1, 0)])
    spread = [((256, 1024), BF16)] * 4
    source, total = call(
        source_kernel,
        "source",
        [(18, 24, 128), (256, 256)],
        spread,
        chi,
        inducing,
        message,
    )
    own, sent = call(
        deposit_kernel,
        "deposit",
        [(39, 16, 128)] * 2,
        [((39, 24, 128), F32)] + spread,
        source,
        spill,
        chi,
        total,
        got,
    )
    swap = [(0, 1), (1, 0), (2, 3), (3, 2)]
    got = lax.ppermute(sent, "gx", swap)
    held = [(ROWS, 16, 128), (ROWS, 16, 128), (12, 16, 128)]
    *fields, message, strip, corner = call(
        pair_kernel, "pair", held + [(10, 16, 128), (PLANES + 6, 8, 128), (6, 8, 128)], [], own, got
    )
    cross = [(0, 2), (2, 0), (1, 3), (3, 1)]
    across = lax.ppermute(message, "gx", cross)
    turns, corners = [], []
    for p in range(2):
        for b in range(n_gy - 1):
            low, high = (2 * p + 1) * n_gy + b, 2 * p * n_gy + b + 1
            turns += [(low, high), (high, low)]
            high = 2 * (1 - p) * n_gy + b + 1
            corners += [(low, high), (high, low)]
    for low, high in ((0, 2 * n_gy), (2 * n_gy - 1, 4 * n_gy - 1)):
        turns += [(low, high), (high, low)]
        corners += [(low, high), (high, low)]
    strip = lax.ppermute(strip, ("gx", "gy"), turns)
    corner = lax.ppermute(corner, ("gx", "gy"), corners)
    *fine, along, beside, message, parts = call(
        functools.partial(down_kernel, n_gy),
        "down",
        [window] * 3 + [(32, 8, 128), (18, 8, 128), (18, 8, 128), (6, 8, 128), (8 * n_gy, 16, 128)],
        big * 7 + [((640, 128), F32), ((48, 128), F32), ((12, 16, 128), F32)]
        + [((ROWS, 16, 128), F32)] * 2
        + [((PLANES + 6, 8, 128), F32)],
        *fields,
        across,
        strip,
        corner,
    )
    blocks = lax.all_to_all(parts, ("gx", "gy", "gz"), split_axis=0, concat_axis=0, tiled=True)
    across = lax.ppermute(message, "gx", cross)
    got = lax.ppermute(jnp.concatenate([along, across]), ("gx", "gy"), turns)
    other = lax.ppermute(jnp.concatenate([beside, across]), "gx", swap)
    window1 = (28, 16, 128)
    big1 = [(window1, F32)]
    coarse = call(
        functools.partial(middle_kernel, n_gy),
        "middle",
        [window1] * 4,
        big1 * 5,
        beside,
        across,
        jnp.concatenate([got, other]),
    )
    level2 = ((4 * n_gy, 16, 128), F32)
    (out,) = call(
        functools.partial(up_kernel, n_gy),
        "up",
        [(32, 8, 128)],
        [level2] * 2
        + [((4 * n_gy + 8, 32, 128), F32), ((512, 128), F32), ((64 * n_gy, 128), F32)]
        + big1 * 5
        + big * 5,
        blocks,
        *coarse,
        *fine,
    )
    c = lax.axis_index("gx") & 1
    keep = lax.dynamic_slice_in_dim(out, 16 * c, 16, axis=0)
    give = lax.dynamic_slice_in_dim(out, 16 - 16 * c, 16, axis=0)
    got = lax.ppermute(give, "gx", swap)
    return jnp.where(
        c == 0, jnp.concatenate([keep, got], axis=1), jnp.concatenate([got, keep], axis=1)
    )


def solution(mesh):
    placed = (
        P("gx", "gy", "gz"),
        P(None, "gx", "gy", "gz"),
        P("gx", "gy", "gz", None, None),
        P("gx", "gy", "gz", None),
        P("gx", "gy", "gz", None),
    )
    small = mesh.shape["gx"] == 4 and mesh.shape["gz"] == 2 and mesh.shape["gy"] <= 4
    return jax.shard_map(
        paired if small else general,
        mesh=mesh,
        in_specs=placed,
        out_specs=P("gx", "gy", "gz"),
        check_vma=False,
    )
```

```python
import functools

import jax
import jax.numpy as jnp
from jax import lax
from jax.experimental import pallas as pl
from jax.experimental.pallas import tpu as pltpu
from jax.sharding import PartitionSpec as P

SMOOTH = 2
LEVELS = 3
COARSE_SWEEPS = 8
CAP = 640


OMEGA = 0.8


def padded_2(cells, sides, width):
    for axis, dim in sides:
        count = lax.axis_size(axis)
        ends = count - 1
        head = lax.slice_in_dim(cells, 0, width, axis=dim)
        tail = lax.slice_in_dim(cells, cells.shape[dim] - width, cells.shape[dim], axis=dim)
        cells = jnp.concatenate(
            [
                lax.ppermute(tail, axis, [(i, (i + 1) % count) for i in range(ends)]),
                cells,
                lax.ppermute(head, axis, [((i + 1) % count, i) for i in range(ends)]),
            ],
            axis=dim,
        )
    return cells


def restrict(x):
    s = x.shape
    return x.reshape(s[0] // 2, 2, s[1] // 2, 2, s[2] // 2, 2).mean(axis=(1, 3, 5))


def prolong(e):
    return jnp.repeat(jnp.repeat(jnp.repeat(e, 2, 0), 2, 1), 2, 2)


def neighbours(padded):
    return [
        padded[2:, 1:-1, 1:-1],
        padded[:-2, 1:-1, 1:-1],
        padded[1:-1, 2:, 1:-1],
        padded[1:-1, :-2, 1:-1],
        padded[1:-1, 1:-1, 2:],
        padded[1:-1, 1:-1, :-2],
    ]


def face_pad(x):
    return padded_2(x, (("gx", 0), ("gy", 1), ("gz", 2)), 1)


def coefficients(kappa):
    return [0.5 * (kappa + other) for other in neighbours(face_pad(kappa))]


def apply_op(v, coefs, scale):
    total = jnp.zeros_like(v)
    for coef, other in zip(coefs, neighbours(face_pad(v))):
        total = total + coef * (v - other)
    return scale * total


def cycle(level, rhs, kappa):
    scale = 0.25**level
    coefs = coefficients(kappa)
    diag = scale * (coefs[0] + coefs[1] + coefs[2] + coefs[3] + coefs[4] + coefs[5])
    v = OMEGA * rhs / diag
    for sweep in range((COARSE_SWEEPS if level == LEVELS else SMOOTH) - 1):
        v = v + OMEGA * (rhs - apply_op(v, coefs, scale)) / diag
    if level == LEVELS:
        return v
    resid = rhs - apply_op(v, coefs, scale)
    corr = cycle(level + 1, restrict(resid), restrict(kappa))
    v = v + prolong(corr)
    for sweep in range(SMOOTH):
        v = v + OMEGA * (rhs - apply_op(v, coefs, scale)) / diag
    return v


def general(chi, inducing, record_dest, record_cell, record_value):
    n_gz = lax.axis_size("gz")
    dest = record_dest[0, 0, 0, :, 0]
    cells = record_cell[0, 0, 0]
    values = record_value[0, 0, 0]
    onehot = (dest[:, None] == jnp.arange(n_gz, dtype=jnp.int32)[None, :]).astype(jnp.int32)
    ranks = jnp.sum((jnp.cumsum(onehot, axis=0) - 1) * onehot, axis=1)
    outgoing = jnp.zeros((n_gz, 2, CAP), jnp.float32)
    outgoing = outgoing.at[dest, 0, ranks].set(values)
    outgoing = outgoing.at[dest, 1, ranks].set(cells.astype(jnp.float32))
    incoming = lax.all_to_all(outgoing, "gz", split_axis=0, concat_axis=0, tiled=True)
    in_values = incoming[:, 0].reshape(-1)
    in_cells = incoming[:, 1].reshape(-1).astype(jnp.int32)
    moment_x = face_pad(chi * inducing[0])
    moment_y = face_pad(chi * inducing[1])
    moment_z = face_pad(chi * inducing[2])
    source = -0.5 * (
        moment_x[2:, 1:-1, 1:-1]
        - moment_x[:-2, 1:-1, 1:-1]
        + (moment_y[1:-1, 2:, 1:-1] - moment_y[1:-1, :-2, 1:-1])
        + (moment_z[1:-1, 1:-1, 2:] - moment_z[1:-1, 1:-1, :-2])
    )
    rhs = source.reshape(-1).at[in_cells].add(in_values).reshape(source.shape)
    return cycle(0, rhs, 1.0 + chi)


F32 = jnp.float32
BF16 = jnp.bfloat16
ROWS = 42
PLANES = 36
SIZE = 12


def iota(shape, dim):
    return lax.broadcasted_iota(jnp.int32, shape, dim)


def roll(x, shift, axis):
    shift = shift % x.shape[axis]
    return pltpu.roll(x, shift, axis) if shift else x


def pick(flag, first, second):
    return jnp.where(jnp.full(first.shape, flag, jnp.int32) == 0, first, second)


def dot(a, b):
    total = 0.0
    for _ in range(3):
        part = a.astype(BF16)
        total = total + jnp.dot(part, b.astype(BF16), preferred_element_type=F32)
        a = a - part.astype(F32)
    return total


def halving(lanes):
    shape = (lanes, 128)
    return jnp.where((iota(shape, 0) >> 1) == iota(shape, 1), 0.125, 0.0).astype(F32)


def place():
    gx, gy, gz = lax.axis_index("gx"), lax.axis_index("gy"), lax.axis_index("gz")
    return gx >> 1, gx & 1, gy, gz


def stretch(x):
    return roll(jnp.concatenate([x, jnp.zeros((8, x.shape[1]), F32)], 0), 4, 0)


def message_kernel(*refs):
    given, (chi, inducing, message, spill), (dest, cell, value, done) = refs[:5], refs[5:9], refs[9:]
    _, _, _, t = place()
    held = (chi, inducing, dest, cell, value)
    pairs = [(a.at[4 * i : 4 * i + 4], b.at[4 * i : 4 * i + 4]) for i in range(4) for a, b in [(given[0], held[0])]]
    pairs += [(given[1].at[:, 4 * i : 4 * i + 4], held[1].at[:, 4 * i : 4 * i + 4]) for i in range(4)]
    pairs += list(zip(given[2:], held[2:]))
    copies = [pltpu.make_async_copy(a, b, done.at[i]) for i, (a, b) in enumerate(pairs)]
    for i in (0, 4, 1, 5, 2, 6, 3, 7, 8, 9, 10):
        copies[i].start()
    lane = iota((16, 128), 1)
    turn = 11 - 10 * t
    wanted = pick(t, (lane < 11).astype(jnp.int32), ((lane >= 1) & (lane < 12)).astype(jnp.int32)) > 0
    packs = [[jnp.zeros((16, 128), F32)] * 2 for _ in range(4)]
    for x in range(16):
        if x % 4 == 0:
            copies[x // 4].wait()
            copies[4 + x // 4].wait()
        near = jnp.where(wanted, pltpu.roll(chi[x], turn, 1), 0.0)
        parts = [jnp.where(wanted, 1.0 + near, 0.0)]
        parts += [near * pltpu.roll(inducing[d, x], turn, 1) for d in range(3)]
        for pack, part in zip(packs, parts):
            pack[x // 8] = pack[x // 8] + roll(part, 16 * (x % 8), 1)
    k, mx, my, mz = [jnp.concatenate(pack, 1) for pack in packs]
    lane = iota((16, 256), 1)
    dx = jnp.where(lane < 240, roll(mx, -16, 1), 0.0) - jnp.where(lane >= 16, roll(mx, 16, 1), 0.0)
    y = stretch(my)
    dz = roll(mz, -1, 1) - roll(mz, 1, 1)
    body = -0.5 * (stretch(dx + dz) + (roll(y, -1, 0) - roll(y, 1, 0)))
    lane = iota((24, 128), 1)
    before, after = stretch(mx[:, :128]), stretch(mx[:, 128:])
    ends = 0.5 * (jnp.where((lane >= 16) & (lane < 32), roll(after, 32, 1), 0.0) - jnp.where(lane < 16, before, 0.0))

    def eleven(tile):
        tile = pick(t, roll(tile, -1, 1), tile)
        return jnp.where((iota(tile.shape, 1) & 15) < 11, tile, 0.0)

    slot = iota((24, 256), 1) & 15
    own = pick(t, jnp.where(slot == 11, body, 0.0), jnp.where(slot == 0, body, 0.0))
    own = pick(t, roll(own, -10, 1), roll(own, 9, 1))
    body = eleven(body)
    k = pick(t, k, roll(k, -1, 1))
    for i in range(2):
        cut = slice(128 * i, 128 * (i + 1))
        spill[24 * i : 24 * (i + 1)] = own[:, cut]
        message[24 * i : 24 * (i + 1)] = body[:, cut]
        message[72 + 16 * i : 88 + 16 * i] = k[:, cut]
    message[48:72] = eleven(ends)
    for copy in copies[8:]:
        copy.wait()
    message[104:112] = value[...]
    message[112:120] = (dest[...] * 32768 + cell[...]).astype(F32)


def spread_records(records, t, at_row, at_column):
    row, slot = iota((256, 128), 0), iota((16, 128), 0)
    z_of = iota((128, 128), 0)
    at_column[432:512] = jnp.zeros((80, 1024), BF16)
    for j in range(8):
        value = records[104 + j : 105 + j, :]
        code = records[112 + j : 113 + j, :].astype(jnp.int32)
        cells = code & 32767
        z = ((code >> 15) - t) * 128 + (cells & 127)
        far = z - 128 + 138 * t
        far = jnp.where((far >= 0) & (far < 10), far + 1 - t, 16)
        cut = slice(128 * j, 128 * (j + 1))
        at_row[:, cut] = jnp.where(row == (cells >> 7), 1.0, 0.0).astype(BF16)
        here, there = z_of == z, slot == far
        for i in range(3):
            short = value.astype(BF16).astype(F32)
            at_column[128 * i : 128 * (i + 1), cut] = jnp.where(here, short, 0.0).astype(BF16)
            at_column[384 + 16 * i : 400 + 16 * i, cut] = jnp.where(there, short, 0.0).astype(BF16)
            value = value - short
    total = lax.dot_general(
        at_row[...], at_column[...], (((1,), (1,)), ((), ())), preferred_element_type=F32
    )
    near = (total[:, 256:384] + total[:, 128:256]) + total[:, 0:128]
    return jnp.concatenate([near, total[:, 384:512]], 1)


def source_kernel(chi, inducing, records, source, total, at_row, at_column):
    _, _, _, t = place()
    lane = iota((16, 128), 1)
    zero = jnp.zeros((16, 128), F32)
    mx = [zero, zero] + [chi[x] * inducing[0, x] for x in range(16)] + [zero, zero]
    for i in range(18):
        flat = mx[i + 2] - mx[i]
        if 1 <= i <= 16:
            my, mz = chi[i - 1] * inducing[1, i - 1], chi[i - 1] * inducing[2, i - 1]
            flat = flat + (jnp.where(lane == 127, 0.0, roll(mz, -1, 1)) - jnp.where(lane == 0, 0.0, roll(mz, 1, 1)))
            y = stretch(my)
            source[i] = -0.5 * (stretch(flat) + (roll(y, -1, 0) - roll(y, 1, 0)))
        else:
            source[i] = -0.5 * stretch(flat)
    total[...] = spread_records(records, t, at_row, at_column)


def deposit_kernel(source, spill, chi, mine, other, own, sent, all_, at_row, at_column):
    _, c, _, t = place()
    total = mine[...] + spread_records(other, t, at_row, at_column)
    lane = iota((24, 128), 1)
    halo = [other[24 * i : 24 * (i + 1)] + spill[24 * i : 24 * (i + 1)] for i in range(2)]
    for i in range(18):
        x = i - 1
        if 0 <= x < 16:
            got = total[16 * x : 16 * x + 16, 128:]
            got = stretch((roll(got, -32, 1) + roll(got, -16, 1)) + got)
            halo[x // 8] = halo[x // 8] + roll(jnp.where(lane < 16, got, 0.0), 16 * (x % 8), 1)
            add = stretch(total[16 * x : 16 * x + 16, :128])
            tile, by = other[24 * (x // 8) : 24 * (x // 8) + 24], 16 * (x % 8)
        else:
            add = jnp.zeros((24, 128), F32)
            tile, by = other[48:72], 0 if i == 0 else 16
        near = pick(t, roll(tile, 127 - by, 1), roll(tile, -10 - by, 1))
        all_[i] = source[i] + add + jnp.where(lane == 127 - 127 * t, near, 0.0)
    for i in range(16):
        all_[18 + i] = stretch(1.0 + chi[i])
    for i in range(2):
        all_[34 + i] = halo[i]
        all_[37 + i] = stretch(other[72 + 16 * i : 88 + 16 * i])
    all_[36] = other[48:72]
    keep, give = pl.multiple_of(8 * c, 8), pl.multiple_of(8 - 8 * c, 8)
    own[...] = all_[:, pl.ds(keep, 16), :]
    sent[...] = all_[:, pl.ds(give, 16), :]


def pair_kernel(own, other, source, kappa, halo, message, strip, corner):
    p, c, _, _ = place()
    source[...] = jnp.zeros_like(source)
    kappa[...] = jnp.zeros_like(kappa)
    source[pl.ds(4 + 16 * c, 18)] = own[0:18]
    low = 4 + 16 * (1 - c)
    source[pl.ds(low, 18)] = source[pl.ds(low, 18)] + other[0:18]
    kappa[pl.ds(5 + 16 * c, 16)] = own[18:34]
    kappa[pl.ds(low + 1, 16)] = other[18:34]
    lane = iota((16, 128), 1)
    tiles = [jnp.zeros((16, 128), F32)] * 12
    for side in range(2):
        for start, at in ((34, 0), (37, 6)):
            for i in range(2):
                cells = roll(pick(c ^ side, own[start + i], other[start + i]), 80, 1)
                n = at + 2 * side + i
                tiles[n] = tiles[n] + jnp.where(lane >= 80, cells, 0.0)
                tiles[n + 1] = tiles[n + 1] + jnp.where(lane < 80, cells, 0.0)
        ends = roll(pick(c ^ side, own[36], other[36]), 64, 1)
        n = 2 * side
        tiles[n] = tiles[n] + jnp.where((lane >= 64) & (lane < 80), ends, 0.0)
        tiles[n + 2] = tiles[n + 2] + jnp.where((lane >= 80) & (lane < 96), ends, 0.0)
    for i in range(12):
        halo[i] = tiles[i]
    message[0:4] = source[pl.ds(34 - 30 * p, 4)]
    message[4:8] = kappa[pl.ds(33 - 28 * p, 4)]
    for i in range(2):
        low = jnp.where(lane < 64, roll(tiles[6 * i], -64, 1), roll(tiles[6 * i + 1], 64, 1))
        message[8 + i] = jnp.where(lane < 80, pick(p, roll(tiles[6 * i + 4], -16, 1), low), 0.0)

    def cut(s, k):
        s = pick(c, roll(s, -3, 1)[:, :8], roll(s, -9, 1)[:, :8])
        k = pick(c, k[:, :8], roll(k, -4, 1)[:, :8])
        return jnp.where(iota(s.shape, 1) < 4, s, k)

    first = 5 - 4 * p
    strip[0:PLANES] = cut(source[pl.ds(first, PLANES)], kappa[pl.ds(first, PLANES)])
    strip[PLANES:] = cut(halo[0:6], halo[6:12])
    first = 33 - 29 * p
    corner[0:5] = cut(source[pl.ds(first, 5)], kappa[pl.ds(first, 5)])
    corner[5:6] = cut(message[8:9], message[9:10])


def chunked(count, body, size=4):
    def step(i, _):
        body(i * size)
        return 0

    lax.fori_loop(0, count // size, step, 0)


def faces(kap, cx, cy, cz, weight, diag, first, count, scale, closed, n):
    shape = (n,) + kap.shape[1:]
    last_y = iota(shape, 1) == shape[1] - 1
    first_y = iota(shape, 1) == 0
    last_z = iota(shape, 2) == shape[2] - 1
    first_z = iota(shape, 2) == 0

    def body(i):
        r = first + i
        near = kap[pl.ds(r - 1, n + 2)]
        k, up, down = near[1 : n + 1], near[2:], near[:n]
        yu, yd, zu, zd = roll(k, -1, 1), roll(k, 1, 1), roll(k, -1, 2), roll(k, 1, 2)
        if closed:
            yu, yd = jnp.where(last_y, 0.0, yu), jnp.where(first_y, 0.0, yd)
            zu, zd = jnp.where(last_z, 0.0, zu), jnp.where(first_z, 0.0, zd)
        half = 0.5 * scale
        total = half * (6.0 * k + ((up + down) + (yu + yd) + (zu + zd)))
        fy, fz = half * (k + yu), half * (k + zu)
        if closed:
            fy, fz = jnp.where(last_y, 0.0, fy), jnp.where(last_z, 0.0, fz)
        cx[pl.ds(r, n)] = half * (k + up)
        cy[pl.ds(r, n)] = fy
        cz[pl.ds(r, n)] = fz
        diag[pl.ds(r, n)] = total
        weight[pl.ds(r, n)] = jnp.where(k > 0.0, OMEGA / jnp.where(k > 0.0, total, 1.0), 0.0)

    chunked(count, body, n)


def around(v, cx, cy, cz, r, n):
    near, fx = v[pl.ds(r - 1, n + 2)], cx[pl.ds(r - 1, n + 1)]
    here, fy, fz = near[1 : n + 1], cy[pl.ds(r, n)], cz[pl.ds(r, n)]
    return here, (
        (fx[1:] * near[2:] + fx[:n] * near[:n])
        + (fy * roll(here, -1, 1) + roll(fy * here, 1, 1))
        + (fz * roll(here, -1, 2) + roll(fz * here, 1, 2))
    )


def sweep(v, out, rhs, cx, cy, cz, weight, first, count, n):
    def body(i):
        r = first + i
        here, total = around(v, cx, cy, cz, r, n)
        out[pl.ds(r, n)] = (1.0 - OMEGA) * here + weight[pl.ds(r, n)] * (rhs[pl.ds(r, n)] + total)

    chunked(count, body, n)


def resid(v, rhs, cx, cy, cz, diag, r, n):
    here, total = around(v, cx, cy, cz, r, n)
    return rhs[pl.ds(r, n)] + total - diag[pl.ds(r, n)] * here


def pair_sums(x):
    x = x.reshape((x.shape[0] // 2, 2) + x.shape[1:])
    return x[:, 0] + x[:, 1]


def down_kernel(
    n_gy, source_in, kappa_in, halo_in, across, along_in, corner, left, kappa, weight, v, along, beside, message, parts,
    rhs, cx, cy, cz, diag, v1, v2, sums, flat, halo, packs, done,
):
    p, c, b, t = place()
    first = 5 - 4 * p
    edge = jnp.where(c == 0, b == 0, b == n_gy - 1).astype(jnp.int32)
    for ref in (kappa, cx, weight, v1, v2, left):
        ref[0:5] = jnp.zeros((5, 16, 256), F32)
        ref[37:42] = jnp.zeros((5, 16, 256), F32)

    sub = iota((1, 8, 128), 1)
    sides = [jnp.full((1, 8, 128), (1 - edge) * side, jnp.int32) for side in (1 - c, c)]

    def merge(got):
        s, k = pltpu.roll(got, 1 + 2 * c, 1), pltpu.roll(got, 4 - 4 * c, 1)
        s = [jnp.where((sub >= at) & (sub < at + 4) & (side > 0), s, 0.0) for at, side in zip((1, 3), sides)]
        k = [jnp.where((sub >= at) & (sub < at + 4) & (side > 0), k, 0.0) for at, side in zip((0, 4), sides)]
        return jnp.concatenate(s, 1), jnp.concatenate(k, 1)

    def packed(got):
        lane = iota(got.shape, 1)
        wide, zero = roll(got, 64, 1), jnp.zeros_like(got)
        return (
            pick(p, zero, roll(got, 16, 1)),
            pick(p, jnp.where(lane >= 64, wide, 0.0), zero),
            pick(p, jnp.where(lane < 16, wide, 0.0), zero),
        )

    s, k = merge(along_in[PLANES:])
    s2, k2 = merge(corner[...])
    halo[0:6] = halo_in[0:6] + s
    halo[6:12] = halo_in[6:12] + k
    for n, more in enumerate((s2, k2)):
        for i, part in zip((0, 4, 5), packed(across[8 + n] + more[5])):
            halo[6 * n + i] = halo[6 * n + i] + part
    lane = iota((16, 128), 1)
    s_lanes = pick(t, (lane < 10).astype(jnp.int32), (lane >= 118).astype(jnp.int32)) > 0
    k_lanes = pick(t, (lane < 11).astype(jnp.int32), (lane >= 117).astype(jnp.int32)) > 0

    def enter(i):
        r = first + i
        rows = pl.ds(r, SIZE)
        s, k = merge(along_in[pl.ds(i, SIZE)])
        far_s, far_k = [], []
        for j in range(SIZE):
            tile, by = (r + j) >> 3, 16 * ((r + j) & 7)
            far_s.append(jnp.where(s_lanes, pltpu.roll(halo[tile], (127 - by - 9 * t) & 127, 1), 0.0)[None])
            far_k.append(jnp.where(k_lanes, pltpu.roll(halo[6 + tile], (128 - by - 11 * t) & 127, 1), 0.0)[None])
        rhs[rows] = jnp.concatenate([source_in[rows] + s, jnp.concatenate(far_s, 0)], 2)
        kappa[rows] = jnp.concatenate([kappa_in[rows] + k, jnp.concatenate(far_k, 0)], 2)

    chunked(PLANES, enter, SIZE)
    at = pl.ds(36 - 34 * p, 4)
    rhs[at, :, 0:128] = rhs[at, :, 0:128] + across[0:4]
    at = pl.ds(37 - 36 * p, 4)
    kappa[at, :, 0:128] = kappa[at, :, 0:128] + across[4:8]
    at = pl.ds(36 - 35 * p, 5)
    rhs[at, :, 0:128] = rhs[at, :, 0:128] + s2[0:5]
    kappa[at, :, 0:128] = kappa[at, :, 0:128] + k2[0:5]
    faces(kappa, cx, cy, cz, weight, diag, first, PLANES, 1.0, False, PLANES)

    def coarse(fine):
        two = pair_sums(fine)
        n = 16 * two.shape[0]
        two = two.reshape(n, 256)
        halves = []
        for i in range(2):
            at = 320 * i
            sums[at : at + n] = two[:, 128 * i : 128 * (i + 1)]
            halves.append(sums[pl.ds(at, n // 2, stride=2), :] + sums[pl.ds(at + 1, n // 2, stride=2), :])
        return dot(jnp.concatenate(halves, 1), halving(256)).reshape(n // 16, 8, 128)

    rows = pl.ds(first, PLANES)
    v1[rows] = weight[rows] * rhs[rows]
    sweep(v1, v2, rhs, cx, cy, cz, weight, first, PLANES, PLANES)
    left[rows] = resid(v2, rhs, cx, cy, cz, diag, first, PLANES)
    k1 = coarse(kappa[1:41])
    r1 = coarse(left[5:37])
    edge = jnp.zeros((2, 8, 128), F32)
    at = iota(r1.shape, 1)
    part = jnp.concatenate([edge, jnp.where((at >= 2) & (at < 6), r1, 0.0), edge], 0)
    level = Level(k1, 0.25, closed=False)
    u1 = level.weight * part
    u2 = level.sweep(u1, part)
    sub, lane = iota((8, 128), 0), iota((8, 128), 1)

    def means(fine):
        n = 2 * fine.shape[0]
        sums[0 : 2 * n] = pair_sums(fine).reshape(2 * n, 128)
        return dot(sums[pl.ds(0, n, stride=2), :] + sums[pl.ds(1, n, stride=2), :], halving(128))

    flat[0:40, :] = means(level.resid(u2, part))
    tile = jnp.zeros((8, 128), F32)
    for y in range(4):
        tile = tile + roll(jnp.where(lane < 32, flat[pl.ds(4 + y, 8, stride=4), :], 0.0), 32 * y, 1)
    beyond = jnp.where((sub < 4) & (lane < 32), pick(p, flat[36:44, :], flat[0:8, :]), 0.0)
    second = roll(beyond, 64, 1)
    flat[0:40, :] = means(k1)
    for y in range(2):
        second = second + roll(jnp.where(lane < 32, flat[pl.ds(5 + y, 8, stride=4), :], 0.0), 32 * y, 1)
    for d in range(parts.shape[0]):
        packs[d, 0:8] = tile
        packs[d, 8:16] = second
    sending = pltpu.make_async_copy(packs, parts, done.at[0])
    sending.start()
    v[...] = roll(v2[5:37, :, :128], -4, 1)[:, :8]
    k = k1[2:18]
    v1c = level.weight[2:18] * r1
    tiles = jnp.where(iota(r1.shape, 1) < 4, roll(r1, -2, 1), roll(k, 2, 1))
    along[0:16] = tiles
    beside[0:16] = tiles
    for i in range(2):
        far, near = jnp.zeros((8, 128), F32), jnp.zeros((8, 128), F32)
        for j in range(8):
            cells = v1c[8 * i + j]
            last, start = roll(cells, j - 5, 0), roll(cells, j - 2, 0)
            far = jnp.where(sub == j, pick(c, last, start), far)
            near = jnp.where(sub == j, pick(c, start, last), near)
        along[16 + i] = far
        beside[16 + i] = near
    message[0:4] = along[pl.ds(12 - 12 * p, 4)]
    message[4] = roll(pick(p, v1c[12], v1c[3]), -2, 0)
    message[5] = roll(pick(p, v1c[15], v1c[0]), -2, 0)
    sending.wait()


def middle_kernel(n_gy, mine, across, both, r1, k1, weight, v2, cx, cy, cz, diag, v1):
    p, c, b, t = place()
    edge = jnp.where(c == 0, b == 0, b == n_gy - 1).astype(jnp.int32)
    for ref in (r1, k1, cx, weight, v1, v2):
        ref[...] = jnp.zeros_like(ref)
    sub = iota((8, 128), 0)
    zero = jnp.zeros((8, 128), F32)
    middle = (sub >= 2) & (sub < 6)

    def around_mine(at):
        s, g = both[24 + at], pick(edge, both[at], zero)
        return pick(c, g, s), pick(c, s, g)

    def joined(low, o, high):
        first = jnp.where(middle, roll(low, 2, 0), jnp.where(sub >= 6, roll(o, 6, 0), 0.0))
        return first, jnp.where(sub < 2, roll(o, -2, 0), jnp.where(middle, roll(high, 2, 0), 0.0))

    for j in range(20):
        row = 6 + j if j < 16 else 6 + j - 20 * p
        o = mine[j] if j < 16 else across[j - 16]
        low, high = around_mine(j if j < 16 else j + 2)
        r1[row, 0:8], r1[row, 8:16] = joined(low, o, high)
        k1[row, 0:8], k1[row, 8:16] = joined(*[roll(tile, 4, 0) for tile in (low, o, high)])
    first = 6 - 4 * p
    faces(k1, cx, cy, cz, weight, diag, first, 20, 0.25, False, 20)
    rows = pl.ds(first, 20)
    v1[rows] = weight[rows] * r1[rows]
    ends = []
    for i in range(2):
        low, high = around_mine(16 + i)
        ends += [(6 + 8 * i + j, roll(low, 2 - j, 0), roll(high, 5 - j, 0)) for j in range(8)]
    low, high = around_mine(23)
    ends.append((22 - 17 * p, roll(low, 2, 0), roll(high, 2, 0)))
    for r, low, high in ends:
        v1[r, 0:8] = jnp.where(sub == 2, low, v1[r, 0:8])
        v1[r, 8:16] = jnp.where(sub == 5, high, v1[r, 8:16])
    low, high = around_mine(22)
    r = 25 - 23 * p
    v1[r, 0:8], v1[r, 8:16] = joined(low, across[4], high)
    sweep(v1, v2, r1, cx, cy, cz, weight, first, 20, 20)


def shift(x, by, axis):
    if axis == 0:
        zero = jnp.zeros((1,) + x.shape[1:], x.dtype)
        return jnp.concatenate([x[1:], zero] if by > 0 else [zero, x[:-1]], 0)
    return roll(x, -by, axis)


SIDES = [(axis, by) for axis in range(3) for by in (1, -1)]


class Level:
    def __init__(self, kappa, scale, closed=True):
        half = 0.5 * scale
        at = iota(kappa.shape, 1)
        ends = {1: at == kappa.shape[1] - 1, -1: at == 0}
        near = [shift(kappa, by, axis) for axis, by in SIDES]
        if closed:
            near[2:4] = [jnp.where(ends[by], 0.0, k) for by, k in zip((1, -1), near[2:4])]
        self.diag = half * (6.0 * kappa + (near[0] + near[1]) + (near[2] + near[3]) + (near[4] + near[5]))
        self.faces = [half * (kappa + other) for other in near]
        if closed:
            self.faces[2:4] = [jnp.where(ends[by], 0.0, f) for by, f in zip((1, -1), self.faces[2:4])]
        inside = kappa > 0.0
        self.weight = jnp.where(inside, OMEGA / jnp.where(inside, self.diag, 1.0), 0.0)

    def around(self, v):
        terms = [f * shift(v, by, axis) for f, (axis, by) in zip(self.faces, SIDES)]
        return (terms[0] + terms[1]) + (terms[2] + terms[3]) + (terms[4] + terms[5])

    def sweep(self, v, rhs):
        return (1.0 - OMEGA) * v + self.weight * (rhs + self.around(v))

    def resid(self, v, rhs):
        return rhs + self.around(v) - self.diag * v


def halved(x, scratch):
    nx, ny = x.shape[0] // 2, x.shape[1] // 2
    pairs = x.reshape(nx, 2, 2 * ny, 128)
    scratch[0 : 2 * nx * ny, :] = (pairs[:, 0] + pairs[:, 1]).reshape(2 * nx * ny, 128)
    return halved_yz(scratch, nx, ny)


def halved_yz(scratch, nx, ny):
    halves = scratch[pl.ds(0, nx * ny, stride=2), :] + scratch[pl.ds(1, nx * ny, stride=2), :]
    return dot(halves, halving(128)).reshape(nx, ny, 128)


def doubling():
    shape = (128, 128)
    return jnp.where((iota(shape, 1) >> 1) == iota(shape, 0), 1.0, 0.0).astype(F32)


def doubled_yz(e, scratch):
    nx, ny, _ = e.shape
    wide = dot(e.reshape(nx * ny, 128), doubling())
    scratch[pl.ds(0, nx * ny, stride=2), :] = wide
    scratch[pl.ds(1, nx * ny, stride=2), :] = wide
    return scratch[0 : 2 * nx * ny, :].reshape(nx, 2 * ny, 128)


def doubled(e, scratch):
    e = doubled_yz(e, scratch)
    nx, ny, _ = e.shape
    return jnp.broadcast_to(e[:, None], (nx, 2, ny, 128)).reshape(2 * nx, ny, 128)


def up_kernel(
    n_gy, blocks, more, r1, k1, w1, v21, left, kappa, weight, v2, keep, give,
    r2, k2, tall, flat, sums, fx, fy, fz, ua, ub, cx, cy, cz, va, vb,
):
    p, c, b, t = place()
    first = 5 - 4 * p
    n_y = 4 * n_gy
    for ref in (va, vb, cx):
        ref[0:5] = jnp.zeros((5, 16, 256), F32)
        ref[37:42] = jnp.zeros((5, 16, 256), F32)
    for ref in (fx, ua, ub):
        ref[...] = jnp.zeros_like(ref)

    lane, sub = iota((8, 128), 1), iota((8, 128), 0)
    cells = {(y, gp): jnp.zeros((8, 128), F32) for y in range(-1, n_y + 1) for gp in range(2)}
    pairs = n_y // 2

    def block(gp, q, gz, half):
        at, rows = (gp * n_gy + q // 2) * 2 + gz, slice(8 * half, 8 * half + 8)
        return pick(c ^ (q % 2), blocks[at, rows, :], more[at, rows, :])

    for gp in range(2):
        for q in range(pairs):
            whole = []
            for gz in range(2):
                ends = jnp.zeros((8, 128), F32)
                if q + 1 < pairs:
                    ends = jnp.where(lane < 32, block(gp, q + 1, gz, 0), ends)
                if q > 0:
                    ends = jnp.where(lane >= 96, block(gp, q - 1, gz, 0), ends)
                whole.append(block(gp, q, gz, 0) + roll(ends, 64, 1))
            near, far = whole
            near2, far2 = [block(gp, q, gz, 1) for gz in range(2)]
            for y in range(2):
                high = jnp.where(lane < 64, roll(far, -32 * y, 1), 0.0)
                own = jnp.where(lane < 32, roll(near, -32 * (y + 1), 1), high)
                cells[2 * q + y, gp] = cells[2 * q + y, gp] + own
                high = jnp.where(lane < 64, roll(far2, 32 * (1 - y), 1), 0.0)
                k2[2 * q + y, 8 * gp : 8 * gp + 8, :] = jnp.where(lane < 32, roll(near2, -32 * y, 1), high)
            high = jnp.where(lane < 64, roll(far2, -32, 1), 0.0)
            beyond = jnp.where(lane < 32, roll(near2, -64, 1), high)
            goal = 0 if gp == 0 else 7
            for y in range(-1, 3):
                spot = 2 * q + y, 1 - gp
                cells[spot] = cells[spot] + jnp.where(sub == goal, roll(beyond, goal - y - 1, 0), 0.0)
    for y in range(n_y):
        for gp in range(2):
            r2[y, 8 * gp : 8 * gp + 8, :] = cells[y, gp]
    middle, rhs2 = Level(k2[...], 0.0625), r2[...]
    m2 = middle.weight * rhs2
    m2 = middle.sweep(m2, rhs2)
    rhs3 = halved(middle.resid(m2, rhs2), sums)
    bottom = Level(halved(k2[...], sums), 0.015625)
    m3 = bottom.weight * rhs3
    for _ in range(COARSE_SWEEPS - 1):
        m3 = bottom.sweep(m3, rhs3)
    m2 = m2 + doubled(m3, sums)
    for _ in range(SMOOTH):
        m2 = middle.sweep(m2, rhs2)

    shape = (128, 128)
    z = iota(shape, 1)
    z = jnp.where(z < 96, z, z - 128)
    spread = jnp.where(32 * t + (z >> 1) == iota(shape, 0), 1.0, 0.0).astype(F32)
    tall[...] = jnp.zeros_like(tall)
    tall[4 : 4 + n_y, 8:24, :] = dot(m2.reshape(16 * n_y, 128), spread).reshape(n_y, 16, 128)
    for j in range(8):
        cells = tall[4 * b + 2 * c + 1 + j]
        flat[64 * j : 64 * j + 32, :] = cells
        flat[64 * j + 32 : 64 * j + 64, :] = cells
    for i in range(14):
        e = pick(p, flat[pl.ds(5 + i, 16, stride=32), :], flat[pl.ds(13 + i, 16, stride=32), :])
        for r in (2 * i, 2 * i + 1):
            ua[r] = v21[r] + jnp.where(w1[r] > 0.0, e, 0.0)
    at = 6 - 4 * p
    rows = pl.ds(at, 20)
    near = k1[pl.ds(at, 21)]
    k = near[:20]
    fx[rows] = 0.125 * (k + near[1:])
    fy[rows] = 0.125 * (k + roll(k, -1, 1))
    fz[rows] = 0.125 * (k + roll(k, -1, 2))
    sweep(ua, ub, r1, fx, fy, fz, w1, at, 20, 20)
    sweep(ub, ua, r1, fx, fy, fz, w1, at, 20, 20)

    e = roll(ua[5:23], -4, 1)[:, :8].reshape(144, 128)
    flat[pl.ds(0, 144, stride=2), :] = e
    flat[pl.ds(1, 144, stride=2), :] = e
    shape = (128, 256)
    spread = jnp.where((iota(shape, 1) >> 1) == iota(shape, 0), 1.0, 0.0).astype(F32)
    e = dot(flat[0:288, :], spread).reshape(18, 16, 256)
    for k in range(18):
        for r in (2 * k + 3, 2 * k + 4):
            va[r] = jnp.where(weight[r] > 0.0, e[k], 0.0)
    rows = pl.ds(first, PLANES)
    near = kappa[pl.ds(first, PLANES + 1)]
    k = near[:PLANES]
    cx[rows] = 0.5 * (k + near[1:])
    cy[rows] = 0.5 * (k + roll(k, -1, 1))
    cz[rows] = 0.5 * (k + roll(k, -1, 2))
    sweep(va, vb, left, cx, cy, cz, weight, first, PLANES, PLANES)
    here, total = around(vb, cx, cy, cz, 5, 32)
    done = (1.0 - OMEGA) * here + weight[5:37] * (left[5:37] + total)
    va[0:32, 0:8, 0:128] = v2[...] + roll(done[:, :, :128], -4, 1)[:, :8]
    keep[...] = va[pl.ds(16 * c, 16), 0:8, 0:128]
    give[...] = va[pl.ds(16 - 16 * c, 16), 0:8, 0:128]


def join_kernel(mine, other, out, done):
    _, c, _, _ = place()
    copies = []
    for i, (part, at) in enumerate(((mine, 8 * c), (other, 8 - 8 * c))):
        copies.append(pltpu.make_async_copy(part, out.at[:, pl.ds(pl.multiple_of(at, 8), 8), :], done.at[i]))
        copies[i].start()
    for copy in copies:
        copy.wait()


def call(kernel, name, outs, scratch, *args):
    where = pltpu.HBM if name == "message" else pltpu.VMEM
    last = 1 if name in ("down", "join") else 0
    if name == "message":
        args = [pltpu.with_memory_space_constraint(a, pltpu.HBM) for a in args]
    return pl.pallas_call(
        kernel,
        name=name,
        out_shape=[jax.ShapeDtypeStruct(s, F32) for s in outs],
        in_specs=[pl.BlockSpec(memory_space=where)] * len(args),
        out_specs=[pl.BlockSpec(memory_space=pltpu.VMEM)] * (len(outs) - last) + [pl.BlockSpec(memory_space=pltpu.HBM)] * last,
        scratch_shapes=[
            pltpu.SemaphoreType.DMA((s,)) if isinstance(s, int) else pltpu.VMEM(*s) for s in scratch
        ],
        compiler_params=pltpu.CompilerParams(vmem_limit_bytes=16 * 1024 * 1024),
        cost_estimate=pl.CostEstimate(flops=10**7, bytes_accessed=4 * 10**6, transcendentals=0),
    )(*args)


def paired(chi, inducing, record_dest, record_cell, record_value):
    n_gy = lax.axis_size("gy")
    everyone = ("gx", "gy", "gz")
    window = (ROWS, 16, 256)
    big = [(window, F32)]
    chi, inducing, message, spill = call(
        message_kernel,
        "message",
        [(16, 16, 128), (3, 16, 16, 128), (120, 128), (48, 128)],
        [((8, 128), jnp.int32)] * 2 + [((8, 128), F32), 11],
        chi,
        inducing,
        record_dest.reshape(8, 128),
        record_cell.reshape(8, 128),
        record_value.reshape(8, 128),
    )
    got = lax.ppermute(message, "gz", [(0, 1), (1, 0)])
    spread = [((256, 1024), BF16), ((512, 1024), BF16)]
    source, total = call(
        source_kernel,
        "source",
        [(18, 24, 128), (256, 256)],
        spread,
        chi,
        inducing,
        message,
    )
    own, sent = call(
        deposit_kernel,
        "deposit",
        [(39, 16, 128)] * 2,
        [((39, 24, 128), F32)] + spread,
        source,
        spill,
        chi,
        total,
        got,
    )
    swap = [(0, 1), (1, 0), (2, 3), (3, 2)]
    got = lax.ppermute(sent, "gx", swap)
    held = [(ROWS, 16, 128), (ROWS, 16, 128), (12, 16, 128)]
    *fields, message, strip, corner = call(
        pair_kernel, "pair", held + [(10, 16, 128), (PLANES + 6, 8, 128), (6, 8, 128)], [], own, got
    )
    cross = [(0, 2), (2, 0), (1, 3), (3, 1)]
    across = lax.ppermute(message, "gx", cross)
    turns, corners = [], []
    for p in range(2):
        for b in range(n_gy - 1):
            low, high = (2 * p + 1) * n_gy + b, 2 * p * n_gy + b + 1
            turns += [(low, high), (high, low)]
            high = 2 * (1 - p) * n_gy + b + 1
            corners += [(low, high), (high, low)]
    for low, high in ((0, 2 * n_gy), (2 * n_gy - 1, 4 * n_gy - 1)):
        turns += [(low, high), (high, low)]
        corners += [(low, high), (high, low)]
    strip = lax.ppermute(strip, ("gx", "gy"), turns)
    corner = lax.ppermute(corner, ("gx", "gy"), corners)
    *fine, along, beside, message, parts = call(
        functools.partial(down_kernel, n_gy),
        "down",
        [window] * 3 + [(32, 8, 128), (18, 8, 128), (18, 8, 128), (6, 8, 128), (4 * n_gy, 16, 128)],
        big * 7 + [((640, 128), F32), ((48, 128), F32), ((12, 16, 128), F32)]
        + [((4 * n_gy, 16, 128), F32), 1],
        *fields,
        across,
        strip,
        corner,
    )
    n = 2 * n_gy
    groups = [[(2 * p + c) * n + i for p in range(2) for i in range(n)] for c in range(2)]
    blocks = lax.all_to_all(
        parts, ("gx", "gy", "gz"), split_axis=0, concat_axis=0, tiled=True, axis_index_groups=groups
    )
    more = lax.ppermute(blocks, "gx", swap)
    across = lax.ppermute(message, "gx", cross)
    got = lax.ppermute(jnp.concatenate([along, across]), ("gx", "gy"), turns)
    other = lax.ppermute(jnp.concatenate([beside, across]), "gx", swap)
    window1 = (28, 16, 128)
    big1 = [(window1, F32)]
    coarse = call(
        functools.partial(middle_kernel, n_gy),
        "middle",
        [window1] * 4,
        big1 * 5,
        beside,
        across,
        jnp.concatenate([got, other]),
    )
    level2 = ((4 * n_gy, 16, 128), F32)
    keep, give = call(
        functools.partial(up_kernel, n_gy),
        "up",
        [(16, 8, 128)] * 2,
        [level2] * 2
        + [((4 * n_gy + 8, 32, 128), F32), ((512, 128), F32), ((64 * n_gy, 128), F32)]
        + big1 * 5
        + big * 5,
        blocks,
        more,
        *coarse,
        *fine,
    )
    got = lax.ppermute(give, "gx", swap)
    (out,) = call(join_kernel, "join", [(16, 16, 128)], [2], keep, got)
    return out


def solution(mesh):
    placed = (
        P("gx", "gy", "gz"),
        P(None, "gx", "gy", "gz"),
        P("gx", "gy", "gz", None, None),
        P("gx", "gy", "gz", None),
        P("gx", "gy", "gz", None),
    )
    small = mesh.shape["gx"] == 4 and mesh.shape["gz"] == 2 and mesh.shape["gy"] <= 4
    return jax.shard_map(
        paired if small else general,
        mesh=mesh,
        in_specs=placed,
        out_specs=P("gx", "gy", "gz"),
        check_vma=False,
    )
```

```python
import functools

import jax
import jax.numpy as jnp
from jax import lax
from jax.experimental import pallas as pl
from jax.experimental.pallas import tpu as pltpu
from jax.sharding import PartitionSpec as P

SMOOTH = 2
LEVELS = 3
COARSE_SWEEPS = 8
CAP = 640


OMEGA = 0.8


def padded_2(cells, sides, width):
    for axis, dim in sides:
        count = lax.axis_size(axis)
        ends = count - 1
        head = lax.slice_in_dim(cells, 0, width, axis=dim)
        tail = lax.slice_in_dim(cells, cells.shape[dim] - width, cells.shape[dim], axis=dim)
        cells = jnp.concatenate(
            [
                lax.ppermute(tail, axis, [(i, (i + 1) % count) for i in range(ends)]),
                cells,
                lax.ppermute(head, axis, [((i + 1) % count, i) for i in range(ends)]),
            ],
            axis=dim,
        )
    return cells


def restrict(x):
    s = x.shape
    return x.reshape(s[0] // 2, 2, s[1] // 2, 2, s[2] // 2, 2).mean(axis=(1, 3, 5))


def prolong(e):
    return jnp.repeat(jnp.repeat(jnp.repeat(e, 2, 0), 2, 1), 2, 2)


def neighbours(padded):
    return [
        padded[2:, 1:-1, 1:-1],
        padded[:-2, 1:-1, 1:-1],
        padded[1:-1, 2:, 1:-1],
        padded[1:-1, :-2, 1:-1],
        padded[1:-1, 1:-1, 2:],
        padded[1:-1, 1:-1, :-2],
    ]


def face_pad(x):
    return padded_2(x, (("gx", 0), ("gy", 1), ("gz", 2)), 1)


def coefficients(kappa):
    return [0.5 * (kappa + other) for other in neighbours(face_pad(kappa))]


def apply_op(v, coefs, scale):
    total = jnp.zeros_like(v)
    for coef, other in zip(coefs, neighbours(face_pad(v))):
        total = total + coef * (v - other)
    return scale * total


def cycle(level, rhs, kappa):
    scale = 0.25**level
    coefs = coefficients(kappa)
    diag = scale * (coefs[0] + coefs[1] + coefs[2] + coefs[3] + coefs[4] + coefs[5])
    v = OMEGA * rhs / diag
    for sweep in range((COARSE_SWEEPS if level == LEVELS else SMOOTH) - 1):
        v = v + OMEGA * (rhs - apply_op(v, coefs, scale)) / diag
    if level == LEVELS:
        return v
    resid = rhs - apply_op(v, coefs, scale)
    corr = cycle(level + 1, restrict(resid), restrict(kappa))
    v = v + prolong(corr)
    for sweep in range(SMOOTH):
        v = v + OMEGA * (rhs - apply_op(v, coefs, scale)) / diag
    return v


def general(chi, inducing, record_dest, record_cell, record_value):
    n_gz = lax.axis_size("gz")
    dest = record_dest[0, 0, 0, :, 0]
    cells = record_cell[0, 0, 0]
    values = record_value[0, 0, 0]
    onehot = (dest[:, None] == jnp.arange(n_gz, dtype=jnp.int32)[None, :]).astype(jnp.int32)
    ranks = jnp.sum((jnp.cumsum(onehot, axis=0) - 1) * onehot, axis=1)
    outgoing = jnp.zeros((n_gz, 2, CAP), jnp.float32)
    outgoing = outgoing.at[dest, 0, ranks].set(values)
    outgoing = outgoing.at[dest, 1, ranks].set(cells.astype(jnp.float32))
    incoming = lax.all_to_all(outgoing, "gz", split_axis=0, concat_axis=0, tiled=True)
    in_values = incoming[:, 0].reshape(-1)
    in_cells = incoming[:, 1].reshape(-1).astype(jnp.int32)
    moment_x = face_pad(chi * inducing[0])
    moment_y = face_pad(chi * inducing[1])
    moment_z = face_pad(chi * inducing[2])
    source = -0.5 * (
        moment_x[2:, 1:-1, 1:-1]
        - moment_x[:-2, 1:-1, 1:-1]
        + (moment_y[1:-1, 2:, 1:-1] - moment_y[1:-1, :-2, 1:-1])
        + (moment_z[1:-1, 1:-1, 2:] - moment_z[1:-1, 1:-1, :-2])
    )
    rhs = source.reshape(-1).at[in_cells].add(in_values).reshape(source.shape)
    return cycle(0, rhs, 1.0 + chi)


F32 = jnp.float32
BF16 = jnp.bfloat16
ROWS = 42
PLANES = 36
SIZE = 12


def iota(shape, dim):
    return lax.broadcasted_iota(jnp.int32, shape, dim)


def roll(x, shift, axis):
    shift = shift % x.shape[axis]
    return pltpu.roll(x, shift, axis) if shift else x


def pick(flag, first, second):
    return jnp.where(jnp.full(first.shape, flag, jnp.int32) == 0, first, second)


def dot(a, b):
    total = 0.0
    for _ in range(3):
        part = a.astype(BF16)
        total = total + jnp.dot(part, b.astype(BF16), preferred_element_type=F32)
        a = a - part.astype(F32)
    return total


def halving(lanes):
    shape = (lanes, 128)
    return jnp.where((iota(shape, 0) >> 1) == iota(shape, 1), 0.125, 0.0).astype(F32)


def place():
    gx, gy, gz = lax.axis_index("gx"), lax.axis_index("gy"), lax.axis_index("gz")
    return gx >> 1, gx & 1, gy, gz


def stretch(x):
    return roll(jnp.concatenate([x, jnp.zeros((8, x.shape[1]), F32)], 0), 4, 0)


def message_kernel(*refs):
    given, (chi, inducing, message, spill), (dest, cell, value, done) = refs[:5], refs[5:9], refs[9:]
    _, _, _, t = place()
    held = (chi, inducing, dest, cell, value)
    pairs = [(a.at[4 * i : 4 * i + 4], b.at[4 * i : 4 * i + 4]) for i in range(4) for a, b in [(given[0], held[0])]]
    pairs += [(given[1].at[:, 4 * i : 4 * i + 4], held[1].at[:, 4 * i : 4 * i + 4]) for i in range(4)]
    pairs += list(zip(given[2:], held[2:]))
    copies = [pltpu.make_async_copy(a, b, done.at[i]) for i, (a, b) in enumerate(pairs)]
    for i in (0, 4, 1, 5, 2, 6, 3, 7, 8, 9, 10):
        copies[i].start()
    lane = iota((16, 128), 1)
    turn = 11 - 10 * t
    packs = [[jnp.zeros((16, 128), F32)] * 2 for _ in range(4)]
    for x in range(16):
        if x % 4 == 0:
            copies[x // 4].wait()
            copies[4 + x // 4].wait()
        by = 16 * (x % 8)
        wanted = (lane >= by + t) & (lane < by + t + 11)
        near = jnp.where(wanted, pltpu.roll(chi[x], (turn + by) & 127, 1), 0.0)
        parts = [1.0 + near]
        parts += [near * pltpu.roll(inducing[d, x], (turn + by) & 127, 1) for d in range(3)]
        for pack, part in zip(packs, parts):
            pack[x // 8] = jnp.where(wanted, part, pack[x // 8])
    k, mx, my, mz = [jnp.concatenate(pack, 1) for pack in packs]
    lane = iota((16, 256), 1)
    dx = jnp.where(lane < 240, roll(mx, -16, 1), 0.0) - jnp.where(lane >= 16, roll(mx, 16, 1), 0.0)
    y = stretch(my)
    dz = roll(mz, -1, 1) - roll(mz, 1, 1)
    body = -0.5 * (stretch(dx + dz) + (roll(y, -1, 0) - roll(y, 1, 0)))
    lane = iota((24, 128), 1)
    before, after = stretch(mx[:, :128]), stretch(mx[:, 128:])
    ends = 0.5 * (jnp.where((lane >= 16) & (lane < 32), roll(after, 32, 1), 0.0) - jnp.where(lane < 16, before, 0.0))

    def eleven(tile):
        tile = pick(t, roll(tile, -1, 1), tile)
        return jnp.where((iota(tile.shape, 1) & 15) < 11, tile, 0.0)

    slot = iota((24, 256), 1) & 15
    own = pick(t, jnp.where(slot == 11, body, 0.0), jnp.where(slot == 0, body, 0.0))
    own = pick(t, roll(own, -10, 1), roll(own, 9, 1))
    body = eleven(body)
    k = pick(t, k, roll(k, -1, 1))
    for i in range(2):
        cut = slice(128 * i, 128 * (i + 1))
        spill[24 * i : 24 * (i + 1)] = own[:, cut]
        message[24 * i : 24 * (i + 1)] = body[:, cut]
        message[72 + 16 * i : 88 + 16 * i] = k[:, cut]
    message[48:72] = eleven(ends)
    for copy in copies[8:]:
        copy.wait()
    message[104:112] = value[...]
    message[112:120] = (dest[...] * 32768 + cell[...]).astype(F32)


def spread_records(records, t, at_row, at_column):
    row, slot = iota((256, 128), 0), iota((16, 128), 0)
    z_of = iota((128, 128), 0)
    at_column[432:512] = jnp.zeros((80, 1024), BF16)
    for j in range(8):
        value = records[104 + j : 105 + j, :]
        code = records[112 + j : 113 + j, :].astype(jnp.int32)
        cells = code & 32767
        z = ((code >> 15) - t) * 128 + (cells & 127)
        far = z - 128 + 138 * t
        far = jnp.where((far >= 0) & (far < 10), far + 1 - t, 16)
        cut = slice(128 * j, 128 * (j + 1))
        at_row[:, cut] = jnp.where(row == (cells >> 7), 1.0, 0.0).astype(BF16)
        here, there = z_of == z, slot == far
        for i in range(3):
            short = value.astype(BF16).astype(F32)
            at_column[128 * i : 128 * (i + 1), cut] = jnp.where(here, short, 0.0).astype(BF16)
            at_column[384 + 16 * i : 400 + 16 * i, cut] = jnp.where(there, short, 0.0).astype(BF16)
            value = value - short
    total = lax.dot_general(
        at_row[...], at_column[...], (((1,), (1,)), ((), ())), preferred_element_type=F32
    )
    near = (total[:, 256:384] + total[:, 128:256]) + total[:, 0:128]
    return jnp.concatenate([near, total[:, 384:512]], 1)


def source_kernel(chi, inducing, records, source, total, at_row, at_column):
    _, _, _, t = place()
    lane = iota((16, 128), 1)
    zero = jnp.zeros((16, 128), F32)
    mx = [zero, zero] + [chi[x] * inducing[0, x] for x in range(16)] + [zero, zero]
    for i in range(18):
        flat = mx[i + 2] - mx[i]
        if 1 <= i <= 16:
            my, mz = chi[i - 1] * inducing[1, i - 1], chi[i - 1] * inducing[2, i - 1]
            flat = flat + (jnp.where(lane == 127, 0.0, roll(mz, -1, 1)) - jnp.where(lane == 0, 0.0, roll(mz, 1, 1)))
            y = stretch(my)
            source[i] = -0.5 * (stretch(flat) + (roll(y, -1, 0) - roll(y, 1, 0)))
        else:
            source[i] = -0.5 * stretch(flat)
    total[...] = spread_records(records, t, at_row, at_column)


def deposit_kernel(source, spill, chi, mine, other, own, sent, all_, at_row, at_column):
    _, c, _, t = place()
    total = mine[...] + spread_records(other, t, at_row, at_column)
    lane = iota((24, 128), 1)
    halo = [other[24 * i : 24 * (i + 1)] + spill[24 * i : 24 * (i + 1)] for i in range(2)]
    for i in range(18):
        x = i - 1
        if 0 <= x < 16:
            got = total[16 * x : 16 * x + 16, 128:]
            got = stretch((roll(got, -32, 1) + roll(got, -16, 1)) + got)
            halo[x // 8] = halo[x // 8] + roll(jnp.where(lane < 16, got, 0.0), 16 * (x % 8), 1)
            add = stretch(total[16 * x : 16 * x + 16, :128])
            tile, by = other[24 * (x // 8) : 24 * (x // 8) + 24], 16 * (x % 8)
        else:
            add = jnp.zeros((24, 128), F32)
            tile, by = other[48:72], 0 if i == 0 else 16
        near = pick(t, roll(tile, 127 - by, 1), roll(tile, -10 - by, 1))
        all_[i] = source[i] + add + jnp.where(lane == 127 - 127 * t, near, 0.0)
    for i in range(16):
        all_[18 + i] = stretch(1.0 + chi[i])
    for i in range(2):
        all_[34 + i] = halo[i]
        all_[37 + i] = stretch(other[72 + 16 * i : 88 + 16 * i])
    all_[36] = other[48:72]
    keep, give = pl.multiple_of(8 * c, 8), pl.multiple_of(8 - 8 * c, 8)
    own[...] = all_[:, pl.ds(keep, 16), :]
    sent[...] = all_[:, pl.ds(give, 16), :]


def pair_kernel(own, other, source, kappa, halo, message, strip, corner):
    p, c, _, _ = place()
    source[...] = jnp.zeros_like(source)
    kappa[...] = jnp.zeros_like(kappa)
    source[pl.ds(4 + 16 * c, 18)] = own[0:18]
    low = 4 + 16 * (1 - c)
    source[pl.ds(low, 18)] = source[pl.ds(low, 18)] + other[0:18]
    kappa[pl.ds(5 + 16 * c, 16)] = own[18:34]
    kappa[pl.ds(low + 1, 16)] = other[18:34]
    lane = iota((16, 128), 1)
    tiles = [jnp.zeros((16, 128), F32)] * 12
    for side in range(2):
        for start, at in ((34, 0), (37, 6)):
            for i in range(2):
                cells = roll(pick(c ^ side, own[start + i], other[start + i]), 80, 1)
                n = at + 2 * side + i
                tiles[n] = tiles[n] + jnp.where(lane >= 80, cells, 0.0)
                tiles[n + 1] = tiles[n + 1] + jnp.where(lane < 80, cells, 0.0)
        ends = roll(pick(c ^ side, own[36], other[36]), 64, 1)
        n = 2 * side
        tiles[n] = tiles[n] + jnp.where((lane >= 64) & (lane < 80), ends, 0.0)
        tiles[n + 2] = tiles[n + 2] + jnp.where((lane >= 80) & (lane < 96), ends, 0.0)
    for i in range(12):
        halo[i] = tiles[i]
    message[0:4] = source[pl.ds(34 - 30 * p, 4)]
    message[4:8] = kappa[pl.ds(33 - 28 * p, 4)]
    for i in range(2):
        low = jnp.where(lane < 64, roll(tiles[6 * i], -64, 1), roll(tiles[6 * i + 1], 64, 1))
        message[8 + i] = jnp.where(lane < 80, pick(p, roll(tiles[6 * i + 4], -16, 1), low), 0.0)

    def cut(s, k):
        s = pick(c, roll(s, -3, 1)[:, :8], roll(s, -9, 1)[:, :8])
        k = pick(c, k[:, :8], roll(k, -4, 1)[:, :8])
        return jnp.where(iota(s.shape, 1) < 4, s, k)

    first = 5 - 4 * p
    strip[0:PLANES] = cut(source[pl.ds(first, PLANES)], kappa[pl.ds(first, PLANES)])
    strip[PLANES:] = cut(halo[0:6], halo[6:12])
    first = 33 - 29 * p
    corner[0:5] = cut(source[pl.ds(first, 5)], kappa[pl.ds(first, 5)])
    corner[5:6] = cut(message[8:9], message[9:10])


def chunked(count, body, size=4):
    def step(i, _):
        body(i * size)
        return 0

    lax.fori_loop(0, count // size, step, 0)


def faces(kap, cx, cy, cz, weight, diag, first, count, scale, closed, n):
    shape = (n,) + kap.shape[1:]
    last_y = iota(shape, 1) == shape[1] - 1
    first_y = iota(shape, 1) == 0
    last_z = iota(shape, 2) == shape[2] - 1
    first_z = iota(shape, 2) == 0

    def body(i):
        r = first + i
        near = kap[pl.ds(r - 1, n + 2)]
        k, up, down = near[1 : n + 1], near[2:], near[:n]
        yu, yd, zu, zd = roll(k, -1, 1), roll(k, 1, 1), roll(k, -1, 2), roll(k, 1, 2)
        if closed:
            yu, yd = jnp.where(last_y, 0.0, yu), jnp.where(first_y, 0.0, yd)
            zu, zd = jnp.where(last_z, 0.0, zu), jnp.where(first_z, 0.0, zd)
        half = 0.5 * scale
        total = half * (6.0 * k + ((up + down) + (yu + yd) + (zu + zd)))
        fy, fz = half * (k + yu), half * (k + zu)
        if closed:
            fy, fz = jnp.where(last_y, 0.0, fy), jnp.where(last_z, 0.0, fz)
        cx[pl.ds(r, n)] = half * (k + up)
        cy[pl.ds(r, n)] = fy
        cz[pl.ds(r, n)] = fz
        diag[pl.ds(r, n)] = total
        weight[pl.ds(r, n)] = jnp.where(k > 0.0, OMEGA / jnp.where(k > 0.0, total, 1.0), 0.0)

    chunked(count, body, n)


def around(v, cx, cy, cz, r, n):
    near, fx = v[pl.ds(r - 1, n + 2)], cx[pl.ds(r - 1, n + 1)]
    here, fy, fz = near[1 : n + 1], cy[pl.ds(r, n)], cz[pl.ds(r, n)]
    return here, (
        (fx[1:] * near[2:] + fx[:n] * near[:n])
        + (fy * roll(here, -1, 1) + roll(fy * here, 1, 1))
        + (fz * roll(here, -1, 2) + roll(fz * here, 1, 2))
    )


def sweep(v, out, rhs, cx, cy, cz, weight, first, count, n):
    def body(i):
        r = first + i
        here, total = around(v, cx, cy, cz, r, n)
        out[pl.ds(r, n)] = (1.0 - OMEGA) * here + weight[pl.ds(r, n)] * (rhs[pl.ds(r, n)] + total)

    chunked(count, body, n)


def resid(v, rhs, cx, cy, cz, diag, r, n):
    here, total = around(v, cx, cy, cz, r, n)
    return rhs[pl.ds(r, n)] + total - diag[pl.ds(r, n)] * here


def pair_sums(x):
    x = x.reshape((x.shape[0] // 2, 2) + x.shape[1:])
    return x[:, 0] + x[:, 1]


def down_kernel(
    n_gy, source_in, kappa_in, halo_in, across, along_in, corner, left, kappa, weight, v, along, beside, message, parts,
    rhs, cx, cy, cz, diag, v1, v2, sums, flat, halo, packs, done,
):
    p, c, b, t = place()
    first = 5 - 4 * p
    edge = jnp.where(c == 0, b == 0, b == n_gy - 1).astype(jnp.int32)
    kappa[0:5] = jnp.zeros((5, 16, 256), F32)
    kappa[37:42] = jnp.zeros((5, 16, 256), F32)
    for ref in (cx, weight, v1, v2):
        for r in (0, 2, 3, 4, 37, 38, 39, 41):
            ref[r] = jnp.zeros((16, 256), F32)

    sub = iota((1, 8, 128), 1)
    sides = [jnp.full((1, 8, 128), (1 - edge) * side, jnp.int32) for side in (1 - c, c)]

    def merge(got):
        s, k = pltpu.roll(got, 1 + 2 * c, 1), pltpu.roll(got, 4 - 4 * c, 1)
        s = [jnp.where((sub >= at) & (sub < at + 4) & (side > 0), s, 0.0) for at, side in zip((1, 3), sides)]
        k = [jnp.where((sub >= at) & (sub < at + 4) & (side > 0), k, 0.0) for at, side in zip((0, 4), sides)]
        return jnp.concatenate(s, 1), jnp.concatenate(k, 1)

    def packed(got):
        lane = iota(got.shape, 1)
        wide, zero = roll(got, 64, 1), jnp.zeros_like(got)
        return (
            pick(p, zero, roll(got, 16, 1)),
            pick(p, jnp.where(lane >= 64, wide, 0.0), zero),
            pick(p, jnp.where(lane < 16, wide, 0.0), zero),
        )

    s, k = merge(along_in[PLANES:])
    s2, k2 = merge(corner[...])
    halo[0:6] = halo_in[0:6] + s
    halo[6:12] = halo_in[6:12] + k
    for n, more in enumerate((s2, k2)):
        for i, part in zip((0, 4, 5), packed(across[8 + n] + more[5])):
            halo[6 * n + i] = halo[6 * n + i] + part
    lane = iota((16, 128), 1)
    s_lanes = pick(t, (lane < 10).astype(jnp.int32), (lane >= 118).astype(jnp.int32)) > 0
    k_lanes = pick(t, (lane < 11).astype(jnp.int32), (lane >= 117).astype(jnp.int32)) > 0

    def enter(i):
        r = first + i
        rows = pl.ds(r, SIZE)
        s, k = merge(along_in[pl.ds(i, SIZE)])
        far_s, far_k = [], []
        for j in range(SIZE):
            tile, by = (r + j) >> 3, 16 * ((r + j) & 7)
            far_s.append(jnp.where(s_lanes, pltpu.roll(halo[tile], (127 - by - 9 * t) & 127, 1), 0.0)[None])
            far_k.append(jnp.where(k_lanes, pltpu.roll(halo[6 + tile], (128 - by - 11 * t) & 127, 1), 0.0)[None])
        rhs[rows] = jnp.concatenate([source_in[rows] + s, jnp.concatenate(far_s, 0)], 2)
        kappa[rows] = jnp.concatenate([kappa_in[rows] + k, jnp.concatenate(far_k, 0)], 2)

    chunked(PLANES, enter, SIZE)
    at = pl.ds(36 - 34 * p, 4)
    rhs[at, :, 0:128] = rhs[at, :, 0:128] + across[0:4]
    at = pl.ds(37 - 36 * p, 4)
    kappa[at, :, 0:128] = kappa[at, :, 0:128] + across[4:8]
    at = pl.ds(36 - 35 * p, 5)
    rhs[at, :, 0:128] = rhs[at, :, 0:128] + s2[0:5]
    kappa[at, :, 0:128] = kappa[at, :, 0:128] + k2[0:5]
    faces(kappa, cx, cy, cz, weight, diag, first, PLANES, 1.0, False, PLANES)

    def coarse(fine):
        two = pair_sums(fine)
        n = 16 * two.shape[0]
        two = two.reshape(n, 256)
        halves = []
        for i in range(2):
            at = 320 * i
            sums[at : at + n] = two[:, 128 * i : 128 * (i + 1)]
            halves.append(sums[pl.ds(at, n // 2, stride=2), :] + sums[pl.ds(at + 1, n // 2, stride=2), :])
        return dot(jnp.concatenate(halves, 1), halving(256)).reshape(n // 16, 8, 128)

    rows = pl.ds(first, PLANES)
    v1[rows] = weight[rows] * rhs[rows]
    sweep(v1, v2, rhs, cx, cy, cz, weight, 5 - 2 * p, 34, 34)
    left[pl.ds(5 - p, 33)] = resid(v2, rhs, cx, cy, cz, diag, 5 - p, 33)
    k1 = coarse(kappa[1:41])
    r1 = coarse(left[5:37])
    edge = jnp.zeros((2, 8, 128), F32)
    at = iota(r1.shape, 1)
    part = jnp.concatenate([edge, jnp.where((at >= 2) & (at < 6), r1, 0.0), edge], 0)
    level = Level(k1, 0.25, closed=False)
    u1 = level.weight * part
    u2 = level.sweep(u1, part)
    sub, lane = iota((8, 128), 0), iota((8, 128), 1)

    def means(fine):
        n = 2 * fine.shape[0]
        sums[0 : 2 * n] = pair_sums(fine).reshape(2 * n, 128)
        return dot(sums[pl.ds(0, n, stride=2), :] + sums[pl.ds(1, n, stride=2), :], halving(128))

    flat[0:40, :] = means(level.resid(u2, part))
    tile = jnp.zeros((8, 128), F32)
    for y in range(4):
        tile = tile + roll(jnp.where(lane < 32, flat[pl.ds(4 + y, 8, stride=4), :], 0.0), 32 * y, 1)
    beyond = jnp.where((sub < 4) & (lane < 32), pick(p, flat[36:44, :], flat[0:8, :]), 0.0)
    second = roll(beyond, 64, 1)
    flat[0:40, :] = means(k1)
    for y in range(2):
        second = second + roll(jnp.where(lane < 32, flat[pl.ds(5 + y, 8, stride=4), :], 0.0), 32 * y, 1)
    for d in range(parts.shape[0]):
        packs[d, 0:8] = tile
        packs[d, 8:16] = second
    sending = pltpu.make_async_copy(packs, parts, done.at[0])
    sending.start()
    v[...] = roll(v2[5:37, :, :128], -4, 1)[:, :8]
    k = k1[2:18]
    v1c = level.weight[2:18] * r1
    tiles = jnp.where(iota(r1.shape, 1) < 4, roll(r1, -2, 1), roll(k, 2, 1))
    along[0:16] = tiles
    beside[0:16] = tiles
    for i in range(2):
        far, near = jnp.zeros((8, 128), F32), jnp.zeros((8, 128), F32)
        for j in range(8):
            cells = v1c[8 * i + j]
            last, start = roll(cells, j - 5, 0), roll(cells, j - 2, 0)
            far = jnp.where(sub == j, pick(c, last, start), far)
            near = jnp.where(sub == j, pick(c, start, last), near)
        along[16 + i] = far
        beside[16 + i] = near
    message[0:4] = along[pl.ds(12 - 12 * p, 4)]
    message[4] = roll(pick(p, v1c[12], v1c[3]), -2, 0)
    message[5] = roll(pick(p, v1c[15], v1c[0]), -2, 0)
    sending.wait()


def middle_kernel(n_gy, mine, across, both, r1, k1, weight, v2, cx, cy, cz, diag, v1):
    p, c, b, t = place()
    edge = jnp.where(c == 0, b == 0, b == n_gy - 1).astype(jnp.int32)
    for ref in (r1, k1, cx, weight, v1, v2):
        ref[...] = jnp.zeros_like(ref)
    sub = iota((8, 128), 0)
    zero = jnp.zeros((8, 128), F32)
    middle = (sub >= 2) & (sub < 6)

    def around_mine(at):
        s, g = both[24 + at], pick(edge, both[at], zero)
        return pick(c, g, s), pick(c, s, g)

    def joined(low, o, high):
        first = jnp.where(middle, roll(low, 2, 0), jnp.where(sub >= 6, roll(o, 6, 0), 0.0))
        return first, jnp.where(sub < 2, roll(o, -2, 0), jnp.where(middle, roll(high, 2, 0), 0.0))

    for j in range(20):
        row = 6 + j if j < 16 else 6 + j - 20 * p
        o = mine[j] if j < 16 else across[j - 16]
        low, high = around_mine(j if j < 16 else j + 2)
        r1[row, 0:8], r1[row, 8:16] = joined(low, o, high)
        k1[row, 0:8], k1[row, 8:16] = joined(*[roll(tile, 4, 0) for tile in (low, o, high)])
    first = 6 - 4 * p
    faces(k1, cx, cy, cz, weight, diag, first, 20, 0.25, False, 20)
    rows = pl.ds(first, 20)
    v1[rows] = weight[rows] * r1[rows]
    ends = []
    for i in range(2):
        low, high = around_mine(16 + i)
        ends += [(6 + 8 * i + j, roll(low, 2 - j, 0), roll(high, 5 - j, 0)) for j in range(8)]
    low, high = around_mine(23)
    ends.append((22 - 17 * p, roll(low, 2, 0), roll(high, 2, 0)))
    for r, low, high in ends:
        v1[r, 0:8] = jnp.where(sub == 2, low, v1[r, 0:8])
        v1[r, 8:16] = jnp.where(sub == 5, high, v1[r, 8:16])
    low, high = around_mine(22)
    r = 25 - 23 * p
    v1[r, 0:8], v1[r, 8:16] = joined(low, across[4], high)
    sweep(v1, v2, r1, cx, cy, cz, weight, first, 20, 20)


def shift(x, by, axis):
    if axis == 0:
        zero = jnp.zeros((1,) + x.shape[1:], x.dtype)
        return jnp.concatenate([x[1:], zero] if by > 0 else [zero, x[:-1]], 0)
    return roll(x, -by, axis)


SIDES = [(axis, by) for axis in range(3) for by in (1, -1)]


class Level:
    def __init__(self, kappa, scale, closed=True):
        half = 0.5 * scale
        at = iota(kappa.shape, 1)
        ends = {1: at == kappa.shape[1] - 1, -1: at == 0}
        near = [shift(kappa, by, axis) for axis, by in SIDES]
        if closed:
            near[2:4] = [jnp.where(ends[by], 0.0, k) for by, k in zip((1, -1), near[2:4])]
        self.diag = half * (6.0 * kappa + (near[0] + near[1]) + (near[2] + near[3]) + (near[4] + near[5]))
        self.faces = [half * (kappa + other) for other in near]
        if closed:
            self.faces[2:4] = [jnp.where(ends[by], 0.0, f) for by, f in zip((1, -1), self.faces[2:4])]
        inside = kappa > 0.0
        self.weight = jnp.where(inside, OMEGA / jnp.where(inside, self.diag, 1.0), 0.0)

    def around(self, v):
        terms = [f * shift(v, by, axis) for f, (axis, by) in zip(self.faces, SIDES)]
        return (terms[0] + terms[1]) + (terms[2] + terms[3]) + (terms[4] + terms[5])

    def sweep(self, v, rhs):
        return (1.0 - OMEGA) * v + self.weight * (rhs + self.around(v))

    def resid(self, v, rhs):
        return rhs + self.around(v) - self.diag * v


def halved(x, scratch):
    nx, ny = x.shape[0] // 2, x.shape[1] // 2
    pairs = x.reshape(nx, 2, 2 * ny, 128)
    scratch[0 : 2 * nx * ny, :] = (pairs[:, 0] + pairs[:, 1]).reshape(2 * nx * ny, 128)
    return halved_yz(scratch, nx, ny)


def halved_yz(scratch, nx, ny):
    halves = scratch[pl.ds(0, nx * ny, stride=2), :] + scratch[pl.ds(1, nx * ny, stride=2), :]
    return dot(halves, halving(128)).reshape(nx, ny, 128)


def doubling():
    shape = (128, 128)
    return jnp.where((iota(shape, 1) >> 1) == iota(shape, 0), 1.0, 0.0).astype(F32)


def doubled_yz(e, scratch):
    nx, ny, _ = e.shape
    wide = dot(e.reshape(nx * ny, 128), doubling())
    scratch[pl.ds(0, nx * ny, stride=2), :] = wide
    scratch[pl.ds(1, nx * ny, stride=2), :] = wide
    return scratch[0 : 2 * nx * ny, :].reshape(nx, 2 * ny, 128)


def doubled(e, scratch):
    e = doubled_yz(e, scratch)
    nx, ny, _ = e.shape
    return jnp.broadcast_to(e[:, None], (nx, 2, ny, 128)).reshape(2 * nx, ny, 128)


def up_kernel(
    n_gy, blocks, more, r1, k1, w1, v21, left, kappa, weight, v2, keep, give,
    r2, k2, tall, flat, sums, fx, fy, fz, ua, ub, cx, cy, cz, va, vb,
):
    p, c, b, t = place()
    first = 5 - 4 * p
    n_y = 4 * n_gy
    for ref in (vb, cx):
        for r in (0, 3, 4, 37, 38):
            ref[r] = jnp.zeros((16, 256), F32)
    for ref in (fx, ua, ub):
        ref[...] = jnp.zeros_like(ref)

    lane, sub = iota((8, 128), 1), iota((8, 128), 0)
    cells = {(y, gp): jnp.zeros((8, 128), F32) for y in range(-1, n_y + 1) for gp in range(2)}
    pairs = n_y // 2

    def block(gp, q, gz, half):
        at, rows = (gp * n_gy + q // 2) * 2 + gz, slice(8 * half, 8 * half + 8)
        return pick(c ^ (q % 2), blocks[at, rows, :], more[at, rows, :])

    for gp in range(2):
        for q in range(pairs):
            whole = []
            for gz in range(2):
                ends = jnp.zeros((8, 128), F32)
                if q + 1 < pairs:
                    ends = jnp.where(lane < 32, block(gp, q + 1, gz, 0), ends)
                if q > 0:
                    ends = jnp.where(lane >= 96, block(gp, q - 1, gz, 0), ends)
                whole.append(block(gp, q, gz, 0) + roll(ends, 64, 1))
            near, far = whole
            near2, far2 = [block(gp, q, gz, 1) for gz in range(2)]
            for y in range(2):
                high = jnp.where(lane < 64, roll(far, -32 * y, 1), 0.0)
                own = jnp.where(lane < 32, roll(near, -32 * (y + 1), 1), high)
                cells[2 * q + y, gp] = cells[2 * q + y, gp] + own
                high = jnp.where(lane < 64, roll(far2, 32 * (1 - y), 1), 0.0)
                k2[2 * q + y, 8 * gp : 8 * gp + 8, :] = jnp.where(lane < 32, roll(near2, -32 * y, 1), high)
            high = jnp.where(lane < 64, roll(far2, -32, 1), 0.0)
            beyond = jnp.where(lane < 32, roll(near2, -64, 1), high)
            goal = 0 if gp == 0 else 7
            for y in range(-1, 3):
                spot = 2 * q + y, 1 - gp
                cells[spot] = cells[spot] + jnp.where(sub == goal, roll(beyond, goal - y - 1, 0), 0.0)
    for y in range(n_y):
        for gp in range(2):
            r2[y, 8 * gp : 8 * gp + 8, :] = cells[y, gp]
    middle, rhs2 = Level(k2[...], 0.0625), r2[...]
    m2 = middle.weight * rhs2
    m2 = middle.sweep(m2, rhs2)
    rhs3 = halved(middle.resid(m2, rhs2), sums)
    bottom = Level(halved(k2[...], sums), 0.015625)
    m3 = bottom.weight * rhs3
    for _ in range(COARSE_SWEEPS - 1):
        m3 = bottom.sweep(m3, rhs3)
    m2 = m2 + doubled(m3, sums)
    for _ in range(SMOOTH):
        m2 = middle.sweep(m2, rhs2)

    shape = (128, 128)
    z = iota(shape, 1)
    z = jnp.where(z < 96, z, z - 128)
    spread = jnp.where(32 * t + (z >> 1) == iota(shape, 0), 1.0, 0.0).astype(F32)
    tall[...] = jnp.zeros_like(tall)
    tall[4 : 4 + n_y, 8:24, :] = dot(m2.reshape(16 * n_y, 128), spread).reshape(n_y, 16, 128)
    for j in range(8):
        cells = tall[4 * b + 2 * c + 1 + j]
        flat[64 * j : 64 * j + 32, :] = cells
        flat[64 * j + 32 : 64 * j + 64, :] = cells
    for i in range(14):
        e = pick(p, flat[pl.ds(5 + i, 16, stride=32), :], flat[pl.ds(13 + i, 16, stride=32), :])
        for r in (2 * i, 2 * i + 1):
            ua[r] = v21[r] + jnp.where(w1[r] > 0.0, e, 0.0)
    at = 6 - 4 * p
    rows = pl.ds(at, 20)
    near = k1[pl.ds(at, 21)]
    k = near[:20]
    fx[rows] = 0.125 * (k + near[1:])
    fy[rows] = 0.125 * (k + roll(k, -1, 1))
    fz[rows] = 0.125 * (k + roll(k, -1, 2))
    sweep(ua, ub, r1, fx, fy, fz, w1, at, 20, 20)
    sweep(ub, ua, r1, fx, fy, fz, w1, at, 20, 20)

    e = roll(ua[5:23], -4, 1)[:, :8].reshape(144, 128)
    flat[pl.ds(0, 144, stride=2), :] = e
    flat[pl.ds(1, 144, stride=2), :] = e
    shape = (128, 256)
    spread = jnp.where((iota(shape, 1) >> 1) == iota(shape, 0), 1.0, 0.0).astype(F32)
    e = dot(flat[0:288, :], spread).reshape(18, 16, 256)
    for k in range(18):
        for r in (2 * k + 3, 2 * k + 4):
            va[r] = jnp.where(weight[r] > 0.0, e[k], 0.0)
    rows = pl.ds(first, PLANES)
    near = kappa[pl.ds(first, PLANES + 1)]
    k = near[:PLANES]
    cx[rows] = 0.5 * (k + near[1:])
    cy[rows] = 0.5 * (k + roll(k, -1, 1))
    cz[rows] = 0.5 * (k + roll(k, -1, 2))
    sweep(va, vb, left, cx, cy, cz, weight, 5 - p, 33, 33)
    here, total = around(vb, cx, cy, cz, 5, 32)
    done = (1.0 - OMEGA) * here + weight[5:37] * (left[5:37] + total)
    va[0:32, 0:8, 0:128] = v2[...] + roll(done[:, :, :128], -4, 1)[:, :8]
    keep[...] = va[pl.ds(16 * c, 16), 0:8, 0:128]
    give[...] = va[pl.ds(16 - 16 * c, 16), 0:8, 0:128]


def join_kernel(mine, other, out, done):
    _, c, _, _ = place()
    copies = []
    for i, (part, at) in enumerate(((mine, 8 * c), (other, 8 - 8 * c))):
        copies.append(pltpu.make_async_copy(part, out.at[:, pl.ds(pl.multiple_of(at, 8), 8), :], done.at[i]))
        copies[i].start()
    for copy in copies:
        copy.wait()


def call(kernel, name, outs, scratch, *args):
    where = pltpu.HBM if name == "message" else pltpu.VMEM
    last = 1 if name in ("down", "join") else 0
    if name == "message":
        args = [pltpu.with_memory_space_constraint(a, pltpu.HBM) for a in args]
    return pl.pallas_call(
        kernel,
        name=name,
        out_shape=[jax.ShapeDtypeStruct(s, F32) for s in outs],
        in_specs=[pl.BlockSpec(memory_space=where)] * len(args),
        out_specs=[pl.BlockSpec(memory_space=pltpu.VMEM)] * (len(outs) - last) + [pl.BlockSpec(memory_space=pltpu.HBM)] * last,
        scratch_shapes=[
            pltpu.SemaphoreType.DMA((s,)) if isinstance(s, int) else pltpu.VMEM(*s) for s in scratch
        ],
        compiler_params=pltpu.CompilerParams(vmem_limit_bytes=16 * 1024 * 1024),
        cost_estimate=pl.CostEstimate(flops=10**7, bytes_accessed=4 * 10**6, transcendentals=0),
    )(*args)


def paired(chi, inducing, record_dest, record_cell, record_value):
    n_gy = lax.axis_size("gy")
    everyone = ("gx", "gy", "gz")
    window = (ROWS, 16, 256)
    big = [(window, F32)]
    chi, inducing, message, spill = call(
        message_kernel,
        "message",
        [(16, 16, 128), (3, 16, 16, 128), (120, 128), (48, 128)],
        [((8, 128), jnp.int32)] * 2 + [((8, 128), F32), 11],
        chi,
        inducing,
        record_dest.reshape(8, 128),
        record_cell.reshape(8, 128),
        record_value.reshape(8, 128),
    )
    got = lax.ppermute(message, "gz", [(0, 1), (1, 0)])
    spread = [((256, 1024), BF16), ((512, 1024), BF16)]
    source, total = call(
        source_kernel,
        "source",
        [(18, 24, 128), (256, 256)],
        spread,
        chi,
        inducing,
        message,
    )
    own, sent = call(
        deposit_kernel,
        "deposit",
        [(39, 16, 128)] * 2,
        [((39, 24, 128), F32)] + spread,
        source,
        spill,
        chi,
        total,
        got,
    )
    swap = [(0, 1), (1, 0), (2, 3), (3, 2)]
    got = lax.ppermute(sent, "gx", swap)
    held = [(ROWS, 16, 128), (ROWS, 16, 128), (12, 16, 128)]
    *fields, message, strip, corner = call(
        pair_kernel, "pair", held + [(10, 16, 128), (PLANES + 6, 8, 128), (6, 8, 128)], [], own, got
    )
    cross = [(0, 2), (2, 0), (1, 3), (3, 1)]
    across = lax.ppermute(message, "gx", cross)
    turns, corners = [], []
    for p in range(2):
        for b in range(n_gy - 1):
            low, high = (2 * p + 1) * n_gy + b, 2 * p * n_gy + b + 1
            turns += [(low, high), (high, low)]
            high = 2 * (1 - p) * n_gy + b + 1
            corners += [(low, high), (high, low)]
    for low, high in ((0, 2 * n_gy), (2 * n_gy - 1, 4 * n_gy - 1)):
        turns += [(low, high), (high, low)]
        corners += [(low, high), (high, low)]
    strip = lax.ppermute(strip, ("gx", "gy"), turns)
    corner = lax.ppermute(corner, ("gx", "gy"), corners)
    *fine, along, beside, message, parts = call(
        functools.partial(down_kernel, n_gy),
        "down",
        [window] * 3 + [(32, 8, 128), (18, 8, 128), (18, 8, 128), (6, 8, 128), (4 * n_gy, 16, 128)],
        big * 7 + [((640, 128), F32), ((48, 128), F32), ((12, 16, 128), F32)]
        + [((4 * n_gy, 16, 128), F32), 1],
        *fields,
        across,
        strip,
        corner,
    )
    n = 2 * n_gy
    groups = [[(2 * p + c) * n + i for p in range(2) for i in range(n)] for c in range(2)]
    blocks = lax.all_to_all(
        parts, ("gx", "gy", "gz"), split_axis=0, concat_axis=0, tiled=True, axis_index_groups=groups
    )
    more = lax.ppermute(blocks, "gx", swap)
    across = lax.ppermute(message, "gx", cross)
    got = lax.ppermute(jnp.concatenate([along, across]), ("gx", "gy"), turns)
    other = lax.ppermute(jnp.concatenate([beside, across]), "gx", swap)
    window1 = (28, 16, 128)
    big1 = [(window1, F32)]
    coarse = call(
        functools.partial(middle_kernel, n_gy),
        "middle",
        [window1] * 4,
        big1 * 5,
        beside,
        across,
        jnp.concatenate([got, other]),
    )
    level2 = ((4 * n_gy, 16, 128), F32)
    keep, give = call(
        functools.partial(up_kernel, n_gy),
        "up",
        [(16, 8, 128)] * 2,
        [level2] * 2
        + [((4 * n_gy + 8, 32, 128), F32), ((512, 128), F32), ((64 * n_gy, 128), F32)]
        + big1 * 5
        + big * 5,
        blocks,
        more,
        *coarse,
        *fine,
    )
    got = lax.ppermute(give, "gx", swap)
    (out,) = call(join_kernel, "join", [(16, 16, 128)], [2], keep, got)
    return out


def solution(mesh):
    placed = (
        P("gx", "gy", "gz"),
        P(None, "gx", "gy", "gz"),
        P("gx", "gy", "gz", None, None),
        P("gx", "gy", "gz", None),
        P("gx", "gy", "gz", None),
    )
    small = mesh.shape["gx"] == 4 and mesh.shape["gz"] == 2 and mesh.shape["gy"] <= 4
    return jax.shard_map(
        paired if small else general,
        mesh=mesh,
        in_specs=placed,
        out_specs=P("gx", "gy", "gz"),
        check_vma=False,
    )
```

```python
import functools

import jax
import jax.numpy as jnp
from jax import lax
from jax.experimental import pallas as pl
from jax.experimental.pallas import tpu as pltpu
from jax.sharding import PartitionSpec as P

SMOOTH = 2
LEVELS = 3
COARSE_SWEEPS = 8
CAP = 640


OMEGA = 0.8


def padded_2(cells, sides, width):
    for axis, dim in sides:
        count = lax.axis_size(axis)
        ends = count - 1
        head = lax.slice_in_dim(cells, 0, width, axis=dim)
        tail = lax.slice_in_dim(cells, cells.shape[dim] - width, cells.shape[dim], axis=dim)
        cells = jnp.concatenate(
            [
                lax.ppermute(tail, axis, [(i, (i + 1) % count) for i in range(ends)]),
                cells,
                lax.ppermute(head, axis, [((i + 1) % count, i) for i in range(ends)]),
            ],
            axis=dim,
        )
    return cells


def restrict(x):
    s = x.shape
    return x.reshape(s[0] // 2, 2, s[1] // 2, 2, s[2] // 2, 2).mean(axis=(1, 3, 5))


def prolong(e):
    return jnp.repeat(jnp.repeat(jnp.repeat(e, 2, 0), 2, 1), 2, 2)


def neighbours(padded):
    return [
        padded[2:, 1:-1, 1:-1],
        padded[:-2, 1:-1, 1:-1],
        padded[1:-1, 2:, 1:-1],
        padded[1:-1, :-2, 1:-1],
        padded[1:-1, 1:-1, 2:],
        padded[1:-1, 1:-1, :-2],
    ]


def face_pad(x):
    return padded_2(x, (("gx", 0), ("gy", 1), ("gz", 2)), 1)


def coefficients(kappa):
    return [0.5 * (kappa + other) for other in neighbours(face_pad(kappa))]


def apply_op(v, coefs, scale):
    total = jnp.zeros_like(v)
    for coef, other in zip(coefs, neighbours(face_pad(v))):
        total = total + coef * (v - other)
    return scale * total


def cycle(level, rhs, kappa):
    scale = 0.25**level
    coefs = coefficients(kappa)
    diag = scale * (coefs[0] + coefs[1] + coefs[2] + coefs[3] + coefs[4] + coefs[5])
    v = OMEGA * rhs / diag
    for sweep in range((COARSE_SWEEPS if level == LEVELS else SMOOTH) - 1):
        v = v + OMEGA * (rhs - apply_op(v, coefs, scale)) / diag
    if level == LEVELS:
        return v
    resid = rhs - apply_op(v, coefs, scale)
    corr = cycle(level + 1, restrict(resid), restrict(kappa))
    v = v + prolong(corr)
    for sweep in range(SMOOTH):
        v = v + OMEGA * (rhs - apply_op(v, coefs, scale)) / diag
    return v


def general(chi, inducing, record_dest, record_cell, record_value):
    n_gz = lax.axis_size("gz")
    dest = record_dest[0, 0, 0, :, 0]
    cells = record_cell[0, 0, 0]
    values = record_value[0, 0, 0]
    onehot = (dest[:, None] == jnp.arange(n_gz, dtype=jnp.int32)[None, :]).astype(jnp.int32)
    ranks = jnp.sum((jnp.cumsum(onehot, axis=0) - 1) * onehot, axis=1)
    outgoing = jnp.zeros((n_gz, 2, CAP), jnp.float32)
    outgoing = outgoing.at[dest, 0, ranks].set(values)
    outgoing = outgoing.at[dest, 1, ranks].set(cells.astype(jnp.float32))
    incoming = lax.all_to_all(outgoing, "gz", split_axis=0, concat_axis=0, tiled=True)
    in_values = incoming[:, 0].reshape(-1)
    in_cells = incoming[:, 1].reshape(-1).astype(jnp.int32)
    moment_x = face_pad(chi * inducing[0])
    moment_y = face_pad(chi * inducing[1])
    moment_z = face_pad(chi * inducing[2])
    source = -0.5 * (
        moment_x[2:, 1:-1, 1:-1]
        - moment_x[:-2, 1:-1, 1:-1]
        + (moment_y[1:-1, 2:, 1:-1] - moment_y[1:-1, :-2, 1:-1])
        + (moment_z[1:-1, 1:-1, 2:] - moment_z[1:-1, 1:-1, :-2])
    )
    rhs = source.reshape(-1).at[in_cells].add(in_values).reshape(source.shape)
    return cycle(0, rhs, 1.0 + chi)


F32 = jnp.float32
BF16 = jnp.bfloat16
ROWS = 42
PLANES = 36
SIZE = 36


def iota(shape, dim):
    return lax.broadcasted_iota(jnp.int32, shape, dim)


def roll(x, shift, axis):
    shift = shift % x.shape[axis]
    return pltpu.roll(x, shift, axis) if shift else x


def pick(flag, first, second):
    return jnp.where(jnp.full(first.shape, flag, jnp.int32) == 0, first, second)


def dot(a, b):
    total = 0.0
    for _ in range(3):
        part = a.astype(BF16)
        total = total + jnp.dot(part, b.astype(BF16), preferred_element_type=F32)
        a = a - part.astype(F32)
    return total


def halving(lanes):
    shape = (lanes, 128)
    return jnp.where((iota(shape, 0) >> 1) == iota(shape, 1), 0.125, 0.0).astype(F32)


def place():
    gx, gy, gz = lax.axis_index("gx"), lax.axis_index("gy"), lax.axis_index("gz")
    return gx >> 1, gx & 1, gy, gz


def stretch(x):
    return roll(jnp.concatenate([x, jnp.zeros((8, x.shape[1]), F32)], 0), 4, 0)


def message_kernel(*refs):
    given, (chi, inducing, message, spill), (dest, cell, value, done) = refs[:5], refs[5:9], refs[9:]
    _, _, _, t = place()
    held = (chi, inducing, dest, cell, value)
    pairs = [(given[0].at[8 * i : 8 * i + 8], held[0].at[8 * i : 8 * i + 8]) for i in range(2)]
    pairs += [(given[1].at[d, 8 * i : 8 * i + 8], held[1].at[d, 8 * i : 8 * i + 8]) for i in range(2) for d in range(3)]
    pairs += list(zip(given[2:], held[2:]))
    copies = [pltpu.make_async_copy(a, b, done.at[i]) for i, (a, b) in enumerate(pairs)]
    for i in (0, 2, 3, 4, 1, 5, 6, 7, 8, 9, 10):
        copies[i].start()
    lane = iota((16, 128), 1)
    turn = 11 - 10 * t
    packs = [[jnp.zeros((16, 128), F32)] * 2 for _ in range(4)]
    for x in range(16):
        if x % 8 == 0:
            copies[x // 8].wait()
            for d in range(3):
                copies[2 + 3 * (x // 8) + d].wait()
        by = 16 * (x % 8)
        wanted = (lane >= by + t) & (lane < by + t + 11)
        near = jnp.where(wanted, pltpu.roll(chi[x], (turn + by) & 127, 1), 0.0)
        parts = [1.0 + near]
        parts += [near * pltpu.roll(inducing[d, x], (turn + by) & 127, 1) for d in range(3)]
        for pack, part in zip(packs, parts):
            pack[x // 8] = jnp.where(wanted, part, pack[x // 8])
    k, mx, my, mz = [jnp.concatenate(pack, 1) for pack in packs]
    lane = iota((16, 256), 1)
    dx = jnp.where(lane < 240, roll(mx, -16, 1), 0.0) - jnp.where(lane >= 16, roll(mx, 16, 1), 0.0)
    y = stretch(my)
    dz = roll(mz, -1, 1) - roll(mz, 1, 1)
    body = -0.5 * (stretch(dx + dz) + (roll(y, -1, 0) - roll(y, 1, 0)))
    lane = iota((24, 128), 1)
    before, after = stretch(mx[:, :128]), stretch(mx[:, 128:])
    ends = 0.5 * (jnp.where((lane >= 16) & (lane < 32), roll(after, 32, 1), 0.0) - jnp.where(lane < 16, before, 0.0))

    def eleven(tile):
        tile = pick(t, roll(tile, -1, 1), tile)
        return jnp.where((iota(tile.shape, 1) & 15) < 11, tile, 0.0)

    slot = iota((24, 256), 1) & 15
    own = pick(t, jnp.where(slot == 11, body, 0.0), jnp.where(slot == 0, body, 0.0))
    own = pick(t, roll(own, -10, 1), roll(own, 9, 1))
    body = eleven(body)
    k = pick(t, k, roll(k, -1, 1))
    for i in range(2):
        cut = slice(128 * i, 128 * (i + 1))
        spill[24 * i : 24 * (i + 1)] = own[:, cut]
        message[24 * i : 24 * (i + 1)] = body[:, cut]
        message[72 + 16 * i : 88 + 16 * i] = k[:, cut]
    message[48:72] = eleven(ends)
    for copy in copies[8:]:
        copy.wait()
    message[104:112] = value[...]
    message[112:120] = (dest[...] * 32768 + cell[...]).astype(F32)


def spread_records(records, t, at_row, at_column):
    row, slot = iota((256, 128), 0), iota((16, 128), 0)
    z_of = iota((128, 128), 0)
    at_column[432:512] = jnp.zeros((80, 1024), BF16)
    for j in range(8):
        value = records[104 + j : 105 + j, :]
        code = records[112 + j : 113 + j, :].astype(jnp.int32)
        cells = code & 32767
        z = ((code >> 15) - t) * 128 + (cells & 127)
        far = z - 128 + 138 * t
        far = jnp.where((far >= 0) & (far < 10), far + 1 - t, 16)
        cut = slice(128 * j, 128 * (j + 1))
        at_row[:, cut] = jnp.where(row == (cells >> 7), 1.0, 0.0).astype(BF16)
        here, there = z_of == z, slot == far
        for i in range(3):
            short = value.astype(BF16).astype(F32)
            at_column[128 * i : 128 * (i + 1), cut] = jnp.where(here, short, 0.0).astype(BF16)
            at_column[384 + 16 * i : 400 + 16 * i, cut] = jnp.where(there, short, 0.0).astype(BF16)
            value = value - short
    total = lax.dot_general(
        at_row[...], at_column[...], (((1,), (1,)), ((), ())), preferred_element_type=F32
    )
    near = (total[:, 256:384] + total[:, 128:256]) + total[:, 0:128]
    return jnp.concatenate([near, total[:, 384:512]], 1)


def source_kernel(chi, inducing, records, source, total, at_row, at_column):
    _, _, _, t = place()
    lane = iota((16, 128), 1)
    zero = jnp.zeros((16, 128), F32)
    mx = [zero, zero] + [chi[x] * inducing[0, x] for x in range(16)] + [zero, zero]
    for i in range(18):
        flat = mx[i + 2] - mx[i]
        if 1 <= i <= 16:
            my, mz = chi[i - 1] * inducing[1, i - 1], chi[i - 1] * inducing[2, i - 1]
            flat = flat + (jnp.where(lane == 127, 0.0, roll(mz, -1, 1)) - jnp.where(lane == 0, 0.0, roll(mz, 1, 1)))
            y = stretch(my)
            source[i] = -0.5 * (stretch(flat) + (roll(y, -1, 0) - roll(y, 1, 0)))
        else:
            source[i] = -0.5 * stretch(flat)
    total[...] = spread_records(records, t, at_row, at_column)


def deposit_kernel(source, spill, chi, mine, other, own, sent, all_, at_row, at_column):
    _, c, _, t = place()
    total = mine[...] + spread_records(other, t, at_row, at_column)
    lane = iota((24, 128), 1)
    halo = [other[24 * i : 24 * (i + 1)] + spill[24 * i : 24 * (i + 1)] for i in range(2)]
    for i in range(18):
        x = i - 1
        if 0 <= x < 16:
            got = total[16 * x : 16 * x + 16, 128:]
            got = stretch((roll(got, -32, 1) + roll(got, -16, 1)) + got)
            halo[x // 8] = halo[x // 8] + roll(jnp.where(lane < 16, got, 0.0), 16 * (x % 8), 1)
            add = stretch(total[16 * x : 16 * x + 16, :128])
            tile, by = other[24 * (x // 8) : 24 * (x // 8) + 24], 16 * (x % 8)
        else:
            add = jnp.zeros((24, 128), F32)
            tile, by = other[48:72], 0 if i == 0 else 16
        near = pick(t, roll(tile, 127 - by, 1), roll(tile, -10 - by, 1))
        all_[i] = source[i] + add + jnp.where(lane == 127 - 127 * t, near, 0.0)
    for i in range(16):
        all_[18 + i] = stretch(1.0 + chi[i])
    for i in range(2):
        all_[34 + i] = halo[i]
        all_[37 + i] = stretch(other[72 + 16 * i : 88 + 16 * i])
    all_[36] = other[48:72]
    keep, give = pl.multiple_of(8 * c, 8), pl.multiple_of(8 - 8 * c, 8)
    own[...] = all_[:, pl.ds(keep, 16), :]
    sent[...] = all_[:, pl.ds(give, 16), :]


def pair_kernel(own, other, source, kappa, halo, message, strip, corner):
    p, c, _, _ = place()
    source[...] = jnp.zeros_like(source)
    kappa[...] = jnp.zeros_like(kappa)
    source[pl.ds(4 + 16 * c, 18)] = own[0:18]
    low = 4 + 16 * (1 - c)
    source[pl.ds(low, 18)] = source[pl.ds(low, 18)] + other[0:18]
    kappa[pl.ds(5 + 16 * c, 16)] = own[18:34]
    kappa[pl.ds(low + 1, 16)] = other[18:34]
    lane = iota((16, 128), 1)
    tiles = [jnp.zeros((16, 128), F32)] * 12
    for side in range(2):
        for start, at in ((34, 0), (37, 6)):
            for i in range(2):
                cells = roll(pick(c ^ side, own[start + i], other[start + i]), 80, 1)
                n = at + 2 * side + i
                tiles[n] = tiles[n] + jnp.where(lane >= 80, cells, 0.0)
                tiles[n + 1] = tiles[n + 1] + jnp.where(lane < 80, cells, 0.0)
        ends = roll(pick(c ^ side, own[36], other[36]), 64, 1)
        n = 2 * side
        tiles[n] = tiles[n] + jnp.where((lane >= 64) & (lane < 80), ends, 0.0)
        tiles[n + 2] = tiles[n + 2] + jnp.where((lane >= 80) & (lane < 96), ends, 0.0)
    for i in range(12):
        halo[i] = tiles[i]
    message[0:4] = source[pl.ds(34 - 30 * p, 4)]
    message[4:8] = kappa[pl.ds(33 - 28 * p, 4)]
    for i in range(2):
        low = jnp.where(lane < 64, roll(tiles[6 * i], -64, 1), roll(tiles[6 * i + 1], 64, 1))
        message[8 + i] = jnp.where(lane < 80, pick(p, roll(tiles[6 * i + 4], -16, 1), low), 0.0)

    def cut(s, k):
        s = pick(c, roll(s, -3, 1)[:, :8], roll(s, -9, 1)[:, :8])
        k = pick(c, k[:, :8], roll(k, -4, 1)[:, :8])
        return jnp.where(iota(s.shape, 1) < 4, s, k)

    first = 5 - 4 * p
    strip[0:PLANES] = cut(source[pl.ds(first, PLANES)], kappa[pl.ds(first, PLANES)])
    strip[PLANES:] = cut(halo[0:6], halo[6:12])
    first = 33 - 29 * p
    corner[0:5] = cut(source[pl.ds(first, 5)], kappa[pl.ds(first, 5)])
    corner[5:6] = cut(message[8:9], message[9:10])


def chunked(count, body, size=4):
    def step(i, _):
        body(i * size)
        return 0

    lax.fori_loop(0, count // size, step, 0)


def faces(kap, cx, cy, cz, weight, diag, first, count, scale, closed, n):
    shape = (n,) + kap.shape[1:]
    last_y = iota(shape, 1) == shape[1] - 1
    first_y = iota(shape, 1) == 0
    last_z = iota(shape, 2) == shape[2] - 1
    first_z = iota(shape, 2) == 0

    def body(i):
        r = first + i
        near = kap[pl.ds(r - 1, n + 2)]
        k, up, down = near[1 : n + 1], near[2:], near[:n]
        yu, yd, zu, zd = roll(k, -1, 1), roll(k, 1, 1), roll(k, -1, 2), roll(k, 1, 2)
        if closed:
            yu, yd = jnp.where(last_y, 0.0, yu), jnp.where(first_y, 0.0, yd)
            zu, zd = jnp.where(last_z, 0.0, zu), jnp.where(first_z, 0.0, zd)
        half = 0.5 * scale
        total = half * (6.0 * k + ((up + down) + (yu + yd) + (zu + zd)))
        fy, fz = half * (k + yu), half * (k + zu)
        if closed:
            fy, fz = jnp.where(last_y, 0.0, fy), jnp.where(last_z, 0.0, fz)
        cx[pl.ds(r, n)] = half * (k + up)
        cy[pl.ds(r, n)] = fy
        cz[pl.ds(r, n)] = fz
        diag[pl.ds(r, n)] = total
        weight[pl.ds(r, n)] = jnp.where(k > 0.0, OMEGA / total, 0.0)

    chunked(count, body, n)


def around(v, cx, cy, cz, r, n):
    near, fx = v[pl.ds(r - 1, n + 2)], cx[pl.ds(r - 1, n + 1)]
    here, fy, fz = near[1 : n + 1], cy[pl.ds(r, n)], cz[pl.ds(r, n)]
    return here, (
        (fx[1:] * near[2:] + fx[:n] * near[:n])
        + (fy * roll(here, -1, 1) + roll(fy * here, 1, 1))
        + (fz * roll(here, -1, 2) + roll(fz * here, 1, 2))
    )


def sweep(v, out, rhs, cx, cy, cz, weight, first, count, n):
    def body(i):
        r = first + i
        here, total = around(v, cx, cy, cz, r, n)
        out[pl.ds(r, n)] = (1.0 - OMEGA) * here + weight[pl.ds(r, n)] * (rhs[pl.ds(r, n)] + total)

    chunked(count, body, n)


def resid(v, rhs, cx, cy, cz, diag, r, n):
    here, total = around(v, cx, cy, cz, r, n)
    return rhs[pl.ds(r, n)] + total - diag[pl.ds(r, n)] * here


def pair_sums(x):
    x = x.reshape((x.shape[0] // 2, 2) + x.shape[1:])
    return x[:, 0] + x[:, 1]


def down_kernel(
    n_gy, source_in, kappa_in, halo_in, across, along_in, corner, left, kappa, weight, v, along, beside, message, parts,
    rhs, cx, cy, cz, diag, v1, v2, sums, flat, halo, packs, done,
):
    p, c, b, t = place()
    first = 5 - 4 * p
    edge = jnp.where(c == 0, b == 0, b == n_gy - 1).astype(jnp.int32)
    kappa[0:5] = jnp.zeros((5, 16, 256), F32)
    kappa[37:42] = jnp.zeros((5, 16, 256), F32)
    for ref in (cx, weight, v1, v2):
        for r in (0, 2, 3, 4, 37, 38, 39, 41):
            ref[r] = jnp.zeros((16, 256), F32)

    sub = iota((1, 8, 128), 1)
    sides = [jnp.full((1, 8, 128), (1 - edge) * side, jnp.int32) for side in (1 - c, c)]

    def merge(got):
        s, k = pltpu.roll(got, 1 + 2 * c, 1), pltpu.roll(got, 4 - 4 * c, 1)
        s = [jnp.where((sub >= at) & (sub < at + 4) & (side > 0), s, 0.0) for at, side in zip((1, 3), sides)]
        k = [jnp.where((sub >= at) & (sub < at + 4) & (side > 0), k, 0.0) for at, side in zip((0, 4), sides)]
        return jnp.concatenate(s, 1), jnp.concatenate(k, 1)

    def packed(got):
        lane = iota(got.shape, 1)
        wide, zero = roll(got, 64, 1), jnp.zeros_like(got)
        return (
            pick(p, zero, roll(got, 16, 1)),
            pick(p, jnp.where(lane >= 64, wide, 0.0), zero),
            pick(p, jnp.where(lane < 16, wide, 0.0), zero),
        )

    s, k = merge(along_in[PLANES:])
    s2, k2 = merge(corner[...])
    halo[0:6] = halo_in[0:6] + s
    halo[6:12] = halo_in[6:12] + k
    for n, more in enumerate((s2, k2)):
        for i, part in zip((0, 4, 5), packed(across[8 + n] + more[5])):
            halo[6 * n + i] = halo[6 * n + i] + part
    lane = iota((16, 128), 1)
    s_lanes = pick(t, (lane < 10).astype(jnp.int32), (lane >= 118).astype(jnp.int32)) > 0
    k_lanes = pick(t, (lane < 11).astype(jnp.int32), (lane >= 117).astype(jnp.int32)) > 0

    def enter(i):
        r = first + i
        rows = pl.ds(r, SIZE)
        s, k = merge(along_in[pl.ds(i, SIZE)])
        far_s, far_k = [], []
        for j in range(SIZE):
            tile, by = (r + j) >> 3, 16 * ((r + j) & 7)
            far_s.append(jnp.where(s_lanes, pltpu.roll(halo[tile], (127 - by - 9 * t) & 127, 1), 0.0)[None])
            far_k.append(jnp.where(k_lanes, pltpu.roll(halo[6 + tile], (128 - by - 11 * t) & 127, 1), 0.0)[None])
        rhs[rows] = jnp.concatenate([source_in[rows] + s, jnp.concatenate(far_s, 0)], 2)
        kappa[rows] = jnp.concatenate([kappa_in[rows] + k, jnp.concatenate(far_k, 0)], 2)

    chunked(PLANES, enter, SIZE)
    at = pl.ds(36 - 34 * p, 4)
    rhs[at, :, 0:128] = rhs[at, :, 0:128] + across[0:4]
    at = pl.ds(37 - 36 * p, 4)
    kappa[at, :, 0:128] = kappa[at, :, 0:128] + across[4:8]
    at = pl.ds(36 - 35 * p, 5)
    rhs[at, :, 0:128] = rhs[at, :, 0:128] + s2[0:5]
    kappa[at, :, 0:128] = kappa[at, :, 0:128] + k2[0:5]
    faces(kappa, cx, cy, cz, weight, diag, first, PLANES, 1.0, False, PLANES)

    def coarse(fine):
        two = pair_sums(fine)
        n = 16 * two.shape[0]
        two = two.reshape(n, 256)
        halves = []
        for i in range(2):
            at = 320 * i
            sums[at : at + n] = two[:, 128 * i : 128 * (i + 1)]
            halves.append(sums[pl.ds(at, n // 2, stride=2), :] + sums[pl.ds(at + 1, n // 2, stride=2), :])
        return dot(jnp.concatenate(halves, 1), halving(256)).reshape(n // 16, 8, 128)

    rows = pl.ds(first, PLANES)
    v1[rows] = weight[rows] * rhs[rows]
    sweep(v1, v2, rhs, cx, cy, cz, weight, 5 - 2 * p, 34, 34)
    left[pl.ds(5 - p, 33)] = resid(v2, rhs, cx, cy, cz, diag, 5 - p, 33)
    k1 = coarse(kappa[1:41])
    r1 = coarse(left[5:37])
    edge = jnp.zeros((2, 8, 128), F32)
    at = iota(r1.shape, 1)
    part = jnp.concatenate([edge, jnp.where((at >= 2) & (at < 6), r1, 0.0), edge], 0)
    level = Level(k1, 0.25, closed=False)
    u1 = level.weight * part
    u2 = level.sweep(u1, part)
    sub, lane = iota((8, 128), 0), iota((8, 128), 1)

    def means(fine):
        n = 2 * fine.shape[0]
        sums[0 : 2 * n] = pair_sums(fine).reshape(2 * n, 128)
        return dot(sums[pl.ds(0, n, stride=2), :] + sums[pl.ds(1, n, stride=2), :], halving(128))

    flat[0:40, :] = means(level.resid(u2, part))
    tile = jnp.zeros((8, 128), F32)
    for y in range(4):
        tile = tile + roll(jnp.where(lane < 32, flat[pl.ds(4 + y, 8, stride=4), :], 0.0), 32 * y, 1)
    beyond = jnp.where((sub < 4) & (lane < 32), pick(p, flat[36:44, :], flat[0:8, :]), 0.0)
    second = roll(beyond, 64, 1)
    flat[0:40, :] = means(k1)
    for y in range(2):
        second = second + roll(jnp.where(lane < 32, flat[pl.ds(5 + y, 8, stride=4), :], 0.0), 32 * y, 1)
    for d in range(parts.shape[0]):
        packs[d, 0:8] = tile
        packs[d, 8:16] = second
    sending = pltpu.make_async_copy(packs, parts, done.at[0])
    sending.start()
    v[...] = roll(v2[5:37, :, :128], -4, 1)[:, :8]
    k = k1[2:18]
    v1c = level.weight[2:18] * r1
    tiles = jnp.where(iota(r1.shape, 1) < 4, roll(r1, -2, 1), roll(k, 2, 1))
    along[0:16] = tiles
    beside[0:16] = tiles
    for i in range(2):
        far, near = jnp.zeros((8, 128), F32), jnp.zeros((8, 128), F32)
        for j in range(8):
            cells = v1c[8 * i + j]
            last, start = roll(cells, j - 5, 0), roll(cells, j - 2, 0)
            far = jnp.where(sub == j, pick(c, last, start), far)
            near = jnp.where(sub == j, pick(c, start, last), near)
        along[16 + i] = far
        beside[16 + i] = near
    message[0:4] = along[pl.ds(12 - 12 * p, 4)]
    message[4] = roll(pick(p, v1c[12], v1c[3]), -2, 0)
    message[5] = roll(pick(p, v1c[15], v1c[0]), -2, 0)
    sending.wait()


def middle_kernel(
    n_gy, mine, across, both, kappa, r1, k1, weight, v2, cx0, cy0, cz0, cx, cy, cz, diag, v1
):
    p, c, b, t = place()
    edge = jnp.where(c == 0, b == 0, b == n_gy - 1).astype(jnp.int32)
    for ref in (r1, k1, cx, weight, v1, v2):
        ref[...] = jnp.zeros_like(ref)
    sub = iota((8, 128), 0)
    zero = jnp.zeros((8, 128), F32)
    middle = (sub >= 2) & (sub < 6)

    def around_mine(at):
        s, g = both[24 + at], pick(edge, both[at], zero)
        return pick(c, g, s), pick(c, s, g)

    def joined(low, o, high):
        first = jnp.where(middle, roll(low, 2, 0), jnp.where(sub >= 6, roll(o, 6, 0), 0.0))
        return first, jnp.where(sub < 2, roll(o, -2, 0), jnp.where(middle, roll(high, 2, 0), 0.0))

    for j in range(20):
        row = 6 + j if j < 16 else 6 + j - 20 * p
        o = mine[j] if j < 16 else across[j - 16]
        low, high = around_mine(j if j < 16 else j + 2)
        r1[row, 0:8], r1[row, 8:16] = joined(low, o, high)
        k1[row, 0:8], k1[row, 8:16] = joined(*[roll(tile, 4, 0) for tile in (low, o, high)])
    first = 6 - 4 * p
    faces(k1, cx, cy, cz, weight, diag, first, 20, 0.25, False, 20)
    rows = pl.ds(first, 20)
    v1[rows] = weight[rows] * r1[rows]
    ends = []
    for i in range(2):
        low, high = around_mine(16 + i)
        ends += [(6 + 8 * i + j, roll(low, 2 - j, 0), roll(high, 5 - j, 0)) for j in range(8)]
    low, high = around_mine(23)
    ends.append((22 - 17 * p, roll(low, 2, 0), roll(high, 2, 0)))
    for r, low, high in ends:
        v1[r, 0:8] = jnp.where(sub == 2, low, v1[r, 0:8])
        v1[r, 8:16] = jnp.where(sub == 5, high, v1[r, 8:16])
    low, high = around_mine(22)
    r = 25 - 23 * p
    v1[r, 0:8], v1[r, 8:16] = joined(low, across[4], high)
    sweep(v1, v2, r1, cx, cy, cz, weight, first, 20, 20)
    for r in (0, 3, 4, 37, 38):
        cx0[r] = jnp.zeros((16, 256), F32)
    first = 5 - 4 * p
    rows = pl.ds(first, PLANES)
    near = kappa[pl.ds(first, PLANES + 1)]
    k = near[:PLANES]
    cx0[rows] = 0.5 * (k + near[1:])
    cy0[rows] = 0.5 * (k + roll(k, -1, 1))
    cz0[rows] = 0.5 * (k + roll(k, -1, 2))


def shift(x, by, axis):
    if axis == 0:
        zero = jnp.zeros((1,) + x.shape[1:], x.dtype)
        return jnp.concatenate([x[1:], zero] if by > 0 else [zero, x[:-1]], 0)
    return roll(x, -by, axis)


SIDES = [(axis, by) for axis in range(3) for by in (1, -1)]


class Level:
    def __init__(self, kappa, scale, closed=True):
        half = 0.5 * scale
        at = iota(kappa.shape, 1)
        ends = {1: at == kappa.shape[1] - 1, -1: at == 0}
        near = [shift(kappa, by, axis) for axis, by in SIDES]
        if closed:
            near[2:4] = [jnp.where(ends[by], 0.0, k) for by, k in zip((1, -1), near[2:4])]
        self.diag = half * (6.0 * kappa + (near[0] + near[1]) + (near[2] + near[3]) + (near[4] + near[5]))
        self.faces = [half * (kappa + other) for other in near]
        if closed:
            self.faces[2:4] = [jnp.where(ends[by], 0.0, f) for by, f in zip((1, -1), self.faces[2:4])]
        inside = kappa > 0.0
        self.weight = jnp.where(inside, OMEGA / jnp.where(inside, self.diag, 1.0), 0.0)

    def around(self, v):
        terms = [f * shift(v, by, axis) for f, (axis, by) in zip(self.faces, SIDES)]
        return (terms[0] + terms[1]) + (terms[2] + terms[3]) + (terms[4] + terms[5])

    def sweep(self, v, rhs):
        return (1.0 - OMEGA) * v + self.weight * (rhs + self.around(v))

    def resid(self, v, rhs):
        return rhs + self.around(v) - self.diag * v


def halved(x, scratch):
    nx, ny = x.shape[0] // 2, x.shape[1] // 2
    pairs = x.reshape(nx, 2, 2 * ny, 128)
    scratch[0 : 2 * nx * ny, :] = (pairs[:, 0] + pairs[:, 1]).reshape(2 * nx * ny, 128)
    return halved_yz(scratch, nx, ny)


def halved_yz(scratch, nx, ny):
    halves = scratch[pl.ds(0, nx * ny, stride=2), :] + scratch[pl.ds(1, nx * ny, stride=2), :]
    return dot(halves, halving(128)).reshape(nx, ny, 128)


def doubling():
    shape = (128, 128)
    return jnp.where((iota(shape, 1) >> 1) == iota(shape, 0), 1.0, 0.0).astype(F32)


def doubled_yz(e, scratch):
    nx, ny, _ = e.shape
    wide = dot(e.reshape(nx * ny, 128), doubling())
    scratch[pl.ds(0, nx * ny, stride=2), :] = wide
    scratch[pl.ds(1, nx * ny, stride=2), :] = wide
    return scratch[0 : 2 * nx * ny, :].reshape(nx, 2 * ny, 128)


def doubled(e, scratch):
    e = doubled_yz(e, scratch)
    nx, ny, _ = e.shape
    return jnp.broadcast_to(e[:, None], (nx, 2, ny, 128)).reshape(2 * nx, ny, 128)


def up_kernel(
    n_gy, blocks, more, r1, k1, w1, v21, cx, cy, cz, left, weight, v2, keep, give,
    r2, k2, tall, flat, sums, fx, fy, fz, ua, ub, va, vb,
):
    p, c, b, t = place()
    first = 5 - 4 * p
    n_y = 4 * n_gy
    for r in (3, 4, 37, 38):
        vb[r] = jnp.zeros((16, 256), F32)
    for ref in (fx, ub):
        for r in (1, 5, 22, 26):
            ref[r] = jnp.zeros((16, 128), F32)

    lane, sub = iota((8, 128), 1), iota((8, 128), 0)
    cells = {(y, gp): jnp.zeros((8, 128), F32) for y in range(-1, n_y + 1) for gp in range(2)}
    pairs = n_y // 2

    def block(gp, q, gz, half):
        at, rows = (gp * n_gy + q // 2) * 2 + gz, slice(8 * half, 8 * half + 8)
        return pick(c ^ (q % 2), blocks[at, rows, :], more[at, rows, :])

    for gp in range(2):
        for q in range(pairs):
            whole = []
            for gz in range(2):
                ends = jnp.zeros((8, 128), F32)
                if q + 1 < pairs:
                    ends = jnp.where(lane < 32, block(gp, q + 1, gz, 0), ends)
                if q > 0:
                    ends = jnp.where(lane >= 96, block(gp, q - 1, gz, 0), ends)
                whole.append(block(gp, q, gz, 0) + roll(ends, 64, 1))
            near, far = whole
            near2, far2 = [block(gp, q, gz, 1) for gz in range(2)]
            for y in range(2):
                high = jnp.where(lane < 64, roll(far, -32 * y, 1), 0.0)
                own = jnp.where(lane < 32, roll(near, -32 * (y + 1), 1), high)
                cells[2 * q + y, gp] = cells[2 * q + y, gp] + own
                high = jnp.where(lane < 64, roll(far2, 32 * (1 - y), 1), 0.0)
                k2[2 * q + y, 8 * gp : 8 * gp + 8, :] = jnp.where(lane < 32, roll(near2, -32 * y, 1), high)
            high = jnp.where(lane < 64, roll(far2, -32, 1), 0.0)
            beyond = jnp.where(lane < 32, roll(near2, -64, 1), high)
            goal = 0 if gp == 0 else 7
            for y in range(-1, 3):
                spot = 2 * q + y, 1 - gp
                cells[spot] = cells[spot] + jnp.where(sub == goal, roll(beyond, goal - y - 1, 0), 0.0)
    for y in range(n_y):
        for gp in range(2):
            r2[y, 8 * gp : 8 * gp + 8, :] = cells[y, gp]
    middle, rhs2 = Level(k2[...], 0.0625), r2[...]
    m2 = middle.weight * rhs2
    m2 = middle.sweep(m2, rhs2)
    rhs3 = halved(middle.resid(m2, rhs2), sums)
    bottom = Level(halved(k2[...], sums), 0.015625)
    m3 = bottom.weight * rhs3
    for _ in range(COARSE_SWEEPS - 1):
        m3 = bottom.sweep(m3, rhs3)
    m2 = m2 + doubled(m3, sums)
    for _ in range(SMOOTH):
        m2 = middle.sweep(m2, rhs2)

    shape = (128, 128)
    z = iota(shape, 1)
    z = jnp.where(z < 96, z, z - 128)
    spread = jnp.where(32 * t + (z >> 1) == iota(shape, 0), 1.0, 0.0).astype(F32)
    tall[...] = jnp.zeros_like(tall)
    tall[4 : 4 + n_y, 8:24, :] = dot(m2.reshape(16 * n_y, 128), spread).reshape(n_y, 16, 128)
    for j in range(8):
        cells = tall[4 * b + 2 * c + 1 + j]
        flat[64 * j : 64 * j + 32, :] = cells
        flat[64 * j + 32 : 64 * j + 64, :] = cells
    for i in range(14):
        e = pick(p, flat[pl.ds(5 + i, 16, stride=32), :], flat[pl.ds(13 + i, 16, stride=32), :])
        for r in (2 * i, 2 * i + 1):
            ua[r] = v21[r] + jnp.where(w1[r] > 0.0, e, 0.0)
    at = 6 - 4 * p
    rows = pl.ds(at, 20)
    near = k1[pl.ds(at, 21)]
    k = near[:20]
    fx[rows] = 0.125 * (k + near[1:])
    fy[rows] = 0.125 * (k + roll(k, -1, 1))
    fz[rows] = 0.125 * (k + roll(k, -1, 2))
    sweep(ua, ub, r1, fx, fy, fz, w1, at, 20, 20)
    sweep(ub, ua, r1, fx, fy, fz, w1, at, 20, 20)

    e = roll(ua[5:23], -4, 1)[:, :8].reshape(144, 128)
    flat[pl.ds(0, 144, stride=2), :] = e
    flat[pl.ds(1, 144, stride=2), :] = e
    shape = (128, 256)
    spread = jnp.where((iota(shape, 1) >> 1) == iota(shape, 0), 1.0, 0.0).astype(F32)
    e = dot(flat[0:288, :], spread).reshape(18, 16, 256)
    for k in range(18):
        for r in (2 * k + 3, 2 * k + 4):
            va[r] = jnp.where(weight[r] > 0.0, e[k], 0.0)
    sweep(va, vb, left, cx, cy, cz, weight, 5 - p, 33, 33)
    here, total = around(vb, cx, cy, cz, 5, 32)
    done = (1.0 - OMEGA) * here + weight[5:37] * (left[5:37] + total)
    va[0:32, 0:8, 0:128] = v2[...] + roll(done[:, :, :128], -4, 1)[:, :8]
    keep[...] = va[pl.ds(16 * c, 16), 0:8, 0:128]
    give[...] = va[pl.ds(16 - 16 * c, 16), 0:8, 0:128]


def join_kernel(mine, other, out, done):
    _, c, _, _ = place()
    copies = []
    for i, (part, at) in enumerate(((mine, 8 * c), (other, 8 - 8 * c))):
        copies.append(pltpu.make_async_copy(part, out.at[:, pl.ds(pl.multiple_of(at, 8), 8), :], done.at[i]))
        copies[i].start()
    for copy in copies:
        copy.wait()


def call(kernel, name, outs, scratch, *args):
    where = pltpu.HBM if name == "message" else pltpu.VMEM
    last = 1 if name in ("down", "join") else 0
    if name == "message":
        args = [pltpu.with_memory_space_constraint(a, pltpu.HBM) for a in args]
    return pl.pallas_call(
        kernel,
        name=name,
        out_shape=[jax.ShapeDtypeStruct(s, F32) for s in outs],
        in_specs=[pl.BlockSpec(memory_space=where)] * len(args),
        out_specs=[pl.BlockSpec(memory_space=pltpu.VMEM)] * (len(outs) - last) + [pl.BlockSpec(memory_space=pltpu.HBM)] * last,
        scratch_shapes=[
            pltpu.SemaphoreType.DMA((s,)) if isinstance(s, int) else pltpu.VMEM(*s) for s in scratch
        ],
        compiler_params=pltpu.CompilerParams(vmem_limit_bytes=16 * 1024 * 1024),
        cost_estimate=pl.CostEstimate(flops=10**7, bytes_accessed=4 * 10**6, transcendentals=0),
    )(*args)


def paired(chi, inducing, record_dest, record_cell, record_value):
    n_gy = lax.axis_size("gy")
    everyone = ("gx", "gy", "gz")
    window = (ROWS, 16, 256)
    big = [(window, F32)]
    chi, inducing, message, spill = call(
        message_kernel,
        "message",
        [(16, 16, 128), (3, 16, 16, 128), (120, 128), (48, 128)],
        [((8, 128), jnp.int32)] * 2 + [((8, 128), F32), 11],
        chi,
        inducing,
        record_dest.reshape(8, 128),
        record_cell.reshape(8, 128),
        record_value.reshape(8, 128),
    )
    got = lax.ppermute(message, "gz", [(0, 1), (1, 0)])
    spread = [((256, 1024), BF16), ((512, 1024), BF16)]
    source, total = call(
        source_kernel,
        "source",
        [(18, 24, 128), (256, 256)],
        spread,
        chi,
        inducing,
        message,
    )
    own, sent = call(
        deposit_kernel,
        "deposit",
        [(39, 16, 128)] * 2,
        [((39, 24, 128), F32)] + spread,
        source,
        spill,
        chi,
        total,
        got,
    )
    swap = [(0, 1), (1, 0), (2, 3), (3, 2)]
    got = lax.ppermute(sent, "gx", swap)
    held = [(ROWS, 16, 128), (ROWS, 16, 128), (12, 16, 128)]
    *fields, message, strip, corner = call(
        pair_kernel, "pair", held + [(10, 16, 128), (PLANES + 6, 8, 128), (6, 8, 128)], [], own, got
    )
    cross = [(0, 2), (2, 0), (1, 3), (3, 1)]
    across = lax.ppermute(message, "gx", cross)
    turns, corners = [], []
    for p in range(2):
        for b in range(n_gy - 1):
            low, high = (2 * p + 1) * n_gy + b, 2 * p * n_gy + b + 1
            turns += [(low, high), (high, low)]
            high = 2 * (1 - p) * n_gy + b + 1
            corners += [(low, high), (high, low)]
    for low, high in ((0, 2 * n_gy), (2 * n_gy - 1, 4 * n_gy - 1)):
        turns += [(low, high), (high, low)]
        corners += [(low, high), (high, low)]
    strip = lax.ppermute(strip, ("gx", "gy"), turns)
    corner = lax.ppermute(corner, ("gx", "gy"), corners)
    *fine, along, beside, message, parts = call(
        functools.partial(down_kernel, n_gy),
        "down",
        [window] * 3 + [(32, 8, 128), (18, 8, 128), (18, 8, 128), (6, 8, 128), (4 * n_gy, 16, 128)],
        big * 7 + [((648, 128), F32), ((48, 128), F32), ((12, 16, 128), F32)]
        + [((4 * n_gy, 16, 128), F32), 1],
        *fields,
        across,
        strip,
        corner,
    )
    n = 2 * n_gy
    groups = [[(2 * p + c) * n + i for p in range(2) for i in range(n)] for c in range(2)]
    blocks = lax.all_to_all(
        parts, ("gx", "gy", "gz"), split_axis=0, concat_axis=0, tiled=True, axis_index_groups=groups
    )
    more = lax.ppermute(blocks, "gx", swap)
    across = lax.ppermute(message, "gx", cross)
    got = lax.ppermute(along, ("gx", "gy"), turns)
    corner = lax.ppermute(message, ("gx", "gy"), corners)
    other = lax.ppermute(beside, "gx", swap)
    beyond = lax.ppermute(across, "gx", swap)
    window1 = (28, 16, 128)
    big1 = [(window1, F32)]
    left, kappa, weight, v = fine
    coarse = call(
        functools.partial(middle_kernel, n_gy),
        "middle",
        [window1] * 4 + [window] * 3,
        big1 * 5,
        beside,
        across,
        jnp.concatenate([got, corner, other, beyond]),
        kappa,
    )
    level2 = ((4 * n_gy, 16, 128), F32)
    keep, give = call(
        functools.partial(up_kernel, n_gy),
        "up",
        [(16, 8, 128)] * 2,
        [level2] * 2
        + [((4 * n_gy + 8, 32, 128), F32), ((544, 128), F32), ((64 * n_gy, 128), F32)]
        + big1 * 5
        + big * 2,
        blocks,
        more,
        *coarse,
        left,
        weight,
        v,
    )
    got = lax.ppermute(give, "gx", swap)
    (out,) = call(join_kernel, "join", [(16, 16, 128)], [2], keep, got)
    return out


def solution(mesh):
    placed = (
        P("gx", "gy", "gz"),
        P(None, "gx", "gy", "gz"),
        P("gx", "gy", "gz", None, None),
        P("gx", "gy", "gz", None),
        P("gx", "gy", "gz", None),
    )
    small = mesh.shape["gx"] == 4 and mesh.shape["gz"] == 2 and mesh.shape["gy"] <= 4
    return jax.shard_map(
        paired if small else general,
        mesh=mesh,
        in_specs=placed,
        out_specs=P("gx", "gy", "gz"),
        check_vma=False,
    )
```
